32 devices in a mesh: wide: 8 (over z, x), narrow: 4 (over y, core).
Axes of the slice: x: 2, y: 2, z: 4, core: 2. Of those that a mesh axis runs over, the one named last changes fastest.
Arguments:
- tokens: bfloat16 [32768, 1024], P(('wide', 'narrow')), may hold values from -6 to 6
- cotangent: bfloat16 [32768, 1024], P(('wide', 'narrow')), may hold values from -12 to 12
- seq_length: int32 [32], P(('wide', 'narrow')), may hold values from 128 to 1024, as said below
- first_gain: bfloat16 [1024], P(('wide', 'narrow')), may hold values from 0.25 to 1.75
- first_shift: bfloat16 [1024], P(('wide', 'narrow')), may hold values from -1.5 to 1.5
- query_weight: bfloat16 [1024, 1024], P(('wide', 'narrow')), may hold values from -0.25 to 0.25
- query_bias: bfloat16 [1024], P(('wide', 'narrow')), may hold values from -1.5 to 1.5
- key_weight: bfloat16 [1024, 1024], P(('wide', 'narrow')), may hold values from -0.1875 to 0.1875
- value_weight: bfloat16 [1024, 1024], P(('wide', 'narrow')), may hold values from -0.1875 to 0.1875
- value_bias: bfloat16 [1024], P(('wide', 'narrow')), may hold values from -1.5 to 1.5
- out_weight: bfloat16 [1024, 1024], P(('wide', 'narrow')), may hold values from -0.5 to 0.5
- out_bias: bfloat16 [1024], P(('wide', 'narrow')), may hold values from -1.5 to 1.5
- second_gain: bfloat16 [1024], P(('wide', 'narrow')), may hold values from 0.25 to 1.75
- second_shift: bfloat16 [1024], P(('wide', 'narrow')), may hold values from -1.5 to 1.5
- up_weight: bfloat16 [1024, 4096], P(('wide', 'narrow')), may hold values from -0.1875 to 0.1875
- up_bias: bfloat16 [4096], P(('wide', 'narrow')), may hold values from -1.5 to 1.5
- down_weight: bfloat16 [4096, 1024], P(('wide', 'narrow')), may hold values from -0.09375 to 0.09375
- down_bias: bfloat16 [1024], P(('wide', 'narrow')), may hold values from -1.5 to 1.5
Outputs:
- output: bfloat16 [32768, 1024], P(('wide', 'narrow'))
- grad_tokens: bfloat16 [32768, 1024], P(('wide', 'narrow'))
- grad_first_gain: float32 [1024], P(('wide', 'narrow'))
- grad_first_shift: float32 [1024], P(('wide', 'narrow'))
- grad_query_weight: float32 [1024, 1024], P(('wide', 'narrow'))
- grad_query_bias: float32 [1024], P(('wide', 'narrow'))
- grad_key_weight: float32 [1024, 1024], P(('wide', 'narrow'))
- grad_value_weight: float32 [1024, 1024], P(('wide', 'narrow'))
- grad_value_bias: float32 [1024], P(('wide', 'narrow'))
- grad_out_weight: float32 [1024, 1024], P(('wide', 'narrow'))
- grad_out_bias: float32 [1024], P(('wide', 'narrow'))
- grad_second_gain: float32 [1024], P(('wide', 'narrow'))
- grad_second_shift: float32 [1024], P(('wide', 'narrow'))
- grad_up_weight: float32 [1024, 4096], P(('wide', 'narrow'))
- grad_up_bias: float32 [4096], P(('wide', 'narrow'))
- grad_down_weight: float32 [4096, 1024], P(('wide', 'narrow'))
- grad_down_bias: float32 [1024], P(('wide', 'narrow'))
The draws below stay inside these ranges and needn't reach their ends.
Inputs may be any that keep to these rules, and one draw needn't show every extreme that they name: `seq_length`: every entry is 128 or 1024; both values occur in every draw.
All inputs are finite; a program needn't handle non-finite values.
Results may differ from the reference program's by a relative error of at most 0.012.
Values may be sent and summed in bfloat16 or wider, within the bound.
A program may use at most 256 MiB of HBM per device.

```python
import jax
import jax.numpy as jnp
from jax import lax

D = 1024
H = 8
HD = 128
FF = 4096
TOK_DEV = 1024
SHORT = 128
BLOCKS = 32
TOKENS = 32768


def draw_seq_length(key, part):
    key = jax.random.fold_in(key, 11)
    key_flags, key_pick = jax.random.split(key)
    flags = jax.random.randint(key_flags, (BLOCKS,), 0, 2)
    pick = jax.random.randint(key_pick, (), 0, BLOCKS)
    index = jnp.arange(BLOCKS)
    flags = jnp.where(index == pick, 1, jnp.where(index == (pick + 1) % BLOCKS, 0, flags))
    return jnp.where(flags == 1, TOK_DEV, SHORT).astype(jnp.int32)


def raised(values, rng, source, target, parts, factor):
    owner, partner = [(jnp.arange(values.shape[axis_at]) // (values.shape[axis_at] // parts)).reshape([-1 if axis == axis_at else 1 for axis in range(values.ndim)]) for axis_at in (source, target)]
    chosen = jax.random.permutation(rng, parts)[partner]
    strong = (owner == chosen) | (owner == (partner + parts // 2) % parts)
    return jnp.where(strong, factor * values, values)


def levels(own_key, extent, shards, least, high):
    def one(dim, parts):
        steps = jax.random.uniform(jax.random.fold_in(jax.random.fold_in(own_key, 6), dim), (parts,), jnp.float32, least / len(shards), high / len(shards))
        return jnp.repeat(jnp.exp(steps), extent[dim] // parts).reshape((-1,) + (1,) * (len(extent) - dim - 1))

    loudness = one(*shards[0])
    for cut in shards[1:]:
        loudness = loudness * one(*cut)
    return loudness


def noise(key, shape, deviation, bound, cuts=(), kind=jnp.bfloat16):
    array = jax.random.normal(key, shape, jnp.float32) * deviation
    if len(cuts) > 0:
        array = levels(key, shape, cuts, -0.22, 0.18) * array
    return jnp.clip(array, min=-bound, max=bound).astype(kind)


def gaussian_with(own_key, dims, deviation, reach, shards, heavy, held_as=jnp.bfloat16):
    values = deviation * jax.random.normal(own_key, dims, jnp.float32)
    if shards:
        values = values * levels(own_key, dims, shards, -0.22, 0.18)
    return jnp.clip(raised(values, jax.random.fold_in(own_key, 3), *heavy), -reach, reach).astype(held_as)


def setup_inputs(seed: int = 0) -> dict:
    key_of = jax.random.split(jax.random.key(seed), 19)
    tokens = noise(key_of[0], (TOKENS, D), 1.0, 6.0, ((0, 32),))
    cotangent = gaussian_with(key_of[1], (TOKENS, D), 1.0, 12.0, ((0, 32),), (0, 1, 32, 2.75))
    seq_length = draw_seq_length(jax.random.fold_in(key_of[18], 71), 0)
    first_gain = jnp.clip(1.0 + 0.15 * jax.random.normal(key_of[3], (D,), jnp.float32), 0.25, 1.75).astype(jnp.bfloat16)
    first_shift = noise(key_of[4], (D,), 0.3, 1.5, ((0, 32),))
    query_weight = noise(key_of[5], (D, D), (D // 2) ** -0.5, 0.25, ((0, 32),))
    query_bias = noise(key_of[6], (D,), 0.3, 1.5, ((0, 32),))
    key_weight = noise(key_of[7], (D, D), D ** -0.5, 0.1875, ((0, 32),))
    value_weight = noise(key_of[8], (D, D), D ** -0.5, 0.1875, ((0, 32),))
    value_bias = noise(key_of[9], (D,), 0.3, 1.5, ((0, 32),))
    out_weight = noise(key_of[10], (D, D), (D // 8) ** -0.5, 0.5, ((0, 32),))
    out_bias = noise(key_of[11], (D,), 0.3, 1.5, ((0, 32),))
    second_gain = jnp.clip(1.0 + 0.15 * jax.random.normal(key_of[12], (D,), jnp.float32), 0.25, 1.75).astype(jnp.bfloat16)
    second_shift = noise(key_of[13], (D,), 0.3, 1.5, ((0, 32),))
    up_weight = noise(key_of[14], (D, FF), D ** -0.5, 0.1875, ((0, 32),))
    up_bias = noise(key_of[15], (FF,), 0.3, 1.5, ((0, 32),))
    down_weight = noise(key_of[16], (FF, D), FF ** -0.5, 0.09375, ((0, 32),))
    down_bias = noise(key_of[17], (D,), 0.3, 1.5, ((0, 32),))
    return {"tokens": tokens, "cotangent": cotangent, "seq_length": seq_length, "first_gain": first_gain, "first_shift": first_shift, "query_weight": query_weight, "query_bias": query_bias, "key_weight": key_weight, "value_weight": value_weight, "value_bias": value_bias, "out_weight": out_weight, "out_bias": out_bias, "second_gain": second_gain, "second_shift": second_shift, "up_weight": up_weight, "up_bias": up_bias, "down_weight": down_weight, "down_bias": down_bias}


@jax.custom_vjp
def low(v):
    return lax.optimization_barrier(v.astype(jnp.bfloat16)).astype(jnp.float32)

@jax.custom_vjp
def low_back(v):
    return v

def low_keep(v):
    return (low(v), None)

def low_pass(kept, grad):
    return (grad,)

def back_keep(v):
    return (v, None)

def back_low(kept, grad):
    return (low(grad),)
low.defvjp(low_keep, low_pass)
low_back.defvjp(back_keep, back_low)
EPSILON = 1e-05

def matmul(left, right):
    return jnp.dot(left, right, precision=lax.Precision.HIGHEST)

def layer_norm(value, gain, shift):
    center = value - lax.optimization_barrier(jnp.mean(value, -1, keepdims=True))
    spread = lax.optimization_barrier(jnp.mean(center * center, -1, keepdims=True))
    return center * lax.rsqrt(spread + EPSILON) * gain + shift

def block_forward(inputs, params, length):
    first_gain, first_shift, query_weight, query_bias, key_weight, value_weight, value_bias, out_weight, out_bias, second_gain, second_shift, up_weight, up_bias, down_weight, down_bias = params
    count = inputs.shape[0]
    attn_in = low(layer_norm(inputs, first_gain, first_shift))
    queries = low(low_back(matmul(attn_in, query_weight) + query_bias)).reshape(count, H, HD)
    keys = low(low_back(matmul(attn_in, key_weight))).reshape(count, H, HD)
    values = low(low_back(matmul(attn_in, value_weight) + value_bias)).reshape(count, H, HD)
    position = jnp.arange(count, dtype=jnp.int32)
    distance = (position[:, None] - position[None, :]).astype(jnp.float32)
    slopes = jnp.exp2(-8.0 * jnp.arange(1, H + 1, dtype=jnp.float32) / H)
    allowed = (position[:, None] >= position[None, :]) & (position[:, None] // length == position[None, :] // length)
    raw = jnp.einsum('qhd,khd->hqk', queries, keys, precision=lax.Precision.HIGHEST) * HD ** (-0.5)
    raw = low_back(raw - slopes[:, None, None] * distance[None])
    scores = jnp.where(allowed[None], raw, -1e+30)
    top = lax.optimization_barrier(jnp.max(scores, -1, keepdims=True))
    expo = jnp.exp(scores - top)
    probs = expo / lax.optimization_barrier(jnp.sum(expo, -1, keepdims=True))
    mixed = jnp.einsum('hqk,khd->qhd', low(probs), values, precision=lax.Precision.HIGHEST)
    mixed = low(low_back(mixed.reshape(count, H * HD)))
    resid = inputs + low_back(matmul(mixed, out_weight) + out_bias)
    ffn_in = low(layer_norm(resid, second_gain, second_shift))
    hidden = low_back(matmul(ffn_in, up_weight) + up_bias)
    active = low(jax.nn.gelu(hidden, approximate=False))
    return resid + low_back(matmul(active, down_weight) + down_bias)

def reference(tokens, cotangent, seq_length, first_gain, first_shift, query_weight, query_bias, key_weight, value_weight, value_bias, out_weight, out_bias, second_gain, second_shift, up_weight, up_bias, down_weight, down_bias):
    params = tuple((item.astype(jnp.float32) for item in (first_gain, first_shift, query_weight, query_bias, key_weight, value_weight, value_bias, out_weight, out_bias, second_gain, second_shift, up_weight, up_bias, down_weight, down_bias)))
    inputs = tokens.astype(jnp.float32).reshape(BLOCKS, TOK_DEV, D)
    grads_in = cotangent.astype(jnp.float32).reshape(BLOCKS, TOK_DEV, D)

    def step(total, item):
        block_in, block_grad, length = item
        result, pull = jax.vjp(lambda value, weights: block_forward(value, weights, length), block_in, params)
        grad_in, grad_params = pull(block_grad)
        total = jax.tree.map(lambda left, right: left + right, total, grad_params)
        return (total, (result.astype(jnp.bfloat16), grad_in.astype(jnp.bfloat16)))
    zeros = tuple((jnp.zeros(item.shape, jnp.float32) for item in params))
    total, (results, grad_blocks) = lax.scan(step, zeros, (inputs, grads_in, seq_length))
    g_first_gain, g_first_shift, g_query_weight, g_query_bias, g_key_weight, g_value_weight, g_value_bias, g_out_weight, g_out_bias, g_second_gain, g_second_shift, g_up_weight, g_up_bias, g_down_weight, g_down_bias = total
    return (results.reshape(TOKENS, D), grad_blocks.reshape(TOKENS, D), g_first_gain, g_first_shift, g_query_weight, g_query_bias, g_key_weight, g_value_weight, g_value_bias, g_out_weight, g_out_bias, g_second_gain, g_second_shift, g_up_weight, g_up_bias, g_down_weight, g_down_bias)
```

```python
import functools

import jax
import jax.numpy as jnp
from jax import lax
from jax.experimental import pallas as pl
from jax.experimental.pallas import tpu as pltpu
from jax.sharding import PartitionSpec as P

H = 8
HD = 128
AXES = ("wide", "narrow")
MESH = pl.DeviceIdType.MESH
BF = jnp.bfloat16
F32 = jnp.float32


class Place:
    def __init__(self):
        wide, narrow = lax.axis_index("wide"), lax.axis_index("narrow")
        self.z, self.x = lax.div(wide, 2), lax.rem(wide, 2)
        self.y, self.c = lax.div(narrow, 2), lax.rem(narrow, 2)
        c, x, y = self.c, self.x, self.y
        self.one = (x + (1 - c) * (1 - 2 * x), y + c * (1 - 2 * y))
        self.two = (x + c * (1 - 2 * x), y + (1 - c) * (1 - 2 * y))
        self.far = (1 - x, 1 - y)
        self.here = (x, y)

    def device(self, z, xy, c):
        return (z * 2 + xy[0], xy[1] * 2 + c)

    def up(self, step):
        return lax.rem(self.z + step, 4)

    def down(self, step):
        return lax.rem(self.z + 4 - step, 4)

    def partners(self):
        z, c = self.z, self.c
        return [self.device(self.up(step), self.here, c) for step in (1, 2, 3)] + [
            self.device(z, self.one, c),
            self.device(z, self.two, c),
            self.device(z, self.here, 1 - c),
        ]

    def greet(self):
        barrier = pltpu.get_barrier_semaphore()
        partners = self.partners()
        for partner in partners:
            pl.semaphore_signal(barrier, inc=1, device_id=partner, device_id_type=MESH)
        pl.semaphore_wait(barrier, len(partners))


def remote(source, target, send, recv, device):
    return pltpu.make_async_remote_copy(
        src_ref=source,
        dst_ref=target,
        send_sem=send,
        recv_sem=recv,
        device_id=device,
        device_id_type=MESH,
    )


class Gathering:
    SEMS = 10
    STAGES = 5

    def __init__(self, place, local, full, send, recv, keep):
        self.place, self.local, self.full = place, local, full
        self.send, self.recv, self.keep = send, recv, keep

    def block(self, xy, c):
        return self.full.at[:, xy[0], xy[1], c]

    def cell(self, z):
        place = self.place
        return self.full.at[z, place.x, place.y, place.c]

    def copy(self, source, target, sem, device):
        return remote(source, target, self.send.at[sem], self.recv.at[sem], device)

    def along(self, step):
        place = self.place
        device = place.device(place.up(step), place.here, place.c)
        return self.copy(self.local, self.cell(place.z), step - 1, device)

    def pieces(self):
        place = self.place
        z, c = place.z, place.c
        one, two = place.device(z, place.one, c), place.device(z, place.two, c)
        twin = place.device(z, place.here, 1 - c)
        mine, first = self.block(place.here, c), self.block(place.one, c)
        second, far = self.block(place.two, c), self.block(place.far, c)
        return {
            3: (mine, one, self.block(place.one, c)),
            4: (mine, two, self.block(place.two, c)),
            5: (mine, twin, self.block(place.here, 1 - c)),
            6: (first, two, self.block(place.far, c)),
            7: (first, twin, self.block(place.two, 1 - c)),
            8: (second, twin, self.block(place.one, 1 - c)),
            9: (far, twin, self.block(place.far, 1 - c)),
        }

    def start(self, sem):
        source, device, _ = self.pieces()[sem]
        self.copy(source, source, sem, device).start()

    def await_recv(self, sem):
        _, device, landing = self.pieces()[sem]
        self.copy(landing, landing, sem, device).wait_recv()

    def own(self):
        return pltpu.make_async_copy(self.local, self.cell(self.place.z), self.keep)

    def stage(self, number):
        place = self.place
        if number == 0:
            self.own().start()
            for step in (1, 2, 3):
                self.along(step).start()
        elif number == 1:
            self.own().wait()
            for step in (1, 2, 3):
                cell = self.cell(place.down(step))
                device = place.device(place.down(step), place.here, place.c)
                self.copy(cell, cell, step - 1, device).wait_recv()
            for sem in (3, 4, 5):
                self.start(sem)
        elif number == 2:
            self.await_recv(3)
            self.start(6)
            self.start(7)
            self.await_recv(4)
            self.start(8)
        elif number == 3:
            self.await_recv(6)
            self.start(9)
        elif number == 4:
            for sem in (5, 7, 8, 9):
                self.await_recv(sem)

    def finish(self):
        for step in (1, 2, 3):
            self.along(step).wait_send()
        for sem in range(3, 10):
            source, device, _ = self.pieces()[sem]
            self.copy(source, source, sem, device).wait_send()


class Scattering:
    SEMS = 7
    STAGES = 5

    def __init__(self, place, partial, mine, total, pair, line, out, send, recv, load):
        self.place, self.partial, self.mine = place, partial, mine
        self.total, self.pair, self.line, self.out = total, pair, line, out
        self.send, self.recv, self.load = send, recv, load

    def pieces(self):
        place = self.place
        z, c = place.z, place.c
        one, two = place.device(z, place.one, c), place.device(z, place.two, c)
        twin = place.device(z, place.here, 1 - c)
        total = self.total

        def block(xy):
            return total.at[:, xy[0], xy[1]]

        table = {
            0: (self.partial.at[:, :, :, 1 - c], total, twin),
            1: (block(place.two), self.pair.at[0], two),
            2: (block(place.far), self.pair.at[1], two),
            3: (block(place.one), self.pair.at[2], one),
        }
        for step in (1, 2, 3):
            device = place.device(place.up(step), place.here, c)
            table[3 + step] = (
                total.at[place.up(step), place.x, place.y],
                self.line.at[step - 1],
                device,
            )
        return table

    def copy(self, sem):
        source, target, device = self.pieces()[sem]
        return remote(source, target, self.send.at[sem], self.recv.at[sem], device)

    def own(self):
        return pltpu.make_async_copy(
            self.partial.at[:, :, :, self.place.c], self.mine, self.load
        )

    def stage(self, number):
        place, total, pair = self.place, self.total, self.pair

        def add(xy, slot):
            def body(z, carry):
                value = total[z, xy[0], xy[1]].astype(F32) + pair[slot, z].astype(F32)
                total[z, xy[0], xy[1]] = value.astype(BF)
                return carry

            lax.fori_loop(0, 4, body, 0)

        if number == 0:
            self.own().start()
            self.copy(0).start()
        elif number == 1:
            self.own().wait()
            self.copy(0).wait_recv()

            def body(z, carry):
                for x in range(2):
                    for y in range(2):
                        value = total[z, x, y].astype(F32) + self.mine[z, x, y].astype(F32)
                        total[z, x, y] = value.astype(BF)
                return carry

            lax.fori_loop(0, 4, body, 0)
            self.copy(2).start()
            self.copy(1).start()
        elif number == 2:
            self.copy(2).wait_recv()
            add(place.one, 1)
            self.copy(3).start()
            self.copy(1).wait_recv()
            add(place.here, 0)
        elif number == 3:
            self.copy(3).wait_recv()
            add(place.here, 2)
            for step in (1, 2, 3):
                self.copy(3 + step).start()
        elif number == 4:
            value = total[place.z, place.x, place.y].astype(F32)
            for step in (1, 2, 3):
                self.copy(3 + step).wait_recv()
                value = value + self.line[step - 1].astype(F32)
            self.out[...] = value

    def finish(self):
        for sem in range(7):
            self.copy(sem).wait_send()


class Summing:
    SEMS = 6

    def __init__(self, place, value, total, slots, send, recv):
        self.place, self.value, self.total, self.slots = place, value, total, slots
        self.send, self.recv = send, recv

    def copy(self, sem):
        place = self.place
        device = [
            place.device(place.z, place.here, 1 - place.c),
            place.device(place.z, place.one, place.c),
            place.device(place.z, place.two, place.c),
        ] + [place.device(place.up(step), place.here, place.c) for step in (1, 2, 3)]
        source = self.total.at[min(sem, 3)]
        return remote(source, self.slots.at[sem], self.send.at[sem], self.recv.at[sem], device[sem])

    def stage(self, number):
        total, slots = self.total, self.slots
        if number == 0:
            total[0] = self.value[...]
            self.copy(0).start()
        elif number < 3:
            self.copy(number - 1).wait_recv()
            total[number] = total[number - 1] + slots[number - 1]
            self.copy(number).start()
        elif number == 3:
            self.copy(2).wait_recv()
            total[3] = total[2] + slots[2]
            for sem in (3, 4, 5):
                self.copy(sem).start()
        elif number == 4:
            value = total[3]
            for sem in (3, 4, 5):
                self.copy(sem).wait_recv()
                value = value + slots[sem]
            total[4] = value

    def finish(self):
        for sem in range(6):
            self.copy(sem).wait_send()


def pipeline(tasks, stages):
    for tick in range(len(tasks) + stages - 1):
        for number in reversed(range(stages)):
            if 0 <= tick - number < len(tasks):
                tasks[tick - number].stage(number)


def halves(ref, count, width):
    if count == 1:
        return [ref]
    lead = (slice(None),) * (len(ref.shape) - 1)
    return [ref.at[lead + (pl.ds(i * width, width),)] for i in range(count)]


CUTS = (1, 1, 1, 1, 1, 2, 2)


def gather_kernel(*refs):
    count = len(CUTS)
    local, full = refs[:count], refs[count : 2 * count]
    send, recv, keep = refs[2 * count :]
    place = Place()
    place.greet()
    tasks = []
    for source, target, cut in zip(local, full, CUTS):
        width = source.shape[-1] // cut
        for one, other in zip(halves(source, cut, width), halves(target, cut, width)):
            g = len(tasks)
            tasks.append(Gathering(place, one, other, send.at[g], recv.at[g], keep.at[g]))
    pipeline(tasks, Gathering.STAGES)
    for task in tasks:
        task.finish()


def gather_all(arrays):
    groups = sum(CUTS)
    results = pl.pallas_call(
        gather_kernel,
        out_shape=[jax.ShapeDtypeStruct((4, 2, 2, 2) + a.shape, a.dtype) for a in arrays],
        in_specs=[pl.BlockSpec(memory_space=pltpu.HBM)] * len(arrays),
        out_specs=[pl.BlockSpec(memory_space=pltpu.HBM)] * len(arrays),
        scratch_shapes=[
            pltpu.SemaphoreType.DMA((groups, Gathering.SEMS)),
            pltpu.SemaphoreType.DMA((groups, Gathering.SEMS)),
            pltpu.SemaphoreType.DMA((groups,)),
        ],
        compiler_params=pltpu.CompilerParams(collective_id=0, has_side_effects=True),
    )(*arrays)
    return results


def scatter_kernel(cuts, *refs):
    count = len(cuts)
    small, partial = refs[0], refs[1 : 1 + count]
    small_out, out = refs[1 + count], refs[2 + count : 2 + 2 * count]
    rest = list(refs[2 + 2 * count :])
    mine, total, pair, line = (rest[i * count : (i + 1) * count] for i in range(4))
    small_total, small_slots, small_send, small_recv, send, recv, load = rest[4 * count :]
    place = Place()
    place.greet()
    tasks = []
    g = 0
    for i, cut in enumerate(cuts):
        width = partial[i].shape[-1] // cut
        views = [
            halves(ref, cut, width)
            for ref in (partial[i], mine[i], total[i], pair[i], line[i], out[i])
        ]
        for j in range(cut):
            tasks.append(
                Scattering(place, *(view[j] for view in views), send.at[g], recv.at[g], load.at[g])
            )
            g += 1
    sums = Summing(place, small, small_total, small_slots, small_send, small_recv)
    tasks.insert(1, sums)
    pipeline(tasks, Scattering.STAGES)
    for task in tasks:
        task.finish()
    small_out[...] = small_total[4]


def scatter_all(small, arrays, cuts):
    groups = sum(cuts)
    shards = [a.shape[4:] for a in arrays]
    vmem = pl.BlockSpec(memory_space=pltpu.VMEM)
    results = pl.pallas_call(
        functools.partial(scatter_kernel, cuts),
        out_shape=[jax.ShapeDtypeStruct(small.shape, F32)]
        + [jax.ShapeDtypeStruct(s, F32) for s in shards],
        in_specs=[vmem] + [pl.BlockSpec(memory_space=pltpu.HBM)] * len(arrays),
        out_specs=[vmem] * (1 + len(arrays)),
        scratch_shapes=[pltpu.VMEM((4, 2, 2) + s, BF) for s in shards]
        + [pltpu.VMEM((4, 2, 2) + s, BF) for s in shards]
        + [pltpu.VMEM((3, 4) + s, BF) for s in shards]
        + [pltpu.VMEM((3,) + s, BF) for s in shards]
        + [
            pltpu.VMEM((5,) + small.shape, F32),
            pltpu.VMEM((6,) + small.shape, F32),
            pltpu.SemaphoreType.DMA((Summing.SEMS,)),
            pltpu.SemaphoreType.DMA((Summing.SEMS,)),
            pltpu.SemaphoreType.DMA((groups, Scattering.SEMS)),
            pltpu.SemaphoreType.DMA((groups, Scattering.SEMS)),
            pltpu.SemaphoreType.DMA((groups,)),
        ],
        compiler_params=pltpu.CompilerParams(
            collective_id=1, has_side_effects=True, vmem_limit_bytes=60 << 20
        ),
    )(small, *arrays)
    return results[0], results[1:]


SMALL = (0, 1, 3, 6, 8, 9, 10, 14, 12)
LARGE = (2, 4, 5, 7, 11, 13)


def collect_fast(parts):
    flat = jnp.concatenate([parts[i].astype(F32) for i in SMALL]).reshape(-1, 128)
    flat = jnp.pad(flat, ((0, 8 - flat.shape[0]), (0, 0)))
    small, *large = gather_all([flat] + [parts[i] for i in LARGE])
    small = small.reshape(32, -1)
    whole = [None] * len(parts)
    start = 0
    for i in SMALL:
        size = parts[i].shape[0]
        whole[i] = small[:, start : start + size].reshape(-1).astype(parts[i].dtype)
        start += size
    for i, array in zip(LARGE, large):
        whole[i] = array.reshape(-1, array.shape[-1])
    return tuple(whole)


def spread_fast(parts):
    small = jnp.concatenate([parts[i] for i in SMALL]).reshape(-1, 1024)
    rows = small.shape[0]
    small = jnp.pad(small, ((0, 16 - rows), (0, 0)))
    order = (13, 11, 7, 2, 4, 5)
    arrays = [
        parts[i].astype(BF).reshape(4, 2, 2, 2, parts[i].shape[0] // 32, parts[i].shape[1])
        for i in order
    ]
    small, large = scatter_all(small, arrays, (2, 2, 1, 1, 1, 1))
    result = [None] * len(parts)
    for i, array in zip(order, large):
        result[i] = array
    flat = small.reshape(-1)
    me = lax.axis_index("wide") * 4 + lax.axis_index("narrow")
    start = 0
    for i in SMALL:
        size = parts[i].shape[0]
        result[i] = lax.dynamic_slice(flat, (start + me * (size // 32),), (size // 32,))
        start += size
    return tuple(result)

EPSILON = 1e-05


def collect_plain(parts):
    (
        first_gain,
        first_shift,
        query_weight,
        query_bias,
        key_weight,
        value_weight,
        value_bias,
        out_weight,
        out_bias,
        second_gain,
        second_shift,
        up_weight,
        up_bias,
        down_weight,
        down_bias,
    ) = parts
    return (
        lax.all_gather(first_gain, ("wide", "narrow"), axis=0, tiled=True),
        lax.all_gather(first_shift, ("wide", "narrow"), axis=0, tiled=True),
        lax.all_gather(query_weight, ("wide", "narrow"), axis=0, tiled=True),
        lax.all_gather(query_bias, ("wide", "narrow"), axis=0, tiled=True),
        lax.all_gather(key_weight, ("wide", "narrow"), axis=0, tiled=True),
        lax.all_gather(value_weight, ("wide", "narrow"), axis=0, tiled=True),
        lax.all_gather(value_bias, ("wide", "narrow"), axis=0, tiled=True),
        lax.all_gather(out_weight, ("wide", "narrow"), axis=0, tiled=True),
        lax.all_gather(out_bias, ("wide", "narrow"), axis=0, tiled=True),
        lax.all_gather(second_gain, ("wide", "narrow"), axis=0, tiled=True),
        lax.all_gather(second_shift, ("wide", "narrow"), axis=0, tiled=True),
        lax.all_gather(up_weight, ("wide", "narrow"), axis=0, tiled=True),
        lax.all_gather(up_bias, ("wide", "narrow"), axis=0, tiled=True),
        lax.all_gather(down_weight, ("wide", "narrow"), axis=0, tiled=True),
        lax.all_gather(down_bias, ("wide", "narrow"), axis=0, tiled=True),
    )


def spread_plain(parts):
    (
        first_gain,
        first_shift,
        query_weight,
        query_bias,
        key_weight,
        value_weight,
        value_bias,
        out_weight,
        out_bias,
        second_gain,
        second_shift,
        up_weight,
        up_bias,
        down_weight,
        down_bias,
    ) = parts
    return (
        lax.psum_scatter(first_gain, ("wide", "narrow"), scatter_dimension=0, tiled=True),
        lax.psum_scatter(first_shift, ("wide", "narrow"), scatter_dimension=0, tiled=True),
        lax.psum_scatter(query_weight, ("wide", "narrow"), scatter_dimension=0, tiled=True),
        lax.psum_scatter(query_bias, ("wide", "narrow"), scatter_dimension=0, tiled=True),
        lax.psum_scatter(key_weight, ("wide", "narrow"), scatter_dimension=0, tiled=True),
        lax.psum_scatter(value_weight, ("wide", "narrow"), scatter_dimension=0, tiled=True),
        lax.psum_scatter(value_bias, ("wide", "narrow"), scatter_dimension=0, tiled=True),
        lax.psum_scatter(out_weight, ("wide", "narrow"), scatter_dimension=0, tiled=True),
        lax.psum_scatter(out_bias, ("wide", "narrow"), scatter_dimension=0, tiled=True),
        lax.psum_scatter(second_gain, ("wide", "narrow"), scatter_dimension=0, tiled=True),
        lax.psum_scatter(second_shift, ("wide", "narrow"), scatter_dimension=0, tiled=True),
        lax.psum_scatter(up_weight, ("wide", "narrow"), scatter_dimension=0, tiled=True),
        lax.psum_scatter(up_bias, ("wide", "narrow"), scatter_dimension=0, tiled=True),
        lax.psum_scatter(down_weight, ("wide", "narrow"), scatter_dimension=0, tiled=True),
        lax.psum_scatter(down_bias, ("wide", "narrow"), scatter_dimension=0, tiled=True),
    )


def is_fast():
    return lax.axis_size("wide") == 8 and lax.axis_size("narrow") == 4


def collect(parts):
    return collect_fast(parts) if is_fast() else collect_plain(parts)


def spread(parts):
    return spread_fast(parts) if is_fast() else spread_plain(parts)


def norm_forward(value, gain, shift):
    center = value - jnp.mean(value, -1, keepdims=True)
    inverse = lax.rsqrt(jnp.mean(center * center, -1, keepdims=True) + EPSILON)
    normed = center * inverse
    return (normed * gain.astype(jnp.float32) + shift.astype(jnp.float32), normed, inverse)


def norm_backward(incoming, normed, inverse, gain):
    scaled = incoming * gain.astype(jnp.float32)
    inner = (
        scaled
        - jnp.mean(scaled, -1, keepdims=True)
        - normed * jnp.mean(scaled * normed, -1, keepdims=True)
    )
    return (inverse * inner, jnp.sum(incoming * normed, 0), jnp.sum(incoming, 0))


def gelu_parts(hidden):
    cdf = 0.5 * (1.0 + lax.erf(hidden * 0.7071067811865476))
    density = jnp.exp(-0.5 * hidden * hidden) * 0.3989422804014327
    return (hidden * cdf, cdf + hidden * density)


def masked_scores(queries, keys, length):
    count = queries.shape[0]
    raw = jnp.einsum("qhd,khd->hqk", queries, keys, preferred_element_type=jnp.float32) * HD ** (
        -0.5
    )
    position = jnp.arange(count, dtype=jnp.int32)
    distance = (position[:, None] - position[None, :]).astype(jnp.float32)
    slopes = jnp.exp2(-8.0 * jnp.arange(1, H + 1, dtype=jnp.float32) / H)
    raw = raw - slopes[:, None, None] * distance[None]
    allowed = (position[:, None] >= position[None, :]) & (
        position[:, None] // length == position[None, :] // length
    )
    return jnp.where(allowed[None], raw, -1e30)


def forward(tokens, length, weights):
    (
        first_gain,
        first_shift,
        query_weight,
        query_bias,
        key_weight,
        value_weight,
        value_bias,
        out_weight,
        out_bias,
        second_gain,
        second_shift,
        up_weight,
        up_bias,
        down_weight,
        down_bias,
    ) = weights
    count = tokens.shape[0]
    width = tokens.shape[1]
    inputs = tokens.astype(jnp.float32)
    first_out, first_normed, first_inverse = norm_forward(inputs, first_gain, first_shift)
    attn_in = first_out.astype(jnp.bfloat16)
    queries = (
        (
            jnp.dot(attn_in, query_weight, preferred_element_type=jnp.float32)
            + query_bias.astype(jnp.float32)
        )
        .astype(jnp.bfloat16)
        .reshape(count, H, HD)
    )
    keys = (
        jnp.dot(attn_in, key_weight, preferred_element_type=jnp.float32)
        .astype(jnp.bfloat16)
        .reshape(count, H, HD)
    )
    values = (
        (
            jnp.dot(attn_in, value_weight, preferred_element_type=jnp.float32)
            + value_bias.astype(jnp.float32)
        )
        .astype(jnp.bfloat16)
        .reshape(count, H, HD)
    )
    scores = masked_scores(queries, keys, length)
    top = jnp.max(scores, -1, keepdims=True)
    expo = jnp.exp(scores - top)
    total = jnp.sum(expo, -1, keepdims=True)
    probs = expo / total
    log_total = top + jnp.log(total)
    mixed = jnp.einsum(
        "hqk,khd->qhd", probs.astype(jnp.bfloat16), values, preferred_element_type=jnp.float32
    )
    mixed = mixed.reshape(count, width).astype(jnp.bfloat16)
    resid = (
        inputs
        + jnp.dot(mixed, out_weight, preferred_element_type=jnp.float32)
        + out_bias.astype(jnp.float32)
    )
    second_out, second_normed, second_inverse = norm_forward(resid, second_gain, second_shift)
    ffn_in = second_out.astype(jnp.bfloat16)
    hidden = jnp.dot(ffn_in, up_weight, preferred_element_type=jnp.float32) + up_bias.astype(
        jnp.float32
    )
    active, active_slope = gelu_parts(hidden)
    active_low = active.astype(jnp.bfloat16)
    result = (
        resid
        + jnp.dot(active_low, down_weight, preferred_element_type=jnp.float32)
        + down_bias.astype(jnp.float32)
    )
    return (
        result.astype(jnp.bfloat16),
        attn_in,
        first_normed,
        first_inverse,
        queries,
        keys,
        values,
        log_total,
        mixed,
        second_normed,
        second_inverse,
        ffn_in,
        active_slope,
        active_low,
    )


def backward(cotangent, length, weights, kept):
    (
        first_gain,
        first_shift,
        query_weight,
        query_bias,
        key_weight,
        value_weight,
        value_bias,
        out_weight,
        out_bias,
        second_gain,
        second_shift,
        up_weight,
        up_bias,
        down_weight,
        down_bias,
    ) = weights
    (
        result,
        attn_in,
        first_normed,
        first_inverse,
        queries,
        keys,
        values,
        log_total,
        mixed,
        second_normed,
        second_inverse,
        ffn_in,
        active_slope,
        active_low,
    ) = kept
    count = cotangent.shape[0]
    width = cotangent.shape[1]
    grad_out = cotangent.astype(jnp.float32)
    grad_down_bias = jnp.sum(grad_out, 0)
    grad_down_weight = jnp.einsum(
        "tf,td->fd", active_low, cotangent, preferred_element_type=jnp.float32
    )
    grad_active = jnp.einsum(
        "td,fd->tf", cotangent, down_weight, preferred_element_type=jnp.float32
    )
    grad_hidden = (grad_active * active_slope).astype(jnp.bfloat16)
    grad_up_bias = jnp.sum(grad_hidden.astype(jnp.float32), 0)
    grad_up_weight = jnp.einsum(
        "td,tf->df", ffn_in, grad_hidden, preferred_element_type=jnp.float32
    )
    grad_ffn_in = jnp.einsum(
        "tf,df->td", grad_hidden, up_weight, preferred_element_type=jnp.float32
    )
    grad_second, grad_second_gain, grad_second_shift = norm_backward(
        grad_ffn_in, second_normed, second_inverse, second_gain
    )
    grad_resid = grad_out + grad_second
    grad_branch = grad_resid.astype(jnp.bfloat16)
    grad_out_bias = jnp.sum(grad_branch.astype(jnp.float32), 0)
    grad_out_weight = jnp.einsum(
        "tc,td->cd", mixed, grad_branch, preferred_element_type=jnp.float32
    )
    grad_mixed = jnp.einsum(
        "td,cd->tc", grad_branch, out_weight, preferred_element_type=jnp.float32
    )
    grad_mixed = grad_mixed.astype(jnp.bfloat16).reshape(count, H, HD)
    scores = masked_scores(queries, keys, length)
    probs = jnp.exp(scores - log_total)
    grad_probs = jnp.einsum("qhd,khd->hqk", grad_mixed, values, preferred_element_type=jnp.float32)
    grad_values = jnp.einsum(
        "hqk,qhd->khd", probs.astype(jnp.bfloat16), grad_mixed, preferred_element_type=jnp.float32
    )
    grad_values = grad_values.astype(jnp.bfloat16).reshape(count, width)
    row_total = jnp.sum(grad_probs * probs, -1, keepdims=True)
    grad_scores = (probs * (grad_probs - row_total)).astype(jnp.bfloat16)
    factor = HD ** (-0.5)
    grad_queries = (
        jnp.einsum("hqk,khd->qhd", grad_scores, keys, preferred_element_type=jnp.float32) * factor
    )
    grad_queries = grad_queries.astype(jnp.bfloat16).reshape(count, width)
    grad_keys = (
        jnp.einsum("hqk,qhd->khd", grad_scores, queries, preferred_element_type=jnp.float32)
        * factor
    )
    grad_keys = grad_keys.astype(jnp.bfloat16).reshape(count, width)
    grad_query_bias = jnp.sum(grad_queries.astype(jnp.float32), 0)
    grad_value_bias = jnp.sum(grad_values.astype(jnp.float32), 0)
    grad_query_weight = jnp.einsum(
        "tc,td->cd", attn_in, grad_queries, preferred_element_type=jnp.float32
    )
    grad_key_weight = jnp.einsum(
        "tc,td->cd", attn_in, grad_keys, preferred_element_type=jnp.float32
    )
    grad_value_weight = jnp.einsum(
        "tc,td->cd", attn_in, grad_values, preferred_element_type=jnp.float32
    )
    grad_attn = jnp.einsum(
        "td,cd->tc", grad_queries, query_weight, preferred_element_type=jnp.float32
    )
    grad_attn = grad_attn + jnp.einsum(
        "td,cd->tc", grad_keys, key_weight, preferred_element_type=jnp.float32
    )
    grad_attn = grad_attn + jnp.einsum(
        "td,cd->tc", grad_values, value_weight, preferred_element_type=jnp.float32
    )
    grad_first, grad_first_gain, grad_first_shift = norm_backward(
        grad_attn, first_normed, first_inverse, first_gain
    )
    grad_tokens = (grad_resid + grad_first).astype(jnp.bfloat16)
    sums = spread(
        (
            grad_first_gain,
            grad_first_shift,
            grad_query_weight,
            grad_query_bias,
            grad_key_weight,
            grad_value_weight,
            grad_value_bias,
            grad_out_weight,
            grad_out_bias,
            grad_second_gain,
            grad_second_shift,
            grad_up_weight,
            grad_up_bias,
            grad_down_weight,
            grad_down_bias,
        )
    )
    return (grad_tokens, sums)


def body(
    tokens,
    cotangent,
    seq_length,
    first_gain,
    first_shift,
    query_weight,
    query_bias,
    key_weight,
    value_weight,
    value_bias,
    out_weight,
    out_bias,
    second_gain,
    second_shift,
    up_weight,
    up_bias,
    down_weight,
    down_bias,
):
    shards = (
        first_gain,
        first_shift,
        query_weight,
        query_bias,
        key_weight,
        value_weight,
        value_bias,
        out_weight,
        out_bias,
        second_gain,
        second_shift,
        up_weight,
        up_bias,
        down_weight,
        down_bias,
    )
    length = seq_length[0]
    weights = collect(shards)
    kept = forward(tokens, length, weights)
    grad_tokens, sums = backward(cotangent, length, weights, kept)
    (
        g_first_gain,
        g_first_shift,
        g_query_weight,
        g_query_bias,
        g_key_weight,
        g_value_weight,
        g_value_bias,
        g_out_weight,
        g_out_bias,
        g_second_gain,
        g_second_shift,
        g_up_weight,
        g_up_bias,
        g_down_weight,
        g_down_bias,
    ) = sums
    return (
        kept[0],
        grad_tokens,
        g_first_gain,
        g_first_shift,
        g_query_weight,
        g_query_bias,
        g_key_weight,
        g_value_weight,
        g_value_bias,
        g_out_weight,
        g_out_bias,
        g_second_gain,
        g_second_shift,
        g_up_weight,
        g_up_bias,
        g_down_weight,
        g_down_bias,
    )


def solution(mesh):
    placed = (
        P(("wide", "narrow"), None),
        P(("wide", "narrow"), None),
        P(("wide", "narrow")),
        P(("wide", "narrow")),
        P(("wide", "narrow")),
        P(("wide", "narrow"), None),
        P(("wide", "narrow")),
        P(("wide", "narrow"), None),
        P(("wide", "narrow"), None),
        P(("wide", "narrow")),
        P(("wide", "narrow"), None),
        P(("wide", "narrow")),
        P(("wide", "narrow")),
        P(("wide", "narrow")),
        P(("wide", "narrow"), None),
        P(("wide", "narrow")),
        P(("wide", "narrow"), None),
        P(("wide", "narrow")),
    )
    return jax.shard_map(
        body,
        mesh=mesh,
        in_specs=placed,
        out_specs=(
            P(("wide", "narrow"), None),
            P(("wide", "narrow"), None),
            P(("wide", "narrow")),
            P(("wide", "narrow")),
            P(("wide", "narrow"), None),
            P(("wide", "narrow")),
            P(("wide", "narrow"), None),
            P(("wide", "narrow"), None),
            P(("wide", "narrow")),
            P(("wide", "narrow"), None),
            P(("wide", "narrow")),
            P(("wide", "narrow")),
            P(("wide", "narrow")),
            P(("wide", "narrow"), None),
            P(("wide", "narrow")),
            P(("wide", "narrow"), None),
            P(("wide", "narrow")),
        ),
        check_vma=False,
    )
```

```python
import functools

import jax
import jax.numpy as jnp
from jax import lax
from jax.experimental import pallas as pl
from jax.experimental.pallas import tpu as pltpu
from jax.sharding import PartitionSpec as P

H = 8
HD = 128
AXES = ("wide", "narrow")
MESH = pl.DeviceIdType.MESH
BF = jnp.bfloat16
F32 = jnp.float32


class Place:
    def __init__(self):
        wide, narrow = lax.axis_index("wide"), lax.axis_index("narrow")
        self.z, self.x = lax.div(wide, 2), lax.rem(wide, 2)
        self.y, self.c = lax.div(narrow, 2), lax.rem(narrow, 2)
        c, x, y = self.c, self.x, self.y
        self.one = (x + (1 - c) * (1 - 2 * x), y + c * (1 - 2 * y))
        self.two = (x + c * (1 - 2 * x), y + (1 - c) * (1 - 2 * y))
        self.far = (1 - x, 1 - y)
        self.here = (x, y)

    def device(self, z, xy, c):
        return (z * 2 + xy[0], xy[1] * 2 + c)

    def up(self, step):
        return lax.rem(self.z + step, 4)

    def down(self, step):
        return lax.rem(self.z + 4 - step, 4)

    def partners(self):
        z, c = self.z, self.c
        return [self.device(self.up(step), self.here, c) for step in (1, 2, 3)] + [
            self.device(z, self.one, c),
            self.device(z, self.two, c),
            self.device(z, self.here, 1 - c),
        ]

    def greet(self):
        barrier = pltpu.get_barrier_semaphore()
        partners = self.partners()
        for partner in partners:
            pl.semaphore_signal(barrier, inc=1, device_id=partner, device_id_type=MESH)
        pl.semaphore_wait(barrier, len(partners))


def remote(source, target, send, recv, device):
    return pltpu.make_async_remote_copy(
        src_ref=source,
        dst_ref=target,
        send_sem=send,
        recv_sem=recv,
        device_id=device,
        device_id_type=MESH,
    )


class Gathering:
    SEMS = 10
    STAGES = 5

    def __init__(self, place, local, full, send, recv, keep):
        self.place, self.local, self.full = place, local, full
        self.send, self.recv, self.keep = send, recv, keep

    def block(self, xy, c):
        return self.full.at[:, xy[0], xy[1], c]

    def cell(self, z):
        place = self.place
        return self.full.at[z, place.x, place.y, place.c]

    def copy(self, source, target, sem, device):
        return remote(source, target, self.send.at[sem], self.recv.at[sem], device)

    def along(self, step):
        place = self.place
        device = place.device(place.up(step), place.here, place.c)
        return self.copy(self.local, self.cell(place.z), step - 1, device)

    def pieces(self):
        place = self.place
        z, c = place.z, place.c
        one, two = place.device(z, place.one, c), place.device(z, place.two, c)
        twin = place.device(z, place.here, 1 - c)
        mine, first = self.block(place.here, c), self.block(place.one, c)
        second, far = self.block(place.two, c), self.block(place.far, c)
        return {
            3: (mine, one, self.block(place.one, c)),
            4: (mine, two, self.block(place.two, c)),
            5: (mine, twin, self.block(place.here, 1 - c)),
            6: (first, two, self.block(place.far, c)),
            7: (first, twin, self.block(place.two, 1 - c)),
            8: (second, twin, self.block(place.one, 1 - c)),
            9: (far, twin, self.block(place.far, 1 - c)),
        }

    def start(self, sem):
        source, device, _ = self.pieces()[sem]
        self.copy(source, source, sem, device).start()

    def await_recv(self, sem):
        _, device, landing = self.pieces()[sem]
        self.copy(landing, landing, sem, device).wait_recv()

    def own(self):
        return pltpu.make_async_copy(self.local, self.cell(self.place.z), self.keep)

    def stage(self, number):
        place = self.place
        if number == 0:
            self.own().start()
            for step in (1, 2, 3):
                self.along(step).start()
        elif number == 1:
            self.own().wait()
            for step in (1, 2, 3):
                cell = self.cell(place.down(step))
                device = place.device(place.down(step), place.here, place.c)
                self.copy(cell, cell, step - 1, device).wait_recv()
            for sem in (3, 4, 5):
                self.start(sem)
        elif number == 2:
            self.await_recv(3)
            self.start(6)
            self.start(7)
            self.await_recv(4)
            self.start(8)
        elif number == 3:
            self.await_recv(6)
            self.start(9)
        elif number == 4:
            for sem in (5, 7, 8, 9):
                self.await_recv(sem)

    def finish(self):
        for step in (1, 2, 3):
            self.along(step).wait_send()
        for sem in range(3, 10):
            source, device, _ = self.pieces()[sem]
            self.copy(source, source, sem, device).wait_send()


class Scattering:
    SEMS = 7
    STAGES = 5

    def __init__(self, place, partial, mine, total, pair, line, out, send, recv, load):
        self.place, self.partial, self.mine = place, partial, mine
        self.total, self.pair, self.line, self.out = total, pair, line, out
        self.send, self.recv, self.load = send, recv, load

    def pieces(self):
        place = self.place
        z, c = place.z, place.c
        one, two = place.device(z, place.one, c), place.device(z, place.two, c)
        twin = place.device(z, place.here, 1 - c)
        total = self.total

        def block(xy):
            return total.at[:, xy[0], xy[1]]

        table = {
            0: (self.partial.at[:, :, :, 1 - c], total, twin),
            1: (block(place.two), self.pair.at[0], two),
            2: (block(place.far), self.pair.at[1], two),
            3: (block(place.one), self.pair.at[2], one),
        }
        for step in (1, 2, 3):
            device = place.device(place.up(step), place.here, c)
            table[3 + step] = (
                total.at[place.up(step), place.x, place.y],
                self.line.at[step - 1],
                device,
            )
        return table

    def copy(self, sem):
        source, target, device = self.pieces()[sem]
        return remote(source, target, self.send.at[sem], self.recv.at[sem], device)

    def own(self):
        return pltpu.make_async_copy(
            self.partial.at[:, :, :, self.place.c], self.mine, self.load
        )

    def stage(self, number):
        place, total, pair = self.place, self.total, self.pair

        def add(xy, slot):
            def body(z, carry):
                value = total[z, xy[0], xy[1]].astype(F32) + pair[slot, z].astype(F32)
                total[z, xy[0], xy[1]] = value.astype(BF)
                return carry

            lax.fori_loop(0, 4, body, 0)

        if number == 0:
            self.own().start()
            self.copy(0).start()
        elif number == 1:
            self.own().wait()
            self.copy(0).wait_recv()

            def body(z, carry):
                for x in range(2):
                    for y in range(2):
                        value = total[z, x, y].astype(F32) + self.mine[z, x, y].astype(F32)
                        total[z, x, y] = value.astype(BF)
                return carry

            lax.fori_loop(0, 4, body, 0)
            self.copy(2).start()
            self.copy(1).start()
        elif number == 2:
            self.copy(2).wait_recv()
            add(place.one, 1)
            self.copy(3).start()
            self.copy(1).wait_recv()
            add(place.here, 0)
        elif number == 3:
            self.copy(3).wait_recv()
            add(place.here, 2)
            for step in (1, 2, 3):
                self.copy(3 + step).start()
        elif number == 4:
            value = total[place.z, place.x, place.y].astype(F32)
            for step in (1, 2, 3):
                self.copy(3 + step).wait_recv()
                value = value + self.line[step - 1].astype(F32)
            self.out[...] = value

    def finish(self):
        for sem in range(7):
            self.copy(sem).wait_send()


class Summing:
    SEMS = 6

    def __init__(self, place, value, total, slots, send, recv):
        self.place, self.value, self.total, self.slots = place, value, total, slots
        self.send, self.recv = send, recv

    def copy(self, sem):
        place = self.place
        device = [
            place.device(place.z, place.here, 1 - place.c),
            place.device(place.z, place.one, place.c),
            place.device(place.z, place.two, place.c),
        ] + [place.device(place.up(step), place.here, place.c) for step in (1, 2, 3)]
        source = self.total.at[min(sem, 3)]
        return remote(source, self.slots.at[sem], self.send.at[sem], self.recv.at[sem], device[sem])

    def stage(self, number):
        total, slots = self.total, self.slots
        if number == 0:
            total[0] = self.value[...]
            self.copy(0).start()
        elif number < 3:
            self.copy(number - 1).wait_recv()
            total[number] = total[number - 1] + slots[number - 1]
            self.copy(number).start()
        elif number == 3:
            self.copy(2).wait_recv()
            total[3] = total[2] + slots[2]
            for sem in (3, 4, 5):
                self.copy(sem).start()
        elif number == 4:
            value = total[3]
            for sem in (3, 4, 5):
                self.copy(sem).wait_recv()
                value = value + slots[sem]
            total[4] = value

    def finish(self):
        for sem in range(6):
            self.copy(sem).wait_send()


def pipeline(tasks, stages):
    for tick in range(len(tasks) + stages - 1):
        for number in reversed(range(stages)):
            if 0 <= tick - number < len(tasks):
                tasks[tick - number].stage(number)


def halves(ref, count, width):
    if count == 1:
        return [ref]
    lead = (slice(None),) * (len(ref.shape) - 1)
    return [ref.at[lead + (pl.ds(i * width, width),)] for i in range(count)]


CUTS = (1, 1, 1, 1, 1, 2, 2)


def gather_kernel(*refs):
    count = len(CUTS)
    local, full = refs[:count], refs[count : 2 * count]
    send, recv, keep = refs[2 * count :]
    place = Place()
    place.greet()
    tasks = []
    for source, target, cut in zip(local, full, CUTS):
        width = source.shape[-1] // cut
        for one, other in zip(halves(source, cut, width), halves(target, cut, width)):
            g = len(tasks)
            tasks.append(Gathering(place, one, other, send.at[g], recv.at[g], keep.at[g]))
    pipeline(tasks, Gathering.STAGES)
    for task in tasks:
        task.finish()


def gather_all(arrays):
    groups = sum(CUTS)
    results = pl.pallas_call(
        gather_kernel,
        out_shape=[jax.ShapeDtypeStruct((4, 2, 2, 2) + a.shape, a.dtype) for a in arrays],
        in_specs=[pl.BlockSpec(memory_space=pltpu.HBM)] * len(arrays),
        out_specs=[pl.BlockSpec(memory_space=pltpu.HBM)] * len(arrays),
        scratch_shapes=[
            pltpu.SemaphoreType.DMA((groups, Gathering.SEMS)),
            pltpu.SemaphoreType.DMA((groups, Gathering.SEMS)),
            pltpu.SemaphoreType.DMA((groups,)),
        ],
        compiler_params=pltpu.CompilerParams(collective_id=0, has_side_effects=True),
    )(*arrays)
    return results


def scatter_kernel(cuts, *refs):
    count = len(cuts)
    small, partial = refs[0], refs[1 : 1 + count]
    small_out, out = refs[1 + count], refs[2 + count : 2 + 2 * count]
    rest = list(refs[2 + 2 * count :])
    mine, total, pair, line = (rest[i * count : (i + 1) * count] for i in range(4))
    small_total, small_slots, small_send, small_recv, send, recv, load = rest[4 * count :]
    place = Place()
    place.greet()
    tasks = []
    g = 0
    for i, cut in enumerate(cuts):
        width = partial[i].shape[-1] // cut
        views = [
            halves(ref, cut, width)
            for ref in (partial[i], mine[i], total[i], pair[i], line[i], out[i])
        ]
        for j in range(cut):
            tasks.append(
                Scattering(place, *(view[j] for view in views), send.at[g], recv.at[g], load.at[g])
            )
            g += 1
    sums = Summing(place, small, small_total, small_slots, small_send, small_recv)
    tasks.insert(1, sums)
    pipeline(tasks, Scattering.STAGES)
    for task in tasks:
        task.finish()
    small_out[...] = small_total[4]


def scatter_all(small, arrays, cuts):
    groups = sum(cuts)
    shards = [a.shape[4:] for a in arrays]
    vmem = pl.BlockSpec(memory_space=pltpu.VMEM)
    results = pl.pallas_call(
        functools.partial(scatter_kernel, cuts),
        out_shape=[jax.ShapeDtypeStruct(small.shape, F32)]
        + [jax.ShapeDtypeStruct(s, F32) for s in shards],
        in_specs=[vmem] + [pl.BlockSpec(memory_space=pltpu.HBM)] * len(arrays),
        out_specs=[vmem] * (1 + len(arrays)),
        scratch_shapes=[pltpu.VMEM((4, 2, 2) + s, BF) for s in shards]
        + [pltpu.VMEM((4, 2, 2) + s, BF) for s in shards]
        + [pltpu.VMEM((3, 4) + s, BF) for s in shards]
        + [pltpu.VMEM((3,) + s, BF) for s in shards]
        + [
            pltpu.VMEM((5,) + small.shape, F32),
            pltpu.VMEM((6,) + small.shape, F32),
            pltpu.SemaphoreType.DMA((Summing.SEMS,)),
            pltpu.SemaphoreType.DMA((Summing.SEMS,)),
            pltpu.SemaphoreType.DMA((groups, Scattering.SEMS)),
            pltpu.SemaphoreType.DMA((groups, Scattering.SEMS)),
            pltpu.SemaphoreType.DMA((groups,)),
        ],
        compiler_params=pltpu.CompilerParams(
            collective_id=1, has_side_effects=True, vmem_limit_bytes=60 << 20
        ),
    )(small, *arrays)
    return results[0], results[1:]


SMALL = (0, 1, 3, 6, 8, 9, 10, 14, 12)
LARGE = (2, 4, 5, 7, 11, 13)


def collect_fast(parts):
    flat = jnp.concatenate([parts[i].astype(F32) for i in SMALL]).reshape(-1, 128)
    flat = jnp.pad(flat, ((0, 8 - flat.shape[0]), (0, 0)))
    small, *large = gather_all([flat] + [parts[i] for i in LARGE])
    small = small.reshape(32, -1)
    whole = [None] * len(parts)
    start = 0
    for i in SMALL:
        size = parts[i].shape[0]
        whole[i] = small[:, start : start + size].reshape(-1).astype(parts[i].dtype)
        start += size
    for i, array in zip(LARGE, large):
        whole[i] = array.reshape(-1, array.shape[-1])
    return tuple(whole)


def spread_fast(parts):
    small = jnp.concatenate([parts[i] for i in SMALL]).reshape(-1, 1024)
    rows = small.shape[0]
    small = jnp.pad(small, ((0, 16 - rows), (0, 0)))
    order = (13, 11, 7, 2, 4, 5)
    arrays = [
        parts[i].astype(BF).reshape(4, 2, 2, 2, parts[i].shape[0] // 32, parts[i].shape[1])
        for i in order
    ]
    small, large = scatter_all(small, arrays, (2, 2, 1, 1, 1, 1))
    result = [None] * len(parts)
    for i, array in zip(order, large):
        result[i] = array
    flat = small.reshape(-1)
    me = lax.axis_index("wide") * 4 + lax.axis_index("narrow")
    start = 0
    for i in SMALL:
        size = parts[i].shape[0]
        result[i] = lax.dynamic_slice(flat, (start + me * (size // 32),), (size // 32,))
        start += size
    return tuple(result)

EPSILON = 1e-05


def collect_plain(parts):
    (
        first_gain,
        first_shift,
        query_weight,
        query_bias,
        key_weight,
        value_weight,
        value_bias,
        out_weight,
        out_bias,
        second_gain,
        second_shift,
        up_weight,
        up_bias,
        down_weight,
        down_bias,
    ) = parts
    return (
        lax.all_gather(first_gain, ("wide", "narrow"), axis=0, tiled=True),
        lax.all_gather(first_shift, ("wide", "narrow"), axis=0, tiled=True),
        lax.all_gather(query_weight, ("wide", "narrow"), axis=0, tiled=True),
        lax.all_gather(query_bias, ("wide", "narrow"), axis=0, tiled=True),
        lax.all_gather(key_weight, ("wide", "narrow"), axis=0, tiled=True),
        lax.all_gather(value_weight, ("wide", "narrow"), axis=0, tiled=True),
        lax.all_gather(value_bias, ("wide", "narrow"), axis=0, tiled=True),
        lax.all_gather(out_weight, ("wide", "narrow"), axis=0, tiled=True),
        lax.all_gather(out_bias, ("wide", "narrow"), axis=0, tiled=True),
        lax.all_gather(second_gain, ("wide", "narrow"), axis=0, tiled=True),
        lax.all_gather(second_shift, ("wide", "narrow"), axis=0, tiled=True),
        lax.all_gather(up_weight, ("wide", "narrow"), axis=0, tiled=True),
        lax.all_gather(up_bias, ("wide", "narrow"), axis=0, tiled=True),
        lax.all_gather(down_weight, ("wide", "narrow"), axis=0, tiled=True),
        lax.all_gather(down_bias, ("wide", "narrow"), axis=0, tiled=True),
    )


def spread_plain(parts):
    (
        first_gain,
        first_shift,
        query_weight,
        query_bias,
        key_weight,
        value_weight,
        value_bias,
        out_weight,
        out_bias,
        second_gain,
        second_shift,
        up_weight,
        up_bias,
        down_weight,
        down_bias,
    ) = parts
    return (
        lax.psum_scatter(first_gain, ("wide", "narrow"), scatter_dimension=0, tiled=True),
        lax.psum_scatter(first_shift, ("wide", "narrow"), scatter_dimension=0, tiled=True),
        lax.psum_scatter(query_weight, ("wide", "narrow"), scatter_dimension=0, tiled=True),
        lax.psum_scatter(query_bias, ("wide", "narrow"), scatter_dimension=0, tiled=True),
        lax.psum_scatter(key_weight, ("wide", "narrow"), scatter_dimension=0, tiled=True),
        lax.psum_scatter(value_weight, ("wide", "narrow"), scatter_dimension=0, tiled=True),
        lax.psum_scatter(value_bias, ("wide", "narrow"), scatter_dimension=0, tiled=True),
        lax.psum_scatter(out_weight, ("wide", "narrow"), scatter_dimension=0, tiled=True),
        lax.psum_scatter(out_bias, ("wide", "narrow"), scatter_dimension=0, tiled=True),
        lax.psum_scatter(second_gain, ("wide", "narrow"), scatter_dimension=0, tiled=True),
        lax.psum_scatter(second_shift, ("wide", "narrow"), scatter_dimension=0, tiled=True),
        lax.psum_scatter(up_weight, ("wide", "narrow"), scatter_dimension=0, tiled=True),
        lax.psum_scatter(up_bias, ("wide", "narrow"), scatter_dimension=0, tiled=True),
        lax.psum_scatter(down_weight, ("wide", "narrow"), scatter_dimension=0, tiled=True),
        lax.psum_scatter(down_bias, ("wide", "narrow"), scatter_dimension=0, tiled=True),
    )


LOG2E = 1.4426950408889634
WEIGHTS = ("query", "key", "value", "out", "up", "down")


def dot(left, right, form):
    dims = (((0,) if form[0] == "T" else (1,), (1,) if form[1] == "T" else (0,)), ((), ()))
    return lax.dot_general(left, right, dims, preferred_element_type=F32)


def at(index, size):
    return pl.ds(pl.multiple_of(index * size, size), size)


def loop(count, body):
    def step(i, carry):
        body(i)
        return carry

    lax.fori_loop(0, count, step, 0)


def normed_rows(value):
    center = value - jnp.mean(value, -1, keepdims=True)
    inverse = lax.rsqrt(jnp.mean(center * center, -1, keepdims=True) + EPSILON)
    return center * inverse, inverse


def gelu_pair(hidden):
    cdf = 0.5 * (1.0 + lax.erf(hidden * 0.7071067811865476))
    density = jnp.exp2(hidden * hidden * (-0.5 * LOG2E)) * 0.3989422804014327
    return hidden * cdf, cdf + hidden * density


def unpack_small(small, vec):
    table = small.reshape(256, 128)
    values = table[...].astype(BF)
    lane = lax.broadcasted_iota(jnp.int32, (128, 1024), 0)
    column = lax.broadcasted_iota(jnp.int32, (128, 1024), 1)
    row = lax.broadcasted_iota(jnp.int32, (256, 1024), 0)
    owner = lax.div(lax.broadcasted_iota(jnp.int32, (256, 1024), 1), 32) * 8
    for part in range(4):
        pick = jnp.where(lane == part * 32 + lax.rem(column, 32), 1.0, 0.0).astype(BF)
        spread_out = dot(values, pick, "NN")
        for line in range(2):
            chosen = jnp.where(row == owner + line, spread_out, 0.0)
            index = line * 4 + part
            vec[index : index + 1, :] = jnp.sum(chosen, 0, keepdims=True)
    for part in range(4):
        for block in range(8):
            source = (part * 8 + block) * 8 + 2
            vec[8 + part : 9 + part, block * 128 : block * 128 + 128] = table[source : source + 1, :]


def prepare_bias(length, mask, ramp):
    key = lax.broadcasted_iota(jnp.int32, (256, 256), 0)
    query = lax.broadcasted_iota(jnp.int32, (256, 256), 1)
    long = length == 1024
    same = (lax.div(key, 128) == lax.div(query, 128)) | long
    mask[...] = jnp.where((key <= query) & same, 0.0, -1e30)
    ramp[...] = lax.broadcasted_iota(jnp.int32, (1024, 128), 0).astype(F32)
    return jnp.where(long, 0.0, -1e30)


def wide(value):
    return jnp.concatenate([value, value], axis=1)


def attention_head(head, slope, off, queries, keys, values, mixed, lse, mask, ramp, tilt):
    cols = at(head, 128)
    factor = HD**-0.5 * LOG2E
    tilt[...] = ramp[...] * slope
    for i in range(4):
        rows, before = slice(i * 256, i * 256 + 256), slice(0, i * 256)
        query = queries[rows, cols]
        near = dot(keys[rows, cols], query, "NT") * factor + wide(tilt[rows, :]) + mask[...]
        top = jnp.max(near, 0, keepdims=True)
        if i:
            past = dot(keys[before, cols], query, "NT") * factor + wide(tilt[before, :])
            top = jnp.maximum(top, jnp.max(past, 0, keepdims=True) + off)
        near = jnp.exp2(near - top)
        total = jnp.sum(near, 0, keepdims=True)
        out = dot(values[rows, cols], near.astype(BF), "TN")
        if i:
            past = jnp.exp2(past + (off - top))
            total = total + jnp.sum(past, 0, keepdims=True)
            out = out + dot(values[before, cols], past.astype(BF), "TN")
        mixed[rows, cols] = (out * (1.0 / total)).T.astype(BF)
        lse[pl.ds(head, 1), rows] = top + jnp.log2(total)


def forward_kernel(length_ref, tokens, *refs):
    refs = list(refs)

    def take(count):
        taken, refs[:count] = refs[:count], []
        return taken

    local = take(7)
    result_out, resid_out, lse_out, small_out = take(4)
    attn_out, query_out, key_out, value_out, mixed_out, ffn_out, active_out, slope_out = take(8)
    weight_out = take(6)
    full = take(7)
    act, slope, mixed, ffn_in = take(4)
    resid, vec, lse, mask, ramp, tilt = take(6)
    send, recv, keep, store, dump = take(5)

    place = Place()
    place.greet()
    tasks, dumps = [], []
    for i, cut in enumerate((1, 1, 1, 1, 1, 4, 4)):
        width = local[i].shape[-1] // cut
        for j in range(cut):
            g = len(tasks)
            views = [halves(ref, cut, width)[j] for ref in (local[i], full[i])]
            tasks.append(Gathering(place, *views, send.at[g], recv.at[g], keep.at[g]))
            if i:
                target = halves(weight_out[i - 1], cut, width)[j]
                dumps.append(pltpu.make_async_copy(views[1], target, dump.at[g - 1]))

    def tick(number):
        for stage in reversed(range(Gathering.STAGES)):
            g = number - stage
            if 0 <= g < len(tasks):
                tasks[g].stage(stage)
                if stage == Gathering.STAGES - 1 and g:
                    dumps[g - 1].start()

    saves = []

    def save(source, target):
        copy = pltpu.make_async_copy(source, target, store.at[len(saves)])
        copy.start()
        saves.append(copy)

    query_w, key_w, value_w, out_w = (ref.reshape(1024, 1024) for ref in full[1:5])
    up_w, down_w = full[5].reshape(1024, 4096), full[6].reshape(4096, 1024)
    attn_in, queries, keys, values = (act.at[i] for i in range(4))
    length = length_ref[0]
    off = prepare_bias(length, mask, ramp)

    for number in range(5):
        tick(number)
    unpack_small(full[0], vec)

    def first_norm(i):
        rows = at(i, 128)
        normed, _ = normed_rows(tokens[rows, :].astype(F32))
        attn_in[rows, :] = (normed * vec[0:1, :] + vec[1:2, :]).astype(BF)

    loop(8, first_norm)
    save(attn_in, attn_out)

    def project(weight, target, bias):
        def body(i):
            cols = at(i, 512)
            value = dot(attn_in[...], weight[:, cols], "NN")
            if bias is not None:
                value = value + vec[bias : bias + 1, cols]
            target[:, cols] = value.astype(BF)

        loop(2, body)

    tick(5)
    project(query_w, queries, 2)
    save(queries, query_out)
    tick(6)
    project(key_w, keys, None)
    save(keys, key_out)
    tick(7)
    project(value_w, values, 3)
    save(values, value_out)

    def heads(first):
        def body(i, slope_now):
            attention_head(
                first + i, slope_now, off, queries, keys, values, mixed, lse, mask, ramp, tilt
            )
            return slope_now * 0.5

        lax.fori_loop(0, 2, body, jnp.float32(LOG2E * 0.5 ** (first + 1)))

    for pair in range(4):
        heads(2 * pair)
        if pair < 3:
            tick(8 + pair)
    save(mixed, mixed_out)
    save(lse, lse_out)

    def close_attention(i):
        rows = at(i, 256)
        value = dot(mixed[rows, :], out_w[...], "NN") + tokens[rows, :].astype(F32) + vec[4:5, :]
        resid[rows, :] = value
        normed, _ = normed_rows(value)
        ffn_in[rows, :] = (normed * vec[5:6, :] + vec[6:7, :]).astype(BF)

    loop(4, close_attention)
    save(resid, resid_out)
    save(ffn_in, ffn_out)
    for copy in saves[:5]:
        copy.wait()

    def widen(chunk):
        def body(i):
            rows, cols = at(lax.div(i, 2), 512), at(lax.rem(i, 2), 512)
            weight = up_w[:, at(chunk * 2 + lax.rem(i, 2), 512)]
            hidden = dot(ffn_in[rows, :], weight, "NN") + vec[8 + chunk : 9 + chunk, cols]
            active, steep = gelu_pair(hidden)
            act[chunk, rows, cols] = active.astype(BF)
            slope[chunk, rows, cols] = steep.astype(BF)

        loop(4, body)
        save(act.at[chunk], active_out.at[chunk])
        save(slope.at[chunk], slope_out.at[chunk])

    widen(0)
    widen(1)
    tick(11)
    widen(2)
    tick(12)
    widen(3)

    def narrow(chunk):
        cols = slice(chunk * 256, chunk * 256 + 256)

        def body(i):
            rows = at(i, 512)
            value = resid[rows, cols] + vec[7:8, cols]
            active = jnp.concatenate([act[j, rows, :] for j in range(4)], axis=1)
            value = value + dot(active, down_w[:, cols], "NN")
            mixed[rows, cols] = value.astype(BF)

        loop(2, body)

    for chunk in range(4):
        tick(13 + chunk)
        narrow(chunk)
    save(mixed, result_out)
    small_out[...] = vec[...]
    for task in tasks:
        task.finish()
    for copy in saves[5:]:
        copy.wait()
    for copy in dumps:
        copy.wait()


def forward_all(length, tokens, flat, weights):
    square = jax.ShapeDtypeStruct((1024, 1024), BF)
    tall = jax.ShapeDtypeStruct((4, 1024, 1024), BF)
    f32 = functools.partial(jax.ShapeDtypeStruct, dtype=F32)
    grid6 = [(4, 2, 2, 2) + w.shape for w in weights]
    hbm, vmem = pl.BlockSpec(memory_space=pltpu.HBM), pl.BlockSpec(memory_space=pltpu.VMEM)
    return pl.pallas_call(
        forward_kernel,
        out_shape=[square, f32((1024, 1024)), f32((8, 1024)), f32((16, 1024))]
        + [square] * 6
        + [tall] * 2
        + [jax.ShapeDtypeStruct(s, BF) for s in grid6],
        in_specs=[pl.BlockSpec(memory_space=pltpu.SMEM)] + [vmem] * 8,
        out_specs=[hbm, hbm, hbm, vmem] + [hbm] * 14,
        scratch_shapes=[pltpu.VMEM((4, 2, 2, 2) + flat.shape, F32)]
        + [pltpu.VMEM(s, BF) for s in grid6]
        + [pltpu.VMEM((4, 1024, 1024), BF)] * 2
        + [pltpu.VMEM((1024, 1024), BF)] * 2
        + [
            pltpu.VMEM((1024, 1024), F32),
            pltpu.VMEM((16, 1024), F32),
            pltpu.VMEM((8, 1024), F32),
            pltpu.VMEM((256, 256), F32),
            pltpu.VMEM((1024, 128), F32),
            pltpu.VMEM((1024, 128), F32),
            pltpu.SemaphoreType.DMA((13, Gathering.SEMS)),
            pltpu.SemaphoreType.DMA((13, Gathering.SEMS)),
            pltpu.SemaphoreType.DMA((13,)),
            pltpu.SemaphoreType.DMA((17,)),
            pltpu.SemaphoreType.DMA((12,)),
        ],
        compiler_params=pltpu.CompilerParams(
            collective_id=2, has_side_effects=True, vmem_limit_bytes=60 << 20
        ),
    )(length, tokens, flat, *weights)


def pack_small(parts):
    flat = jnp.concatenate([parts[i].astype(F32) for i in SMALL]).reshape(-1, 128)
    return jnp.pad(flat, ((0, 8 - flat.shape[0]), (0, 0)))


def forward_fast(tokens, seq_length, parts):
    out = forward_all(seq_length, tokens, pack_small(parts), [parts[i] for i in LARGE])
    result, resid, lse, vec, attn_in, queries, keys, values, mixed, ffn_in, active, slope = out[:12]
    large = out[12:]
    whole = [None] * 15
    for row, i in enumerate((0, 1, 3, 6, 8, 9, 10, 14)):
        whole[i] = vec[row].astype(BF)
    whole[12] = vec[8:12].reshape(-1).astype(BF)
    for i, array in zip(LARGE, large):
        whole[i] = array.reshape(-1, array.shape[-1])
    count = tokens.shape[0]
    center = tokens.astype(F32)
    center = center - jnp.mean(center, -1, keepdims=True)
    inv1 = lax.rsqrt(jnp.mean(center * center, -1, keepdims=True) + EPSILON)
    c2 = resid - jnp.mean(resid, -1, keepdims=True)
    inv2 = lax.rsqrt(jnp.mean(c2 * c2, -1, keepdims=True) + EPSILON)
    slopes = jnp.exp2(-8.0 * jnp.arange(1, H + 1, dtype=F32) / H)
    natural = lse / LOG2E - slopes[:, None] * jnp.arange(count, dtype=F32)[None]
    flat4 = lambda a: a.transpose(1, 0, 2).reshape(count, -1)
    kept = (result, attn_in, center * inv1, inv1) + tuple(
        a.reshape(count, H, HD) for a in (queries, keys, values)
    ) + (natural[:, :, None], mixed, c2 * inv2, inv2, ffn_in, flat4(slope).astype(F32), flat4(active))
    return tuple(whole), kept


def is_fast():
    return lax.axis_size("wide") == 8 and lax.axis_size("narrow") == 4


def collect(parts):
    return collect_fast(parts) if is_fast() else collect_plain(parts)


def spread(parts):
    return spread_fast(parts) if is_fast() else spread_plain(parts)


def norm_forward(value, gain, shift):
    center = value - jnp.mean(value, -1, keepdims=True)
    inverse = lax.rsqrt(jnp.mean(center * center, -1, keepdims=True) + EPSILON)
    normed = center * inverse
    return (normed * gain.astype(jnp.float32) + shift.astype(jnp.float32), normed, inverse)


def norm_backward(incoming, normed, inverse, gain):
    scaled = incoming * gain.astype(jnp.float32)
    inner = (
        scaled
        - jnp.mean(scaled, -1, keepdims=True)
        - normed * jnp.mean(scaled * normed, -1, keepdims=True)
    )
    return (inverse * inner, jnp.sum(incoming * normed, 0), jnp.sum(incoming, 0))


def gelu_parts(hidden):
    cdf = 0.5 * (1.0 + lax.erf(hidden * 0.7071067811865476))
    density = jnp.exp(-0.5 * hidden * hidden) * 0.3989422804014327
    return (hidden * cdf, cdf + hidden * density)


def masked_scores(queries, keys, length):
    count = queries.shape[0]
    raw = jnp.einsum("qhd,khd->hqk", queries, keys, preferred_element_type=jnp.float32) * HD ** (
        -0.5
    )
    position = jnp.arange(count, dtype=jnp.int32)
    distance = (position[:, None] - position[None, :]).astype(jnp.float32)
    slopes = jnp.exp2(-8.0 * jnp.arange(1, H + 1, dtype=jnp.float32) / H)
    raw = raw - slopes[:, None, None] * distance[None]
    allowed = (position[:, None] >= position[None, :]) & (
        position[:, None] // length == position[None, :] // length
    )
    return jnp.where(allowed[None], raw, -1e30)


def forward(tokens, length, weights):
    (
        first_gain,
        first_shift,
        query_weight,
        query_bias,
        key_weight,
        value_weight,
        value_bias,
        out_weight,
        out_bias,
        second_gain,
        second_shift,
        up_weight,
        up_bias,
        down_weight,
        down_bias,
    ) = weights
    count = tokens.shape[0]
    width = tokens.shape[1]
    inputs = tokens.astype(jnp.float32)
    first_out, first_normed, first_inverse = norm_forward(inputs, first_gain, first_shift)
    attn_in = first_out.astype(jnp.bfloat16)
    queries = (
        (
            jnp.dot(attn_in, query_weight, preferred_element_type=jnp.float32)
            + query_bias.astype(jnp.float32)
        )
        .astype(jnp.bfloat16)
        .reshape(count, H, HD)
    )
    keys = (
        jnp.dot(attn_in, key_weight, preferred_element_type=jnp.float32)
        .astype(jnp.bfloat16)
        .reshape(count, H, HD)
    )
    values = (
        (
            jnp.dot(attn_in, value_weight, preferred_element_type=jnp.float32)
            + value_bias.astype(jnp.float32)
        )
        .astype(jnp.bfloat16)
        .reshape(count, H, HD)
    )
    scores = masked_scores(queries, keys, length)
    top = jnp.max(scores, -1, keepdims=True)
    expo = jnp.exp(scores - top)
    total = jnp.sum(expo, -1, keepdims=True)
    probs = expo / total
    log_total = top + jnp.log(total)
    mixed = jnp.einsum(
        "hqk,khd->qhd", probs.astype(jnp.bfloat16), values, preferred_element_type=jnp.float32
    )
    mixed = mixed.reshape(count, width).astype(jnp.bfloat16)
    resid = (
        inputs
        + jnp.dot(mixed, out_weight, preferred_element_type=jnp.float32)
        + out_bias.astype(jnp.float32)
    )
    second_out, second_normed, second_inverse = norm_forward(resid, second_gain, second_shift)
    ffn_in = second_out.astype(jnp.bfloat16)
    hidden = jnp.dot(ffn_in, up_weight, preferred_element_type=jnp.float32) + up_bias.astype(
        jnp.float32
    )
    active, active_slope = gelu_parts(hidden)
    active_low = active.astype(jnp.bfloat16)
    result = (
        resid
        + jnp.dot(active_low, down_weight, preferred_element_type=jnp.float32)
        + down_bias.astype(jnp.float32)
    )
    return (
        result.astype(jnp.bfloat16),
        attn_in,
        first_normed,
        first_inverse,
        queries,
        keys,
        values,
        log_total,
        mixed,
        second_normed,
        second_inverse,
        ffn_in,
        active_slope,
        active_low,
    )


def backward(cotangent, length, weights, kept):
    (
        first_gain,
        first_shift,
        query_weight,
        query_bias,
        key_weight,
        value_weight,
        value_bias,
        out_weight,
        out_bias,
        second_gain,
        second_shift,
        up_weight,
        up_bias,
        down_weight,
        down_bias,
    ) = weights
    (
        result,
        attn_in,
        first_normed,
        first_inverse,
        queries,
        keys,
        values,
        log_total,
        mixed,
        second_normed,
        second_inverse,
        ffn_in,
        active_slope,
        active_low,
    ) = kept
    count = cotangent.shape[0]
    width = cotangent.shape[1]
    grad_out = cotangent.astype(jnp.float32)
    grad_down_bias = jnp.sum(grad_out, 0)
    grad_down_weight = jnp.einsum(
        "tf,td->fd", active_low, cotangent, preferred_element_type=jnp.float32
    )
    grad_active = jnp.einsum(
        "td,fd->tf", cotangent, down_weight, preferred_element_type=jnp.float32
    )
    grad_hidden = (grad_active * active_slope).astype(jnp.bfloat16)
    grad_up_bias = jnp.sum(grad_hidden.astype(jnp.float32), 0)
    grad_up_weight = jnp.einsum(
        "td,tf->df", ffn_in, grad_hidden, preferred_element_type=jnp.float32
    )
    grad_ffn_in = jnp.einsum(
        "tf,df->td", grad_hidden, up_weight, preferred_element_type=jnp.float32
    )
    grad_second, grad_second_gain, grad_second_shift = norm_backward(
        grad_ffn_in, second_normed, second_inverse, second_gain
    )
    grad_resid = grad_out + grad_second
    grad_branch = grad_resid.astype(jnp.bfloat16)
    grad_out_bias = jnp.sum(grad_branch.astype(jnp.float32), 0)
    grad_out_weight = jnp.einsum(
        "tc,td->cd", mixed, grad_branch, preferred_element_type=jnp.float32
    )
    grad_mixed = jnp.einsum(
        "td,cd->tc", grad_branch, out_weight, preferred_element_type=jnp.float32
    )
    grad_mixed = grad_mixed.astype(jnp.bfloat16).reshape(count, H, HD)
    scores = masked_scores(queries, keys, length)
    probs = jnp.exp(scores - log_total)
    grad_probs = jnp.einsum("qhd,khd->hqk", grad_mixed, values, preferred_element_type=jnp.float32)
    grad_values = jnp.einsum(
        "hqk,qhd->khd", probs.astype(jnp.bfloat16), grad_mixed, preferred_element_type=jnp.float32
    )
    grad_values = grad_values.astype(jnp.bfloat16).reshape(count, width)
    row_total = jnp.sum(grad_probs * probs, -1, keepdims=True)
    grad_scores = (probs * (grad_probs - row_total)).astype(jnp.bfloat16)
    factor = HD ** (-0.5)
    grad_queries = (
        jnp.einsum("hqk,khd->qhd", grad_scores, keys, preferred_element_type=jnp.float32) * factor
    )
    grad_queries = grad_queries.astype(jnp.bfloat16).reshape(count, width)
    grad_keys = (
        jnp.einsum("hqk,qhd->khd", grad_scores, queries, preferred_element_type=jnp.float32)
        * factor
    )
    grad_keys = grad_keys.astype(jnp.bfloat16).reshape(count, width)
    grad_query_bias = jnp.sum(grad_queries.astype(jnp.float32), 0)
    grad_value_bias = jnp.sum(grad_values.astype(jnp.float32), 0)
    grad_query_weight = jnp.einsum(
        "tc,td->cd", attn_in, grad_queries, preferred_element_type=jnp.float32
    )
    grad_key_weight = jnp.einsum(
        "tc,td->cd", attn_in, grad_keys, preferred_element_type=jnp.float32
    )
    grad_value_weight = jnp.einsum(
        "tc,td->cd", attn_in, grad_values, preferred_element_type=jnp.float32
    )
    grad_attn = jnp.einsum(
        "td,cd->tc", grad_queries, query_weight, preferred_element_type=jnp.float32
    )
    grad_attn = grad_attn + jnp.einsum(
        "td,cd->tc", grad_keys, key_weight, preferred_element_type=jnp.float32
    )
    grad_attn = grad_attn + jnp.einsum(
        "td,cd->tc", grad_values, value_weight, preferred_element_type=jnp.float32
    )
    grad_first, grad_first_gain, grad_first_shift = norm_backward(
        grad_attn, first_normed, first_inverse, first_gain
    )
    grad_tokens = (grad_resid + grad_first).astype(jnp.bfloat16)
    sums = spread(
        (
            grad_first_gain,
            grad_first_shift,
            grad_query_weight,
            grad_query_bias,
            grad_key_weight,
            grad_value_weight,
            grad_value_bias,
            grad_out_weight,
            grad_out_bias,
            grad_second_gain,
            grad_second_shift,
            grad_up_weight,
            grad_up_bias,
            grad_down_weight,
            grad_down_bias,
        )
    )
    return (grad_tokens, sums)


def body(
    tokens,
    cotangent,
    seq_length,
    first_gain,
    first_shift,
    query_weight,
    query_bias,
    key_weight,
    value_weight,
    value_bias,
    out_weight,
    out_bias,
    second_gain,
    second_shift,
    up_weight,
    up_bias,
    down_weight,
    down_bias,
):
    shards = (
        first_gain,
        first_shift,
        query_weight,
        query_bias,
        key_weight,
        value_weight,
        value_bias,
        out_weight,
        out_bias,
        second_gain,
        second_shift,
        up_weight,
        up_bias,
        down_weight,
        down_bias,
    )
    length = seq_length[0]
    if is_fast():
        weights, kept = forward_fast(tokens, seq_length, shards)
    else:
        weights = collect(shards)
        kept = forward(tokens, length, weights)
    grad_tokens, sums = backward(cotangent, length, weights, kept)
    (
        g_first_gain,
        g_first_shift,
        g_query_weight,
        g_query_bias,
        g_key_weight,
        g_value_weight,
        g_value_bias,
        g_out_weight,
        g_out_bias,
        g_second_gain,
        g_second_shift,
        g_up_weight,
        g_up_bias,
        g_down_weight,
        g_down_bias,
    ) = sums
    return (
        kept[0],
        grad_tokens,
        g_first_gain,
        g_first_shift,
        g_query_weight,
        g_query_bias,
        g_key_weight,
        g_value_weight,
        g_value_bias,
        g_out_weight,
        g_out_bias,
        g_second_gain,
        g_second_shift,
        g_up_weight,
        g_up_bias,
        g_down_weight,
        g_down_bias,
    )


def solution(mesh):
    placed = (
        P(("wide", "narrow"), None),
        P(("wide", "narrow"), None),
        P(("wide", "narrow")),
        P(("wide", "narrow")),
        P(("wide", "narrow")),
        P(("wide", "narrow"), None),
        P(("wide", "narrow")),
        P(("wide", "narrow"), None),
        P(("wide", "narrow"), None),
        P(("wide", "narrow")),
        P(("wide", "narrow"), None),
        P(("wide", "narrow")),
        P(("wide", "narrow")),
        P(("wide", "narrow")),
        P(("wide", "narrow"), None),
        P(("wide", "narrow")),
        P(("wide", "narrow"), None),
        P(("wide", "narrow")),
    )
    return jax.shard_map(
        body,
        mesh=mesh,
        in_specs=placed,
        out_specs=(
            P(("wide", "narrow"), None),
            P(("wide", "narrow"), None),
            P(("wide", "narrow")),
            P(("wide", "narrow")),
            P(("wide", "narrow"), None),
            P(("wide", "narrow")),
            P(("wide", "narrow"), None),
            P(("wide", "narrow"), None),
            P(("wide", "narrow")),
            P(("wide", "narrow"), None),
            P(("wide", "narrow")),
            P(("wide", "narrow")),
            P(("wide", "narrow")),
            P(("wide", "narrow"), None),
            P(("wide", "narrow")),
            P(("wide", "narrow"), None),
            P(("wide", "narrow")),
        ),
        check_vma=False,
    )
```

```python
import functools

import jax
import jax.numpy as jnp
from jax import lax
from jax.experimental import pallas as pl
from jax.experimental.pallas import tpu as pltpu
from jax.sharding import PartitionSpec as P

H = 8
HD = 128
AXES = ("wide", "narrow")
MESH = pl.DeviceIdType.MESH
BF = jnp.bfloat16
F32 = jnp.float32


class Place:
    def __init__(self):
        wide, narrow = lax.axis_index("wide"), lax.axis_index("narrow")
        self.z, self.x = lax.div(wide, 2), lax.rem(wide, 2)
        self.y, self.c = lax.div(narrow, 2), lax.rem(narrow, 2)
        c, x, y = self.c, self.x, self.y
        self.one = (x + (1 - c) * (1 - 2 * x), y + c * (1 - 2 * y))
        self.two = (x + c * (1 - 2 * x), y + (1 - c) * (1 - 2 * y))
        self.far = (1 - x, 1 - y)
        self.here = (x, y)

    def device(self, z, xy, c):
        return (z * 2 + xy[0], xy[1] * 2 + c)

    def up(self, step):
        return lax.rem(self.z + step, 4)

    def down(self, step):
        return lax.rem(self.z + 4 - step, 4)

    def partners(self):
        z, c = self.z, self.c
        return [self.device(self.up(step), self.here, c) for step in (1, 2, 3)] + [
            self.device(z, self.one, c),
            self.device(z, self.two, c),
            self.device(z, self.here, 1 - c),
        ]

    def greet(self):
        barrier = pltpu.get_barrier_semaphore()
        partners = self.partners()
        for partner in partners:
            pl.semaphore_signal(barrier, inc=1, device_id=partner, device_id_type=MESH)
        pl.semaphore_wait(barrier, len(partners))


def remote(source, target, send, recv, device):
    return pltpu.make_async_remote_copy(
        src_ref=source,
        dst_ref=target,
        send_sem=send,
        recv_sem=recv,
        device_id=device,
        device_id_type=MESH,
    )


class Gathering:
    SEMS = 10
    STAGES = 5

    def __init__(self, place, local, full, send, recv, keep):
        self.place, self.local, self.full = place, local, full
        self.send, self.recv, self.keep = send, recv, keep

    def block(self, xy, c):
        return self.full.at[:, xy[0], xy[1], c]

    def cell(self, z):
        place = self.place
        return self.full.at[z, place.x, place.y, place.c]

    def copy(self, source, target, sem, device):
        return remote(source, target, self.send.at[sem], self.recv.at[sem], device)

    def along(self, step):
        place = self.place
        device = place.device(place.up(step), place.here, place.c)
        return self.copy(self.local, self.cell(place.z), step - 1, device)

    def pieces(self):
        place = self.place
        z, c = place.z, place.c
        one, two = place.device(z, place.one, c), place.device(z, place.two, c)
        twin = place.device(z, place.here, 1 - c)
        mine, first = self.block(place.here, c), self.block(place.one, c)
        second, far = self.block(place.two, c), self.block(place.far, c)
        return {
            3: (mine, one, self.block(place.one, c)),
            4: (mine, two, self.block(place.two, c)),
            5: (mine, twin, self.block(place.here, 1 - c)),
            6: (first, two, self.block(place.far, c)),
            7: (first, twin, self.block(place.two, 1 - c)),
            8: (second, twin, self.block(place.one, 1 - c)),
            9: (far, twin, self.block(place.far, 1 - c)),
        }

    def start(self, sem):
        source, device, _ = self.pieces()[sem]
        self.copy(source, source, sem, device).start()

    def await_recv(self, sem):
        _, device, landing = self.pieces()[sem]
        self.copy(landing, landing, sem, device).wait_recv()

    def own(self):
        return pltpu.make_async_copy(self.local, self.cell(self.place.z), self.keep)

    def stage(self, number):
        place = self.place
        if number == 0:
            self.own().start()
            for step in (1, 2, 3):
                self.along(step).start()
        elif number == 1:
            self.own().wait()
            for step in (1, 2, 3):
                cell = self.cell(place.down(step))
                device = place.device(place.down(step), place.here, place.c)
                self.copy(cell, cell, step - 1, device).wait_recv()
            for sem in (3, 4, 5):
                self.start(sem)
        elif number == 2:
            self.await_recv(3)
            self.start(6)
            self.start(7)
            self.await_recv(4)
            self.start(8)
        elif number == 3:
            self.await_recv(6)
            self.start(9)
        elif number == 4:
            for sem in (5, 7, 8, 9):
                self.await_recv(sem)

    def finish(self):
        for step in (1, 2, 3):
            self.along(step).wait_send()
        for sem in range(3, 10):
            source, device, _ = self.pieces()[sem]
            self.copy(source, source, sem, device).wait_send()


class Scattering:
    SEMS = 7
    STAGES = 5

    def __init__(self, place, partial, mine, total, pair, line, out, send, recv, load):
        self.place, self.partial, self.mine = place, partial, mine
        self.total, self.pair, self.line, self.out = total, pair, line, out
        self.send, self.recv, self.load = send, recv, load

    def pieces(self):
        place = self.place
        z, c = place.z, place.c
        one, two = place.device(z, place.one, c), place.device(z, place.two, c)
        twin = place.device(z, place.here, 1 - c)
        total = self.total

        def block(xy):
            return total.at[:, xy[0], xy[1]]

        table = {
            0: (self.partial.at[:, :, :, 1 - c], total, twin),
            1: (block(place.two), self.pair.at[0], two),
            2: (block(place.far), self.pair.at[1], two),
            3: (block(place.one), self.pair.at[2], one),
        }
        for step in (1, 2, 3):
            device = place.device(place.up(step), place.here, c)
            table[3 + step] = (
                total.at[place.up(step), place.x, place.y],
                self.line.at[step - 1],
                device,
            )
        return table

    def copy(self, sem):
        source, target, device = self.pieces()[sem]
        return remote(source, target, self.send.at[sem], self.recv.at[sem], device)

    def own(self):
        return pltpu.make_async_copy(
            self.partial.at[:, :, :, self.place.c], self.mine, self.load
        )

    def stage(self, number):
        place, total, pair = self.place, self.total, self.pair

        def add(xy, slot):
            def body(z, carry):
                value = total[z, xy[0], xy[1]].astype(F32) + pair[slot, z].astype(F32)
                total[z, xy[0], xy[1]] = value.astype(BF)
                return carry

            lax.fori_loop(0, 4, body, 0)

        if number == 0:
            self.own().start()
            self.copy(0).start()
        elif number == 1:
            self.own().wait()
            self.copy(0).wait_recv()

            def body(z, carry):
                for x in range(2):
                    for y in range(2):
                        value = total[z, x, y].astype(F32) + self.mine[z, x, y].astype(F32)
                        total[z, x, y] = value.astype(BF)
                return carry

            lax.fori_loop(0, 4, body, 0)
            self.copy(2).start()
            self.copy(1).start()
        elif number == 2:
            self.copy(2).wait_recv()
            add(place.one, 1)
            self.copy(3).start()
            self.copy(1).wait_recv()
            add(place.here, 0)
        elif number == 3:
            self.copy(3).wait_recv()
            add(place.here, 2)
            for step in (1, 2, 3):
                self.copy(3 + step).start()
        elif number == 4:
            value = total[place.z, place.x, place.y].astype(F32)
            for step in (1, 2, 3):
                self.copy(3 + step).wait_recv()
                value = value + self.line[step - 1].astype(F32)
            self.out[...] = value

    def finish(self):
        for sem in range(7):
            self.copy(sem).wait_send()


class Summing:
    SEMS = 6

    def __init__(self, place, value, total, slots, send, recv):
        self.place, self.value, self.total, self.slots = place, value, total, slots
        self.send, self.recv = send, recv

    def copy(self, sem):
        place = self.place
        device = [
            place.device(place.z, place.here, 1 - place.c),
            place.device(place.z, place.one, place.c),
            place.device(place.z, place.two, place.c),
        ] + [place.device(place.up(step), place.here, place.c) for step in (1, 2, 3)]
        source = self.total.at[min(sem, 3)]
        return remote(source, self.slots.at[sem], self.send.at[sem], self.recv.at[sem], device[sem])

    def stage(self, number):
        total, slots = self.total, self.slots
        if number == 0:
            total[0] = self.value[...]
            self.copy(0).start()
        elif number < 3:
            self.copy(number - 1).wait_recv()
            total[number] = total[number - 1] + slots[number - 1]
            self.copy(number).start()
        elif number == 3:
            self.copy(2).wait_recv()
            total[3] = total[2] + slots[2]
            for sem in (3, 4, 5):
                self.copy(sem).start()
        elif number == 4:
            value = total[3]
            for sem in (3, 4, 5):
                self.copy(sem).wait_recv()
                value = value + slots[sem]
            total[4] = value

    def finish(self):
        for sem in range(6):
            self.copy(sem).wait_send()


def pipeline(tasks, stages):
    for tick in range(len(tasks) + stages - 1):
        for number in reversed(range(stages)):
            if 0 <= tick - number < len(tasks):
                tasks[tick - number].stage(number)


def halves(ref, count, width):
    if count == 1:
        return [ref]
    lead = (slice(None),) * (len(ref.shape) - 1)
    return [ref.at[lead + (pl.ds(i * width, width),)] for i in range(count)]


SMALL = (0, 1, 3, 6, 8, 9, 10, 14, 12)
LARGE = (2, 4, 5, 7, 11, 13)


EPSILON = 1e-05


def collect(parts):
    (
        first_gain,
        first_shift,
        query_weight,
        query_bias,
        key_weight,
        value_weight,
        value_bias,
        out_weight,
        out_bias,
        second_gain,
        second_shift,
        up_weight,
        up_bias,
        down_weight,
        down_bias,
    ) = parts
    return (
        lax.all_gather(first_gain, ("wide", "narrow"), axis=0, tiled=True),
        lax.all_gather(first_shift, ("wide", "narrow"), axis=0, tiled=True),
        lax.all_gather(query_weight, ("wide", "narrow"), axis=0, tiled=True),
        lax.all_gather(query_bias, ("wide", "narrow"), axis=0, tiled=True),
        lax.all_gather(key_weight, ("wide", "narrow"), axis=0, tiled=True),
        lax.all_gather(value_weight, ("wide", "narrow"), axis=0, tiled=True),
        lax.all_gather(value_bias, ("wide", "narrow"), axis=0, tiled=True),
        lax.all_gather(out_weight, ("wide", "narrow"), axis=0, tiled=True),
        lax.all_gather(out_bias, ("wide", "narrow"), axis=0, tiled=True),
        lax.all_gather(second_gain, ("wide", "narrow"), axis=0, tiled=True),
        lax.all_gather(second_shift, ("wide", "narrow"), axis=0, tiled=True),
        lax.all_gather(up_weight, ("wide", "narrow"), axis=0, tiled=True),
        lax.all_gather(up_bias, ("wide", "narrow"), axis=0, tiled=True),
        lax.all_gather(down_weight, ("wide", "narrow"), axis=0, tiled=True),
        lax.all_gather(down_bias, ("wide", "narrow"), axis=0, tiled=True),
    )


def spread(parts):
    (
        first_gain,
        first_shift,
        query_weight,
        query_bias,
        key_weight,
        value_weight,
        value_bias,
        out_weight,
        out_bias,
        second_gain,
        second_shift,
        up_weight,
        up_bias,
        down_weight,
        down_bias,
    ) = parts
    return (
        lax.psum_scatter(first_gain, ("wide", "narrow"), scatter_dimension=0, tiled=True),
        lax.psum_scatter(first_shift, ("wide", "narrow"), scatter_dimension=0, tiled=True),
        lax.psum_scatter(query_weight, ("wide", "narrow"), scatter_dimension=0, tiled=True),
        lax.psum_scatter(query_bias, ("wide", "narrow"), scatter_dimension=0, tiled=True),
        lax.psum_scatter(key_weight, ("wide", "narrow"), scatter_dimension=0, tiled=True),
        lax.psum_scatter(value_weight, ("wide", "narrow"), scatter_dimension=0, tiled=True),
        lax.psum_scatter(value_bias, ("wide", "narrow"), scatter_dimension=0, tiled=True),
        lax.psum_scatter(out_weight, ("wide", "narrow"), scatter_dimension=0, tiled=True),
        lax.psum_scatter(out_bias, ("wide", "narrow"), scatter_dimension=0, tiled=True),
        lax.psum_scatter(second_gain, ("wide", "narrow"), scatter_dimension=0, tiled=True),
        lax.psum_scatter(second_shift, ("wide", "narrow"), scatter_dimension=0, tiled=True),
        lax.psum_scatter(up_weight, ("wide", "narrow"), scatter_dimension=0, tiled=True),
        lax.psum_scatter(up_bias, ("wide", "narrow"), scatter_dimension=0, tiled=True),
        lax.psum_scatter(down_weight, ("wide", "narrow"), scatter_dimension=0, tiled=True),
        lax.psum_scatter(down_bias, ("wide", "narrow"), scatter_dimension=0, tiled=True),
    )


LOG2E = 1.4426950408889634
WEIGHTS = ("query", "key", "value", "out", "up", "down")


def dot(left, right, form):
    dims = (((0,) if form[0] == "T" else (1,), (1,) if form[1] == "T" else (0,)), ((), ()))
    return lax.dot_general(left, right, dims, preferred_element_type=F32)


def at(index, size):
    return pl.ds(pl.multiple_of(index * size, size), size)


def loop(count, body):
    def step(i, carry):
        body(i)
        return carry

    lax.fori_loop(0, count, step, 0)


def normed_rows(value):
    center = value - jnp.mean(value, -1, keepdims=True)
    inverse = lax.rsqrt(jnp.mean(center * center, -1, keepdims=True) + EPSILON)
    return center * inverse, inverse


def gelu_pair(hidden):
    cdf = 0.5 * (1.0 + lax.erf(hidden * 0.7071067811865476))
    density = jnp.exp2(hidden * hidden * (-0.5 * LOG2E)) * 0.3989422804014327
    return hidden * cdf, cdf + hidden * density


def unpack_small(small, vec):
    table = small.reshape(256, 128)
    values = table[...].astype(BF)
    lane = lax.broadcasted_iota(jnp.int32, (128, 1024), 0)
    column = lax.broadcasted_iota(jnp.int32, (128, 1024), 1)
    row = lax.broadcasted_iota(jnp.int32, (256, 1024), 0)
    owner = lax.div(lax.broadcasted_iota(jnp.int32, (256, 1024), 1), 32) * 8
    for part in range(4):
        pick = jnp.where(lane == part * 32 + lax.rem(column, 32), 1.0, 0.0).astype(BF)
        spread_out = dot(values, pick, "NN")
        for line in range(2):
            chosen = jnp.where(row == owner + line, spread_out, 0.0)
            index = line * 4 + part
            vec[index : index + 1, :] = jnp.sum(chosen, 0, keepdims=True)
    for part in range(4):
        for block in range(8):
            source = (part * 8 + block) * 8 + 2
            vec[8 + part : 9 + part, block * 128 : block * 128 + 128] = table[source : source + 1, :]


def prepare_bias(length, mask, ramp):
    key = lax.broadcasted_iota(jnp.int32, (256, 256), 0)
    query = lax.broadcasted_iota(jnp.int32, (256, 256), 1)
    long = length == 1024
    same = (lax.div(key, 128) == lax.div(query, 128)) | long
    mask[...] = jnp.where((key <= query) & same, 0.0, -1e30)
    ramp[...] = lax.broadcasted_iota(jnp.int32, (1024, 128), 0).astype(F32)
    return jnp.where(long, 0.0, -1e30)


def wide(value):
    return jnp.concatenate([value, value], axis=1)


def attention_head(head, slope, off, queries, keys, values, mixed, lse, mask, ramp, tilt):
    cols = at(head, 128)
    factor = HD**-0.5 * LOG2E
    tilt[...] = ramp[...] * slope
    for i in range(4):
        rows, before = slice(i * 256, i * 256 + 256), slice(0, i * 256)
        query = queries[rows, cols]
        near = dot(keys[rows, cols], query, "NT") * factor + wide(tilt[rows, :]) + mask[...]
        top = jnp.max(near, 0, keepdims=True)
        if i:
            past = dot(keys[before, cols], query, "NT") * factor + wide(tilt[before, :])
            top = jnp.maximum(top, jnp.max(past, 0, keepdims=True) + off)
        near = jnp.exp2(near - top)
        total = jnp.sum(near, 0, keepdims=True)
        out = dot(values[rows, cols], near.astype(BF), "TN")
        if i:
            past = jnp.exp2(past + (off - top))
            total = total + jnp.sum(past, 0, keepdims=True)
            out = out + dot(values[before, cols], past.astype(BF), "TN")
        mixed[rows, cols] = (out * (1.0 / total)).T.astype(BF)
        lse[pl.ds(head, 1), rows] = top + jnp.log2(total)


def forward_kernel(length_ref, tokens, cotangent, *refs):
    refs = list(refs)

    def take(count):
        taken, refs[:count] = refs[:count], []
        return taken

    local = take(7)
    result_out, resid_out, lse_out, small_out, down_out = take(5)
    attn_out, query_out, key_out, value_out, mixed_out, ffn_out, slope_out = take(7)
    weight_out = take(6)
    full = take(7)
    act, slope, mixed, ffn_in = take(4)
    resid, vec, lse, mask, ramp, tilt, stage = take(7)
    send, recv, keep, store, dump, stage_sem = take(6)

    place = Place()
    place.greet()
    tasks, dumps = [], []
    for i, cut in enumerate((1, 1, 1, 1, 1, 4, 4)):
        width = local[i].shape[-1] // cut
        for j in range(cut):
            g = len(tasks)
            views = [halves(ref, cut, width)[j] for ref in (local[i], full[i])]
            tasks.append(Gathering(place, *views, send.at[g], recv.at[g], keep.at[g]))
            if i:
                target = halves(weight_out[i - 1], cut, width)[j]
                dumps.append(pltpu.make_async_copy(views[1], target, dump.at[g - 1]))

    def tick(number):
        for stage in reversed(range(Gathering.STAGES)):
            g = number - stage
            if 0 <= g < len(tasks):
                tasks[g].stage(stage)
                if stage == Gathering.STAGES - 1 and g:
                    dumps[g - 1].start()

    saves = []

    def save(source, target):
        copy = pltpu.make_async_copy(source, target, store.at[len(saves)])
        copy.start()
        saves.append(copy)

    query_w, key_w, value_w, out_w = (ref.reshape(1024, 1024) for ref in full[1:5])
    up_w, down_w = full[5].reshape(1024, 4096), full[6].reshape(4096, 1024)
    attn_in, queries, keys, values = (act.at[i] for i in range(4))
    length = length_ref[0]
    off = prepare_bias(length, mask, ramp)

    for number in range(5):
        tick(number)
    unpack_small(full[0], vec)

    def first_norm(i):
        rows = at(i, 128)
        normed, _ = normed_rows(tokens[rows, :].astype(F32))
        attn_in[rows, :] = (normed * vec[0:1, :] + vec[1:2, :]).astype(BF)

    loop(8, first_norm)
    save(attn_in, attn_out)

    def project(weight, target, bias):
        def body(i):
            cols = at(i, 512)
            value = dot(attn_in[...], weight[:, cols], "NN")
            if bias is not None:
                value = value + vec[bias : bias + 1, cols]
            target[:, cols] = value.astype(BF)

        loop(2, body)

    tick(5)
    project(query_w, queries, 2)
    save(queries, query_out)
    tick(6)
    project(key_w, keys, None)
    save(keys, key_out)
    tick(7)
    project(value_w, values, 3)
    save(values, value_out)

    def heads(first):
        def body(i, slope_now):
            attention_head(
                first + i, slope_now, off, queries, keys, values, mixed, lse, mask, ramp, tilt
            )
            return slope_now * 0.5

        lax.fori_loop(0, 2, body, jnp.float32(LOG2E * 0.5 ** (first + 1)))

    for pair in range(4):
        heads(2 * pair)
        if pair < 3:
            tick(8 + pair)
    save(mixed, mixed_out)
    save(lse, lse_out)

    def close_attention(i):
        rows = at(i, 256)
        value = dot(mixed[rows, :], out_w[...], "NN") + tokens[rows, :].astype(F32) + vec[4:5, :]
        resid[rows, :] = value
        normed, _ = normed_rows(value)
        ffn_in[rows, :] = (normed * vec[5:6, :] + vec[6:7, :]).astype(BF)

    loop(4, close_attention)
    save(resid, resid_out)
    save(ffn_in, ffn_out)
    for copy in saves[:5]:
        copy.wait()

    def widen(chunk):
        def body(i):
            rows, cols = at(lax.div(i, 2), 512), at(lax.rem(i, 2), 512)
            weight = up_w[:, at(chunk * 2 + lax.rem(i, 2), 512)]
            hidden = dot(ffn_in[rows, :], weight, "NN") + vec[8 + chunk : 9 + chunk, cols]
            active, steep = gelu_pair(hidden)
            act[chunk, rows, cols] = active.astype(BF)
            slope[chunk % 2, rows, cols] = steep.astype(BF)

        if chunk > 1:
            saves[8 + chunk - 2].wait()
        loop(4, body)
        save(slope.at[chunk % 2], slope_out.at[chunk])

    widen(0)
    widen(1)
    tick(11)
    widen(2)
    tick(12)
    widen(3)

    def spill(j, half):
        rows = pl.ds(pl.multiple_of(j * 1024 + half * 512, 512), 512)
        return pltpu.make_async_copy(stage.at[half], down_out.at[rows, :], stage_sem.at[half])

    def grad_down(j):
        for half in range(2):

            @pl.when(j > 0)
            def _():
                spill(j - 1, half).wait()

            active = act[j, :, half * 512 : half * 512 + 512]
            stage[half] = dot(active, cotangent[...], "TN").astype(BF)
            spill(j, half).start()

    loop(4, grad_down)

    def narrow(chunk):
        cols = slice(chunk * 256, chunk * 256 + 256)

        def body(i):
            rows = at(i, 512)
            value = resid[rows, cols] + vec[7:8, cols]
            active = jnp.concatenate([act[j, rows, :] for j in range(4)], axis=1)
            value = value + dot(active, down_w[:, cols], "NN")
            mixed[rows, cols] = value.astype(BF)

        loop(2, body)

    for chunk in range(4):
        tick(13 + chunk)
        narrow(chunk)
    save(mixed, result_out)
    small_out[...] = vec[...]
    for half in range(2):
        spill(3, half).wait()
    for task in tasks:
        task.finish()
    for copy in saves[5:8] + saves[10:]:
        copy.wait()
    for copy in dumps:
        copy.wait()


def forward_all(length, tokens, cotangent, flat, weights):
    square = jax.ShapeDtypeStruct((1024, 1024), BF)
    tall = jax.ShapeDtypeStruct((4, 1024, 1024), BF)
    f32 = functools.partial(jax.ShapeDtypeStruct, dtype=F32)
    grid6 = [(4, 2, 2, 2) + w.shape for w in weights]
    hbm, vmem = pl.BlockSpec(memory_space=pltpu.HBM), pl.BlockSpec(memory_space=pltpu.VMEM)
    return pl.pallas_call(
        forward_kernel,
        out_shape=[square, f32((1024, 1024)), f32((8, 1024)), f32((16, 1024))]
        + [jax.ShapeDtypeStruct((4096, 1024), BF)]
        + [square] * 6
        + [tall]
        + [jax.ShapeDtypeStruct(s, BF) for s in grid6],
        in_specs=[pl.BlockSpec(memory_space=pltpu.SMEM)] + [vmem] * 9,
        out_specs=[hbm, hbm, hbm, vmem] + [hbm] * 14,
        scratch_shapes=[pltpu.VMEM((4, 2, 2, 2) + flat.shape, F32)]
        + [pltpu.VMEM(s, BF) for s in grid6]
        + [pltpu.VMEM((4, 1024, 1024), BF), pltpu.VMEM((2, 1024, 1024), BF)]
        + [pltpu.VMEM((1024, 1024), BF)] * 2
        + [
            pltpu.VMEM((1024, 1024), F32),
            pltpu.VMEM((16, 1024), F32),
            pltpu.VMEM((8, 1024), F32),
            pltpu.VMEM((256, 256), F32),
            pltpu.VMEM((1024, 128), F32),
            pltpu.VMEM((1024, 128), F32),
            pltpu.VMEM((2, 512, 1024), BF),
            pltpu.SemaphoreType.DMA((13, Gathering.SEMS)),
            pltpu.SemaphoreType.DMA((13, Gathering.SEMS)),
            pltpu.SemaphoreType.DMA((13,)),
            pltpu.SemaphoreType.DMA((17,)),
            pltpu.SemaphoreType.DMA((12,)),
            pltpu.SemaphoreType.DMA((2,)),
        ],
        compiler_params=pltpu.CompilerParams(
            collective_id=2, has_side_effects=True, vmem_limit_bytes=62 << 20
        ),
    )(length, tokens, cotangent, flat, *weights)


def pack_small(parts):
    flat = jnp.concatenate([parts[i].astype(F32) for i in SMALL]).reshape(-1, 128)
    return jnp.pad(flat, ((0, 8 - flat.shape[0]), (0, 0)))


SHARDS = ("down", "up", "out", "query", "key", "value")
SCATTER_CUTS = (4, 4, 1, 1, 1, 1)


def attention_head_back(head, slope, off, refs, lse, mask, ramp, tilt, key_sum, value_sum):
    queries, keys, values, mixed, grad_mixed = refs
    cols = at(head, 128)
    factor = HD**-0.5 * LOG2E
    tilt[...] = ramp[...] * slope
    for i in (3, 2, 1, 0):
        rows, upto, before = slice(i * 256, i * 256 + 256), slice(0, i * 256 + 256), i * 256
        query, grad = queries[rows, cols], grad_mixed[rows, cols]
        product = grad.astype(F32) * mixed[rows, cols].astype(F32)
        inner = jnp.sum(product.T, 0, keepdims=True)
        level = lse[pl.ds(head, 1), rows]
        raw = dot(keys[upto, cols], query, "NT") * factor + wide(tilt[upto, :])
        probs = jnp.exp2(raw[before:] + mask[...] - level)
        if i:
            probs = jnp.concatenate([jnp.exp2(raw[:before] + (off - level)), probs], axis=0)
        grad_probs = dot(values[upto, cols], grad, "NT")
        grad_scores = (probs * (grad_probs - inner)).astype(BF)
        value_part = dot(probs.astype(BF), grad, "NN")
        key_part = dot(grad_scores, query, "NN")
        if i == 3:
            value_sum[...] = value_part
            key_sum[...] = key_part
        else:
            value_sum[upto, :] += value_part
            key_sum[upto, :] += key_part
        query_part = dot(keys[upto, cols], grad_scores, "TN") * HD**-0.5
        queries[rows, cols] = query_part.T.astype(BF)
    keys[:, cols] = (key_sum[...] * HD**-0.5).astype(BF)
    values[:, cols] = value_sum[...].astype(BF)


def backward_kernel(length_ref, vec, lse, *refs):
    refs = list(refs)

    def take(count):
        taken, refs[:count] = refs[:count], []
        return taken

    tokens, cotangent, attn_in, queries, keys, values, mixed, ffn_in, slope, resid = take(10)
    query_w, key_w, value_w, out_w, up_w, down_w, down_part = take(7)
    grad_tokens_out, small_out = take(2)
    out = take(6)
    parts = [down_part] + take(5)
    total, pair, line = take(6), take(6), take(6)
    mine_down, mine, arena, grad, stage, strip = take(6)
    key_sum, value_sum, mask, ramp, tilt, sums = take(6)
    small_total, small_slots, small_send, small_recv = take(4)
    send, recv, load_sem, slot_sem, stage_sem, strip_sem = take(6)

    place = Place()
    loads = {}

    def load(source, slot):
        copy = pltpu.make_async_copy(source, arena.at[slot], slot_sem.at[slot])
        copy.start()
        loads[slot] = copy

    def ready(slot):
        loads.pop(slot).wait()
        return arena.at[slot]

    def load_chunk(j):
        load(slope.at[j], j % 2)
        load(down_w.at[pl.ds(j * 1024, 1024), :], 2 + j % 2)
        load(up_w.at[:, pl.ds(j * 1024, 1024)], 4 + j % 2)

    load(cotangent, 6)
    load_chunk(0)
    load(ffn_in, 7)
    place.greet()

    tasks = []
    for i, cut in enumerate(SCATTER_CUTS):
        width = parts[i].shape[-1] // cut
        for j in range(cut):
            g = len(tasks)
            own = mine_down if i == 0 else mine
            views = [halves(r, cut, width)[j] for r in (parts[i], total[i], pair[i], line[i], out[i])]
            tasks.append(
                Scattering(
                    place, views[0], own, *views[1:], send.at[g], recv.at[g], load_sem.at[g]
                )
            )
    tasks.append(Summing(place, sums, small_total, small_slots, small_send, small_recv))

    def tick(number):
        for step in reversed(range(Scattering.STAGES)):
            if 0 <= number - step < len(tasks):
                tasks[number - step].stage(step)

    stages = {}

    def emit(part, left, right, width=1024, first=0):
        copies = []
        for half in range(2):
            if half in stages:
                stages.pop(half).wait()
            value = dot(left[:, half * 512 : half * 512 + 512], right[...], "TN")
            stage[half] = value.astype(BF).reshape(2, 2, 2, 2, 32, 1024)
            target = part.at[half * 2 : half * 2 + 2, :, :, :, :, pl.ds(first, width)]
            copy = pltpu.make_async_copy(stage.at[half], target, stage_sem.at[half])
            copy.start()
            stages[half] = copy
            copies.append(copy)

    def settle():
        for half in list(stages):
            stages.pop(half).wait()

    ones = jnp.ones((8, 1024), BF)

    def column_sums(source, row):
        def body(i):
            cols = at(i, 256)
            sums[row : row + 1, cols] = dot(ones, source[:, cols], "NN")[0:1]

        loop(4, body)

    length = length_ref[0]
    off = prepare_bias(length, mask, ramp)
    sums[...] = jnp.zeros_like(sums)
    tick(0)
    cot = ready(6)
    up_part = parts[1]

    for j in range(4):
        if j < 3:
            load_chunk(j + 1)
        hidden_slope, down_chunk, up_chunk = ready(j % 2), ready(2 + j % 2), ready(4 + j % 2)
        if j == 0:
            ffn = ready(7)

        def grad_hidden(i):
            cols = at(i, 512)
            value = dot(cot[...], down_chunk[cols, :], "NT") * hidden_slope[:, cols].astype(F32)
            hidden_slope[:, cols] = value.astype(BF)

        loop(2, grad_hidden)
        column_sums(hidden_slope, 8 + j)
        emit(up_part, ffn, hidden_slope, 1024, j * 1024)

        def grad_ffn(i):
            rows = at(i, 512)
            value = dot(hidden_slope[rows, :], up_chunk[...], "NT")
            if j:
                value = value + grad[rows, :]
            grad[rows, :] = value

        loop(2, grad_ffn)
        if j == 3:
            settle()
        tick(j + 1)

    def load_strip(i):
        return pltpu.make_async_copy(
            resid.at[at(i, 128), :], strip.at[lax.rem(i, 2)], strip_sem.at[lax.rem(i, 2)]
        )

    load(mixed, 2)
    load(out_w, 4)
    load(queries, 3)
    load(keys, 5)
    load(values, 7)
    load_strip(0).start()
    gain = vec[5:6, :]
    branch = arena.at[0]

    def second_norm_back(i):
        @pl.when(i < 7)
        def _():
            load_strip(i + 1).start()

        load_strip(i).wait()
        rows = at(i, 128)
        normed, inverse = normed_rows(strip[lax.rem(i, 2)])
        incoming = grad[rows, :]
        sums[5:6, :] += jnp.sum(incoming * normed, 0, keepdims=True)
        sums[6:7, :] += jnp.sum(incoming, 0, keepdims=True)
        scaled = incoming * gain
        inner = (
            scaled
            - jnp.mean(scaled, -1, keepdims=True)
            - normed * jnp.mean(scaled * normed, -1, keepdims=True)
        )
        value = cot[rows, :].astype(F32) + inverse * inner
        grad[rows, :] = value
        branch[rows, :] = value.astype(BF)

    loop(8, second_norm_back)
    column_sums(cot, 7)
    column_sums(branch, 4)
    load(query_w, 6)
    mix, out_full = ready(2), ready(4)
    grad_mixed = arena.at[1]

    def back_out(i):
        cols = at(i, 512)
        grad_mixed[:, cols] = dot(branch[...], out_full[cols, :], "NT").astype(BF)

    loop(2, back_out)
    emit(parts[2], mix, branch)
    load(key_w, 4)
    query, key, value = ready(3), ready(5), ready(7)
    tick(5)
    settle()
    load(attn_in, 0)

    def heads(first, count):
        def body(i, slope_now):
            attention_head_back(
                first + i,
                slope_now,
                off,
                (query, key, value, mix, grad_mixed),
                lse,
                mask,
                ramp,
                tilt,
                key_sum,
                value_sum,
            )
            return slope_now * 0.5

        lax.fori_loop(0, count, body, jnp.float32(LOG2E * 0.5 ** (first + 1)))

    heads(0, 3)
    tick(6)
    heads(3, 3)
    tick(7)
    heads(6, 2)
    load(value_w, 2)
    attn = ready(0)
    emit(parts[3], attn, query)
    tick(8)
    emit(parts[4], attn, key)
    emit(parts[5], attn, value)
    column_sums(query, 2)
    column_sums(value, 3)
    settle()
    tick(9)
    query_full, key_full, value_full = ready(6), ready(4), ready(2)
    load(tokens, 1)
    first_gain = vec[0:1, :]
    token_rows = ready(1)

    def first_norm_back(i):
        rows = at(i, 256)
        incoming = dot(query[rows, :], query_full[...], "NT")
        incoming = incoming + dot(key[rows, :], key_full[...], "NT")
        incoming = incoming + dot(value[rows, :], value_full[...], "NT")
        normed, inverse = normed_rows(token_rows[rows, :].astype(F32))
        sums[0:1, :] += jnp.sum(incoming * normed, 0, keepdims=True)
        sums[1:2, :] += jnp.sum(incoming, 0, keepdims=True)
        scaled = incoming * first_gain
        inner = (
            scaled
            - jnp.mean(scaled, -1, keepdims=True)
            - normed * jnp.mean(scaled * normed, -1, keepdims=True)
        )
        arena[1, rows, :] = (grad[rows, :] + inverse * inner).astype(BF)

    loop(4, first_norm_back)
    result = pltpu.make_async_copy(arena.at[1], grad_tokens_out, slot_sem.at[1])
    result.start()
    for number in range(10, len(tasks) + Scattering.STAGES - 1):
        tick(number)
    small_out[...] = small_total[4]
    result.wait()
    for task in tasks:
        task.finish()


def backward_all(length, vec, lse, arrays, shards):
    hbm, vmem = pl.BlockSpec(memory_space=pltpu.HBM), pl.BlockSpec(memory_space=pltpu.VMEM)
    groups = sum(SCATTER_CUTS)
    results = pl.pallas_call(
        backward_kernel,
        out_shape=[jax.ShapeDtypeStruct((1024, 1024), BF), jax.ShapeDtypeStruct((16, 1024), F32)]
        + [jax.ShapeDtypeStruct(s, F32) for s in shards]
        + [jax.ShapeDtypeStruct((4, 2, 2, 2) + s, BF) for s in shards[1:]],
        in_specs=[pl.BlockSpec(memory_space=pltpu.SMEM), vmem, vmem] + [hbm] * len(arrays),
        out_specs=[hbm, vmem] + [vmem] * 6 + [hbm] * 5,
        scratch_shapes=[pltpu.VMEM((4, 2, 2) + s, BF) for s in shards]
        + [pltpu.VMEM((3, 4) + s, BF) for s in shards]
        + [pltpu.VMEM((3,) + s, BF) for s in shards]
        + [
            pltpu.VMEM((4, 2, 2, 128, 256), BF),
            pltpu.VMEM((4, 2, 2, 32, 1024), BF),
            pltpu.VMEM((8, 1024, 1024), BF),
            pltpu.VMEM((1024, 1024), F32),
            pltpu.VMEM((2, 2, 2, 2, 2, 32, 1024), BF),
            pltpu.VMEM((2, 128, 1024), F32),
            pltpu.VMEM((1024, 128), F32),
            pltpu.VMEM((1024, 128), F32),
            pltpu.VMEM((256, 256), F32),
            pltpu.VMEM((1024, 128), F32),
            pltpu.VMEM((1024, 128), F32),
            pltpu.VMEM((16, 1024), F32),
            pltpu.VMEM((5, 16, 1024), F32),
            pltpu.VMEM((6, 16, 1024), F32),
            pltpu.SemaphoreType.DMA((Summing.SEMS,)),
            pltpu.SemaphoreType.DMA((Summing.SEMS,)),
            pltpu.SemaphoreType.DMA((groups, Scattering.SEMS)),
            pltpu.SemaphoreType.DMA((groups, Scattering.SEMS)),
            pltpu.SemaphoreType.DMA((groups,)),
            pltpu.SemaphoreType.DMA((8,)),
            pltpu.SemaphoreType.DMA((2,)),
            pltpu.SemaphoreType.DMA((2,)),
        ],
        compiler_params=pltpu.CompilerParams(
            collective_id=3, has_side_effects=True, vmem_limit_bytes=62 << 20
        ),
    )(length, vec, lse, *arrays)
    return results[0], results[1], results[2:8]


def fused(tokens, cotangent, seq_length, parts):
    shards = [parts[i] for i in LARGE]
    (
        result, resid, lse, vec, down_part,
        attn_in, queries, keys, values, mixed, ffn_in, slope,
        *weights,
    ) = forward_all(seq_length, tokens, cotangent, pack_small(parts), shards)
    query_w, key_w, value_w, out_w, up_w, down_w = (
        w.reshape(-1, w.shape[-1]) for w in weights
    )
    down_part = down_part.reshape(weights[5].shape)
    order = (13, 11, 7, 2, 4, 5)
    grad_tokens, small, large = backward_all(
        seq_length,
        vec,
        lse,
        [tokens, cotangent, attn_in, queries, keys, values, mixed, ffn_in, slope, resid]
        + [query_w, key_w, value_w, out_w, up_w, down_w, down_part],
        [parts[i].shape for i in order],
    )
    sums = [None] * 15
    for i, array in zip(order, large):
        sums[i] = array
    flat = small.reshape(-1)
    me = lax.axis_index("wide") * 4 + lax.axis_index("narrow")
    start = 0
    for i in SMALL:
        size = parts[i].shape[0]
        sums[i] = lax.dynamic_slice(flat, (start + me * size,), (size,))
        start += size * 32
    return result, grad_tokens, sums


def is_fast():
    return lax.axis_size("wide") == 8 and lax.axis_size("narrow") == 4


def norm_forward(value, gain, shift):
    center = value - jnp.mean(value, -1, keepdims=True)
    inverse = lax.rsqrt(jnp.mean(center * center, -1, keepdims=True) + EPSILON)
    normed = center * inverse
    return (normed * gain.astype(jnp.float32) + shift.astype(jnp.float32), normed, inverse)


def norm_backward(incoming, normed, inverse, gain):
    scaled = incoming * gain.astype(jnp.float32)
    inner = (
        scaled
        - jnp.mean(scaled, -1, keepdims=True)
        - normed * jnp.mean(scaled * normed, -1, keepdims=True)
    )
    return (inverse * inner, jnp.sum(incoming * normed, 0), jnp.sum(incoming, 0))


def gelu_parts(hidden):
    cdf = 0.5 * (1.0 + lax.erf(hidden * 0.7071067811865476))
    density = jnp.exp(-0.5 * hidden * hidden) * 0.3989422804014327
    return (hidden * cdf, cdf + hidden * density)


def masked_scores(queries, keys, length):
    count = queries.shape[0]
    raw = jnp.einsum("qhd,khd->hqk", queries, keys, preferred_element_type=jnp.float32) * HD ** (
        -0.5
    )
    position = jnp.arange(count, dtype=jnp.int32)
    distance = (position[:, None] - position[None, :]).astype(jnp.float32)
    slopes = jnp.exp2(-8.0 * jnp.arange(1, H + 1, dtype=jnp.float32) / H)
    raw = raw - slopes[:, None, None] * distance[None]
    allowed = (position[:, None] >= position[None, :]) & (
        position[:, None] // length == position[None, :] // length
    )
    return jnp.where(allowed[None], raw, -1e30)


def forward(tokens, length, weights):
    (
        first_gain,
        first_shift,
        query_weight,
        query_bias,
        key_weight,
        value_weight,
        value_bias,
        out_weight,
        out_bias,
        second_gain,
        second_shift,
        up_weight,
        up_bias,
        down_weight,
        down_bias,
    ) = weights
    count = tokens.shape[0]
    width = tokens.shape[1]
    inputs = tokens.astype(jnp.float32)
    first_out, first_normed, first_inverse = norm_forward(inputs, first_gain, first_shift)
    attn_in = first_out.astype(jnp.bfloat16)
    queries = (
        (
            jnp.dot(attn_in, query_weight, preferred_element_type=jnp.float32)
            + query_bias.astype(jnp.float32)
        )
        .astype(jnp.bfloat16)
        .reshape(count, H, HD)
    )
    keys = (
        jnp.dot(attn_in, key_weight, preferred_element_type=jnp.float32)
        .astype(jnp.bfloat16)
        .reshape(count, H, HD)
    )
    values = (
        (
            jnp.dot(attn_in, value_weight, preferred_element_type=jnp.float32)
            + value_bias.astype(jnp.float32)
        )
        .astype(jnp.bfloat16)
        .reshape(count, H, HD)
    )
    scores = masked_scores(queries, keys, length)
    top = jnp.max(scores, -1, keepdims=True)
    expo = jnp.exp(scores - top)
    total = jnp.sum(expo, -1, keepdims=True)
    probs = expo / total
    log_total = top + jnp.log(total)
    mixed = jnp.einsum(
        "hqk,khd->qhd", probs.astype(jnp.bfloat16), values, preferred_element_type=jnp.float32
    )
    mixed = mixed.reshape(count, width).astype(jnp.bfloat16)
    resid = (
        inputs
        + jnp.dot(mixed, out_weight, preferred_element_type=jnp.float32)
        + out_bias.astype(jnp.float32)
    )
    second_out, second_normed, second_inverse = norm_forward(resid, second_gain, second_shift)
    ffn_in = second_out.astype(jnp.bfloat16)
    hidden = jnp.dot(ffn_in, up_weight, preferred_element_type=jnp.float32) + up_bias.astype(
        jnp.float32
    )
    active, active_slope = gelu_parts(hidden)
    active_low = active.astype(jnp.bfloat16)
    result = (
        resid
        + jnp.dot(active_low, down_weight, preferred_element_type=jnp.float32)
        + down_bias.astype(jnp.float32)
    )
    return (
        result.astype(jnp.bfloat16),
        attn_in,
        first_normed,
        first_inverse,
        queries,
        keys,
        values,
        log_total,
        mixed,
        second_normed,
        second_inverse,
        ffn_in,
        active_slope,
        active_low,
    )


def backward(cotangent, length, weights, kept):
    (
        first_gain,
        first_shift,
        query_weight,
        query_bias,
        key_weight,
        value_weight,
        value_bias,
        out_weight,
        out_bias,
        second_gain,
        second_shift,
        up_weight,
        up_bias,
        down_weight,
        down_bias,
    ) = weights
    (
        result,
        attn_in,
        first_normed,
        first_inverse,
        queries,
        keys,
        values,
        log_total,
        mixed,
        second_normed,
        second_inverse,
        ffn_in,
        active_slope,
        active_low,
    ) = kept
    count = cotangent.shape[0]
    width = cotangent.shape[1]
    grad_out = cotangent.astype(jnp.float32)
    grad_down_bias = jnp.sum(grad_out, 0)
    grad_down_weight = jnp.einsum(
        "tf,td->fd", active_low, cotangent, preferred_element_type=jnp.float32
    )
    grad_active = jnp.einsum(
        "td,fd->tf", cotangent, down_weight, preferred_element_type=jnp.float32
    )
    grad_hidden = (grad_active * active_slope).astype(jnp.bfloat16)
    grad_up_bias = jnp.sum(grad_hidden.astype(jnp.float32), 0)
    grad_up_weight = jnp.einsum(
        "td,tf->df", ffn_in, grad_hidden, preferred_element_type=jnp.float32
    )
    grad_ffn_in = jnp.einsum(
        "tf,df->td", grad_hidden, up_weight, preferred_element_type=jnp.float32
    )
    grad_second, grad_second_gain, grad_second_shift = norm_backward(
        grad_ffn_in, second_normed, second_inverse, second_gain
    )
    grad_resid = grad_out + grad_second
    grad_branch = grad_resid.astype(jnp.bfloat16)
    grad_out_bias = jnp.sum(grad_branch.astype(jnp.float32), 0)
    grad_out_weight = jnp.einsum(
        "tc,td->cd", mixed, grad_branch, preferred_element_type=jnp.float32
    )
    grad_mixed = jnp.einsum(
        "td,cd->tc", grad_branch, out_weight, preferred_element_type=jnp.float32
    )
    grad_mixed = grad_mixed.astype(jnp.bfloat16).reshape(count, H, HD)
    scores = masked_scores(queries, keys, length)
    probs = jnp.exp(scores - log_total)
    grad_probs = jnp.einsum("qhd,khd->hqk", grad_mixed, values, preferred_element_type=jnp.float32)
    grad_values = jnp.einsum(
        "hqk,qhd->khd", probs.astype(jnp.bfloat16), grad_mixed, preferred_element_type=jnp.float32
    )
    grad_values = grad_values.astype(jnp.bfloat16).reshape(count, width)
    row_total = jnp.sum(grad_probs * probs, -1, keepdims=True)
    grad_scores = (probs * (grad_probs - row_total)).astype(jnp.bfloat16)
    factor = HD ** (-0.5)
    grad_queries = (
        jnp.einsum("hqk,khd->qhd", grad_scores, keys, preferred_element_type=jnp.float32) * factor
    )
    grad_queries = grad_queries.astype(jnp.bfloat16).reshape(count, width)
    grad_keys = (
        jnp.einsum("hqk,qhd->khd", grad_scores, queries, preferred_element_type=jnp.float32)
        * factor
    )
    grad_keys = grad_keys.astype(jnp.bfloat16).reshape(count, width)
    grad_query_bias = jnp.sum(grad_queries.astype(jnp.float32), 0)
    grad_value_bias = jnp.sum(grad_values.astype(jnp.float32), 0)
    grad_query_weight = jnp.einsum(
        "tc,td->cd", attn_in, grad_queries, preferred_element_type=jnp.float32
    )
    grad_key_weight = jnp.einsum(
        "tc,td->cd", attn_in, grad_keys, preferred_element_type=jnp.float32
    )
    grad_value_weight = jnp.einsum(
        "tc,td->cd", attn_in, grad_values, preferred_element_type=jnp.float32
    )
    grad_attn = jnp.einsum(
        "td,cd->tc", grad_queries, query_weight, preferred_element_type=jnp.float32
    )
    grad_attn = grad_attn + jnp.einsum(
        "td,cd->tc", grad_keys, key_weight, preferred_element_type=jnp.float32
    )
    grad_attn = grad_attn + jnp.einsum(
        "td,cd->tc", grad_values, value_weight, preferred_element_type=jnp.float32
    )
    grad_first, grad_first_gain, grad_first_shift = norm_backward(
        grad_attn, first_normed, first_inverse, first_gain
    )
    grad_tokens = (grad_resid + grad_first).astype(jnp.bfloat16)
    sums = spread(
        (
            grad_first_gain,
            grad_first_shift,
            grad_query_weight,
            grad_query_bias,
            grad_key_weight,
            grad_value_weight,
            grad_value_bias,
            grad_out_weight,
            grad_out_bias,
            grad_second_gain,
            grad_second_shift,
            grad_up_weight,
            grad_up_bias,
            grad_down_weight,
            grad_down_bias,
        )
    )
    return (grad_tokens, sums)


def body(
    tokens,
    cotangent,
    seq_length,
    first_gain,
    first_shift,
    query_weight,
    query_bias,
    key_weight,
    value_weight,
    value_bias,
    out_weight,
    out_bias,
    second_gain,
    second_shift,
    up_weight,
    up_bias,
    down_weight,
    down_bias,
):
    shards = (
        first_gain,
        first_shift,
        query_weight,
        query_bias,
        key_weight,
        value_weight,
        value_bias,
        out_weight,
        out_bias,
        second_gain,
        second_shift,
        up_weight,
        up_bias,
        down_weight,
        down_bias,
    )
    if is_fast():
        result, grad_tokens, sums = fused(tokens, cotangent, seq_length, shards)
        return (result, grad_tokens, *sums)
    length = seq_length[0]
    weights = collect(shards)
    kept = forward(tokens, length, weights)
    grad_tokens, sums = backward(cotangent, length, weights, kept)
    (
        g_first_gain,
        g_first_shift,
        g_query_weight,
        g_query_bias,
        g_key_weight,
        g_value_weight,
        g_value_bias,
        g_out_weight,
        g_out_bias,
        g_second_gain,
        g_second_shift,
        g_up_weight,
        g_up_bias,
        g_down_weight,
        g_down_bias,
    ) = sums
    return (
        kept[0],
        grad_tokens,
        g_first_gain,
        g_first_shift,
        g_query_weight,
        g_query_bias,
        g_key_weight,
        g_value_weight,
        g_value_bias,
        g_out_weight,
        g_out_bias,
        g_second_gain,
        g_second_shift,
        g_up_weight,
        g_up_bias,
        g_down_weight,
        g_down_bias,
    )


def solution(mesh):
    placed = (
        P(("wide", "narrow"), None),
        P(("wide", "narrow"), None),
        P(("wide", "narrow")),
        P(("wide", "narrow")),
        P(("wide", "narrow")),
        P(("wide", "narrow"), None),
        P(("wide", "narrow")),
        P(("wide", "narrow"), None),
        P(("wide", "narrow"), None),
        P(("wide", "narrow")),
        P(("wide", "narrow"), None),
        P(("wide", "narrow")),
        P(("wide", "narrow")),
        P(("wide", "narrow")),
        P(("wide", "narrow"), None),
        P(("wide", "narrow")),
        P(("wide", "narrow"), None),
        P(("wide", "narrow")),
    )
    return jax.shard_map(
        body,
        mesh=mesh,
        in_specs=placed,
        out_specs=(
            P(("wide", "narrow"), None),
            P(("wide", "narrow"), None),
            P(("wide", "narrow")),
            P(("wide", "narrow")),
            P(("wide", "narrow"), None),
            P(("wide", "narrow")),
            P(("wide", "narrow"), None),
            P(("wide", "narrow"), None),
            P(("wide", "narrow")),
            P(("wide", "narrow"), None),
            P(("wide", "narrow")),
            P(("wide", "narrow")),
            P(("wide", "narrow")),
            P(("wide", "narrow"), None),
            P(("wide", "narrow")),
            P(("wide", "narrow"), None),
            P(("wide", "narrow")),
        ),
        check_vma=False,
    )
```

```python
import functools

import jax
import jax.numpy as jnp
from jax import lax
from jax.experimental import pallas as pl
from jax.experimental.pallas import tpu as pltpu
from jax.sharding import PartitionSpec as P

H = 8
HD = 128
AXES = ("wide", "narrow")
MESH = pl.DeviceIdType.MESH
BF = jnp.bfloat16
F32 = jnp.float32


class Place:
    def __init__(self):
        wide, narrow = lax.axis_index("wide"), lax.axis_index("narrow")
        self.z, self.x = lax.div(wide, 2), lax.rem(wide, 2)
        self.y, self.c = lax.div(narrow, 2), lax.rem(narrow, 2)
        c, x, y = self.c, self.x, self.y
        self.one = (x + (1 - c) * (1 - 2 * x), y + c * (1 - 2 * y))
        self.two = (x + c * (1 - 2 * x), y + (1 - c) * (1 - 2 * y))
        self.far = (1 - x, 1 - y)
        self.here = (x, y)

    def device(self, z, xy, c):
        return (z * 2 + xy[0], xy[1] * 2 + c)

    def up(self, step):
        return lax.rem(self.z + step, 4)

    def down(self, step):
        return lax.rem(self.z + 4 - step, 4)

    def partners(self):
        z, c = self.z, self.c
        return [self.device(self.up(step), self.here, c) for step in (1, 2, 3)] + [
            self.device(z, self.one, c),
            self.device(z, self.two, c),
            self.device(z, self.here, 1 - c),
        ]

    def greet(self):
        barrier = pltpu.get_barrier_semaphore()
        partners = self.partners()
        for partner in partners:
            pl.semaphore_signal(barrier, inc=1, device_id=partner, device_id_type=MESH)
        pl.semaphore_wait(barrier, len(partners))


def remote(source, target, send, recv, device):
    return pltpu.make_async_remote_copy(
        src_ref=source,
        dst_ref=target,
        send_sem=send,
        recv_sem=recv,
        device_id=device,
        device_id_type=MESH,
    )


class Gathering:
    SEMS = 10
    STAGES = 5

    def __init__(self, place, local, full, send, recv, keep):
        self.place, self.local, self.full = place, local, full
        self.send, self.recv, self.keep = send, recv, keep

    def block(self, xy, c):
        return self.full.at[:, xy[0], xy[1], c]

    def cell(self, z):
        place = self.place
        return self.full.at[z, place.x, place.y, place.c]

    def copy(self, source, target, sem, device):
        return remote(source, target, self.send.at[sem], self.recv.at[sem], device)

    def along(self, step):
        place = self.place
        device = place.device(place.up(step), place.here, place.c)
        return self.copy(self.local, self.cell(place.z), step - 1, device)

    def pieces(self):
        place = self.place
        z, c = place.z, place.c
        one, two = place.device(z, place.one, c), place.device(z, place.two, c)
        twin = place.device(z, place.here, 1 - c)
        mine, first = self.block(place.here, c), self.block(place.one, c)
        second, far = self.block(place.two, c), self.block(place.far, c)
        return {
            3: (mine, one, self.block(place.one, c)),
            4: (mine, two, self.block(place.two, c)),
            5: (mine, twin, self.block(place.here, 1 - c)),
            6: (first, two, self.block(place.far, c)),
            7: (first, twin, self.block(place.two, 1 - c)),
            8: (second, twin, self.block(place.one, 1 - c)),
            9: (far, twin, self.block(place.far, 1 - c)),
        }

    def start(self, sem):
        source, device, _ = self.pieces()[sem]
        self.copy(source, source, sem, device).start()

    def await_recv(self, sem):
        _, device, landing = self.pieces()[sem]
        self.copy(landing, landing, sem, device).wait_recv()

    def own(self):
        return pltpu.make_async_copy(self.local, self.cell(self.place.z), self.keep)

    def stage(self, number):
        place = self.place
        if number == 0:
            self.own().start()
            for step in (1, 2, 3):
                self.along(step).start()
        elif number == 1:
            self.own().wait()
            for step in (1, 2, 3):
                cell = self.cell(place.down(step))
                device = place.device(place.down(step), place.here, place.c)
                self.copy(cell, cell, step - 1, device).wait_recv()
            for sem in (3, 4, 5):
                self.start(sem)
        elif number == 2:
            self.await_recv(3)
            self.start(6)
            self.start(7)
            self.await_recv(4)
            self.start(8)
        elif number == 3:
            self.await_recv(6)
            self.start(9)
        elif number == 4:
            for sem in (5, 7, 8, 9):
                self.await_recv(sem)

    def finish(self):
        for step in (1, 2, 3):
            self.along(step).wait_send()
        for sem in range(3, 10):
            source, device, _ = self.pieces()[sem]
            self.copy(source, source, sem, device).wait_send()


class GatheringSides(Gathering):
    def cell_at(self, xy):
        return self.full.at[self.place.z, xy[0], xy[1], self.place.c]

    def layer(self, z, c):
        return self.full.at[z, :, :, c]

    def moves(self):
        place = self.place
        z, c = place.z, place.c
        one, two = place.device(z, place.one, c), place.device(z, place.two, c)
        twin = place.device(z, place.here, 1 - c)
        here, first, mine = self.cell_at(place.here), self.cell_at(place.one), self.layer(z, c)
        table = {
            0: (self.local, here, one, first),
            1: (self.local, here, two, self.cell_at(place.two)),
            2: (first, first, two, self.cell_at(place.far)),
            6: (mine, mine, twin, self.layer(z, 1 - c)),
        }
        for step in (1, 2, 3):
            other = place.down(step)
            block = self.layer(other, c)
            table[2 + step] = (mine, mine, place.device(place.up(step), place.here, c), block)
            table[6 + step] = (block, block, twin, self.layer(other, 1 - c))
        return table

    def start(self, sem):
        source, target, device, _ = self.moves()[sem]
        self.copy(source, target, sem, device).start()

    def await_recv(self, sem):
        _, _, device, landing = self.moves()[sem]
        self.copy(landing, landing, sem, device).wait_recv()

    def stage(self, number):
        if number == 0:
            self.own().start()
            self.start(0)
            self.start(1)
        elif number == 1:
            self.await_recv(0)
            self.start(2)
            self.await_recv(1)
            self.own().wait()
        elif number == 2:
            self.await_recv(2)
            for sem in (3, 4, 5, 6):
                self.start(sem)
        elif number == 3:
            for step in (1, 2, 3):
                self.await_recv(2 + step)
                self.start(6 + step)
        elif number == 4:
            for sem in (6, 7, 8, 9):
                self.await_recv(sem)

    def finish(self):
        for sem in range(10):
            source, target, device, _ = self.moves()[sem]
            self.copy(source, target, sem, device).wait_send()


class Scattering:
    SEMS = 7
    STAGES = 5

    def __init__(self, place, partial, mine, total, pair, line, out, send, recv, load):
        self.place, self.partial, self.mine = place, partial, mine
        self.total, self.pair, self.line, self.out = total, pair, line, out
        self.send, self.recv, self.load = send, recv, load

    def pieces(self):
        place = self.place
        z, c = place.z, place.c
        one, two = place.device(z, place.one, c), place.device(z, place.two, c)
        twin = place.device(z, place.here, 1 - c)
        total = self.total

        def block(xy):
            return total.at[:, xy[0], xy[1]]

        table = {
            0: (self.partial.at[:, :, :, 1 - c], total, twin),
            1: (block(place.two), self.pair.at[0], two),
            2: (block(place.far), self.pair.at[1], two),
            3: (block(place.one), self.pair.at[2], one),
        }
        for step in (1, 2, 3):
            device = place.device(place.up(step), place.here, c)
            table[3 + step] = (
                total.at[place.up(step), place.x, place.y],
                self.line.at[step - 1],
                device,
            )
        return table

    def copy(self, sem):
        source, target, device = self.pieces()[sem]
        return remote(source, target, self.send.at[sem], self.recv.at[sem], device)

    def own(self):
        return pltpu.make_async_copy(
            self.partial.at[:, :, :, self.place.c], self.mine, self.load
        )

    def join(self):
        total, mine = self.total, self.mine
        self.own().wait()
        self.copy(0).wait_recv()

        def body(z, carry):
            for x in range(2):
                for y in range(2):
                    value = total[z, x, y].astype(F32) + mine[z, x, y].astype(F32)
                    total[z, x, y] = value.astype(BF)
            return carry

        lax.fori_loop(0, 4, body, 0)

    def stage(self, number):
        place, total, pair = self.place, self.total, self.pair

        def add(xy, slot):
            def body(z, carry):
                value = total[z, xy[0], xy[1]].astype(F32) + pair[slot, z].astype(F32)
                total[z, xy[0], xy[1]] = value.astype(BF)
                return carry

            lax.fori_loop(0, 4, body, 0)

        if number == 0:
            self.own().start()
            self.copy(0).start()
        elif number == 1:
            self.join()
            self.copy(2).start()
            self.copy(1).start()
        elif number == 2:
            self.copy(2).wait_recv()
            add(place.one, 1)
            self.copy(3).start()
            self.copy(1).wait_recv()
            add(place.here, 0)
        elif number == 3:
            self.copy(3).wait_recv()
            add(place.here, 2)
            for step in (1, 2, 3):
                self.copy(3 + step).start()
        elif number == 4:
            value = total[place.z, place.x, place.y].astype(F32)
            for step in (1, 2, 3):
                self.copy(3 + step).wait_recv()
                value = value + self.line[step - 1].astype(F32)
            self.out[...] = value

    def finish(self):
        for sem in range(7):
            self.copy(sem).wait_send()


class ScatteringSides(Scattering):
    def pieces(self):
        place, total = self.place, self.total
        z, c = place.z, place.c
        one, two = place.device(z, place.one, c), place.device(z, place.two, c)
        twin = place.device(z, place.here, 1 - c)

        def cell(xy):
            return total.at[z, xy[0], xy[1]]

        table = {
            0: (self.partial.at[:, :, :, 1 - c], total, twin),
            1: (cell(place.two), self.line.at[0], two),
            2: (cell(place.far), self.line.at[1], two),
            3: (cell(place.one), self.line.at[2], one),
        }
        for step in (1, 2, 3):
            device = place.device(place.up(step), place.here, c)
            table[3 + step] = (total.at[place.up(step)], self.pair.at[step - 1], device)
        return table

    def stage(self, number):
        place, total, pair, line = self.place, self.total, self.pair, self.line
        z = place.z

        def add(xy, slot):
            value = total[z, xy[0], xy[1]].astype(F32) + line[slot].astype(F32)
            total[z, xy[0], xy[1]] = value.astype(BF)

        if number == 0:
            self.own().start()
            self.copy(0).start()
        elif number == 1:
            self.join()
            for step in (1, 2, 3):
                self.copy(3 + step).start()
        elif number == 2:
            for step in (1, 2, 3):
                self.copy(3 + step).wait_recv()

            def body(x, carry):
                for y in range(2):
                    value = total[z, x, y].astype(F32)
                    for step in range(3):
                        value = value + pair[step, x, y].astype(F32)
                    total[z, x, y] = value.astype(BF)
                return carry

            lax.fori_loop(0, 2, body, 0)
            self.copy(2).start()
            self.copy(1).start()
        elif number == 3:
            self.copy(2).wait_recv()
            add(place.one, 1)
            self.copy(3).start()
            self.copy(1).wait_recv()
            add(place.here, 0)
        elif number == 4:
            self.copy(3).wait_recv()
            value = total[z, place.x, place.y].astype(F32) + line[2].astype(F32)
            self.out[...] = value


class Summing:
    SEMS = 6

    def __init__(self, place, value, total, slots, send, recv):
        self.place, self.value, self.total, self.slots = place, value, total, slots
        self.send, self.recv = send, recv

    def copy(self, sem):
        place = self.place
        device = [
            place.device(place.z, place.here, 1 - place.c),
            place.device(place.z, place.one, place.c),
            place.device(place.z, place.two, place.c),
        ] + [place.device(place.up(step), place.here, place.c) for step in (1, 2, 3)]
        source = self.total.at[min(sem, 3)]
        return remote(source, self.slots.at[sem], self.send.at[sem], self.recv.at[sem], device[sem])

    def stage(self, number):
        total, slots = self.total, self.slots
        if number == 0:
            total[0] = self.value[...]
            self.copy(0).start()
        elif number < 3:
            self.copy(number - 1).wait_recv()
            total[number] = total[number - 1] + slots[number - 1]
            self.copy(number).start()
        elif number == 3:
            self.copy(2).wait_recv()
            total[3] = total[2] + slots[2]
            for sem in (3, 4, 5):
                self.copy(sem).start()
        elif number == 4:
            value = total[3]
            for sem in (3, 4, 5):
                self.copy(sem).wait_recv()
                value = value + slots[sem]
            total[4] = value

    def finish(self):
        for sem in range(6):
            self.copy(sem).wait_send()


def run_tick(tasks, ticks, number, done=None):
    for stage in reversed(range(5)):
        for g, task in enumerate(tasks):
            if ticks[g][stage] == number:
                task.stage(stage)
                if stage == 4 and done is not None:
                    done(g)


def halves(ref, count, width):
    if count == 1:
        return [ref]
    lead = (slice(None),) * (len(ref.shape) - 1)
    return [ref.at[lead + (pl.ds(i * width, width),)] for i in range(count)]


SMALL = (0, 1, 3, 6, 8, 9, 10, 14, 12)
LARGE = (2, 4, 5, 7, 11, 13)


EPSILON = 1e-05


def collect(parts):
    (
        first_gain,
        first_shift,
        query_weight,
        query_bias,
        key_weight,
        value_weight,
        value_bias,
        out_weight,
        out_bias,
        second_gain,
        second_shift,
        up_weight,
        up_bias,
        down_weight,
        down_bias,
    ) = parts
    return (
        lax.all_gather(first_gain, ("wide", "narrow"), axis=0, tiled=True),
        lax.all_gather(first_shift, ("wide", "narrow"), axis=0, tiled=True),
        lax.all_gather(query_weight, ("wide", "narrow"), axis=0, tiled=True),
        lax.all_gather(query_bias, ("wide", "narrow"), axis=0, tiled=True),
        lax.all_gather(key_weight, ("wide", "narrow"), axis=0, tiled=True),
        lax.all_gather(value_weight, ("wide", "narrow"), axis=0, tiled=True),
        lax.all_gather(value_bias, ("wide", "narrow"), axis=0, tiled=True),
        lax.all_gather(out_weight, ("wide", "narrow"), axis=0, tiled=True),
        lax.all_gather(out_bias, ("wide", "narrow"), axis=0, tiled=True),
        lax.all_gather(second_gain, ("wide", "narrow"), axis=0, tiled=True),
        lax.all_gather(second_shift, ("wide", "narrow"), axis=0, tiled=True),
        lax.all_gather(up_weight, ("wide", "narrow"), axis=0, tiled=True),
        lax.all_gather(up_bias, ("wide", "narrow"), axis=0, tiled=True),
        lax.all_gather(down_weight, ("wide", "narrow"), axis=0, tiled=True),
        lax.all_gather(down_bias, ("wide", "narrow"), axis=0, tiled=True),
    )


def spread(parts):
    (
        first_gain,
        first_shift,
        query_weight,
        query_bias,
        key_weight,
        value_weight,
        value_bias,
        out_weight,
        out_bias,
        second_gain,
        second_shift,
        up_weight,
        up_bias,
        down_weight,
        down_bias,
    ) = parts
    return (
        lax.psum_scatter(first_gain, ("wide", "narrow"), scatter_dimension=0, tiled=True),
        lax.psum_scatter(first_shift, ("wide", "narrow"), scatter_dimension=0, tiled=True),
        lax.psum_scatter(query_weight, ("wide", "narrow"), scatter_dimension=0, tiled=True),
        lax.psum_scatter(query_bias, ("wide", "narrow"), scatter_dimension=0, tiled=True),
        lax.psum_scatter(key_weight, ("wide", "narrow"), scatter_dimension=0, tiled=True),
        lax.psum_scatter(value_weight, ("wide", "narrow"), scatter_dimension=0, tiled=True),
        lax.psum_scatter(value_bias, ("wide", "narrow"), scatter_dimension=0, tiled=True),
        lax.psum_scatter(out_weight, ("wide", "narrow"), scatter_dimension=0, tiled=True),
        lax.psum_scatter(out_bias, ("wide", "narrow"), scatter_dimension=0, tiled=True),
        lax.psum_scatter(second_gain, ("wide", "narrow"), scatter_dimension=0, tiled=True),
        lax.psum_scatter(second_shift, ("wide", "narrow"), scatter_dimension=0, tiled=True),
        lax.psum_scatter(up_weight, ("wide", "narrow"), scatter_dimension=0, tiled=True),
        lax.psum_scatter(up_bias, ("wide", "narrow"), scatter_dimension=0, tiled=True),
        lax.psum_scatter(down_weight, ("wide", "narrow"), scatter_dimension=0, tiled=True),
        lax.psum_scatter(down_bias, ("wide", "narrow"), scatter_dimension=0, tiled=True),
    )


LOG2E = 1.4426950408889634
WEIGHTS = ("query", "key", "value", "out", "up", "down")


def dot(left, right, form):
    dims = (((0,) if form[0] == "T" else (1,), (1,) if form[1] == "T" else (0,)), ((), ()))
    return lax.dot_general(left, right, dims, preferred_element_type=F32)


def at(index, size):
    return pl.ds(pl.multiple_of(index * size, size), size)


def loop(count, body):
    def step(i, carry):
        body(i)
        return carry

    lax.fori_loop(0, count, step, 0)


def normed_rows(value):
    center = value - jnp.mean(value, -1, keepdims=True)
    inverse = lax.rsqrt(jnp.mean(center * center, -1, keepdims=True) + EPSILON)
    return center * inverse, inverse


def gelu_pair(hidden):
    cdf = 0.5 * (1.0 + lax.erf(hidden * 0.7071067811865476))
    density = jnp.exp2(hidden * hidden * (-0.5 * LOG2E)) * 0.3989422804014327
    return hidden * cdf, cdf + hidden * density


def pack_small(vectors, packed):
    packed[...] = jnp.zeros_like(packed)
    for row, vector in enumerate(vectors):
        size = vector.shape[0]
        packed[row : row + 1, :size] = vector[...].astype(F32).reshape(1, size)


def unpack_small(small, vec):
    table = small.reshape(512, 128)
    lane = lax.broadcasted_iota(jnp.int32, (128, 1024), 0)
    column = lax.broadcasted_iota(jnp.int32, (128, 1024), 1)
    pick = jnp.where(lane == lax.rem(column, 32), 1.0, 0.0).astype(BF)
    device = lax.broadcasted_iota(jnp.int32, (32, 16, 1024), 0)
    owner = lax.div(lax.broadcasted_iota(jnp.int32, (32, 16, 1024), 2), 32)
    spread_out = dot(table[...].astype(BF), pick, "NN").reshape(32, 16, 1024)
    vec[...] = jnp.sum(jnp.where(device == owner, spread_out, 0.0), 0)
    for part in range(4):
        for block in range(8):
            source = (part * 8 + block) * 16 + 8
            vec[8 + part : 9 + part, block * 128 : block * 128 + 128] = table[source : source + 1, :]


def prepare_bias(length, mask, ramp):
    key = lax.broadcasted_iota(jnp.int32, (256, 256), 0)
    query = lax.broadcasted_iota(jnp.int32, (256, 256), 1)
    long = length == 1024
    same = (lax.div(key, 128) == lax.div(query, 128)) | long
    mask[...] = jnp.where((key <= query) & same, 0.0, -1e30)
    ramp[...] = lax.broadcasted_iota(jnp.int32, (1024, 128), 0).astype(F32)
    return jnp.where(long, 0.0, -1e30)


def wide(value):
    return jnp.concatenate([value, value], axis=1)


def attention_head(head, slope, off, queries, keys, values, mixed, lse, mask, ramp, tilt):
    cols = at(head, 128)
    factor = HD**-0.5 * LOG2E
    tilt[...] = ramp[...] * slope
    for i in range(4):
        rows, before = slice(i * 256, i * 256 + 256), slice(0, i * 256)
        query = queries[rows, cols]
        near = dot(keys[rows, cols], query, "NT") * factor + wide(tilt[rows, :]) + mask[...]
        top = jnp.max(near, 0, keepdims=True)
        if i:
            past = dot(keys[before, cols], query, "NT") * factor + wide(tilt[before, :])
            top = jnp.maximum(top, jnp.max(past, 0, keepdims=True) + off)
        near = jnp.exp2(near - top)
        total = jnp.sum(near, 0, keepdims=True)
        out = dot(values[rows, cols], near.astype(BF), "TN")
        if i:
            past = jnp.exp2(past + (off - top))
            total = total + jnp.sum(past, 0, keepdims=True)
            out = out + dot(values[before, cols], past.astype(BF), "TN")
        mixed[rows, cols] = (out * (1.0 / total)).T.astype(BF)
        lse[pl.ds(head, 1), rows] = top + jnp.log2(total)


def forward_kernel(length_ref, tokens_in, cotangent_in, *refs):
    refs = list(refs)

    def take(count):
        taken, refs[:count] = refs[:count], []
        return taken

    vectors = take(9)
    local = take(6)
    result_out, resid_out, lse_out, small_out, down_out = take(5)
    attn_out, query_out, key_out, value_out, mixed_out, ffn_out, slope_out = take(7)
    weight_out = take(6)
    full = take(7)
    act, slope, mixed, ffn_in = take(4)
    resid, vec, lse, mask, ramp, tilt, stage = take(7)
    tokens, cotangent, packed = take(3)
    send, recv, keep, store, dump, stage_sem, input_sem = take(7)
    local = [packed] + local
    fetches = [
        pltpu.make_async_copy(source, target, input_sem.at[i])
        for i, (source, target) in enumerate(((tokens_in, tokens), (cotangent_in, cotangent)))
    ]
    for fetch in fetches:
        fetch.start()
    pack_small(vectors, packed)

    place = Place()
    place.greet()
    tasks, dumps = [], []
    for i, cut in enumerate((1, 1, 1, 1, 1, 4, 4)):
        width = local[i].shape[-1] // cut
        for j in range(cut):
            g = len(tasks)
            views = [halves(ref, cut, width)[j] for ref in (local[i], full[i])]
            kind = GatheringSides if g == 12 else Gathering
            tasks.append(kind(place, *views, send.at[g], recv.at[g], keep.at[g]))
            if i:
                target = halves(weight_out[i - 1], cut, width)[j]
                dumps.append(pltpu.make_async_copy(views[1], target, dump.at[g - 1]))

    ticks = [[0, 1, 2, 3, 4]] + [[g - 1 + stage for stage in range(5)] for g in range(1, 5)]
    ticks += [[g - 3, g - 1, g + 1, g + 2, g + 3] for g in range(5, 12)]
    ticks += [[0, 1, 5, 11, 12]]

    def done(g):
        if g:
            dumps[g - 1].start()

    def tick(number):
        run_tick(tasks, ticks, number, done)

    saves = []

    def save(source, target):
        copy = pltpu.make_async_copy(source, target, store.at[len(saves)])
        copy.start()
        saves.append(copy)

    query_w, key_w, value_w, out_w = (ref.reshape(1024, 1024) for ref in full[1:5])
    up_w, down_w = full[5].reshape(1024, 4096), full[6].reshape(4096, 1024)
    attn_in, queries, keys, values = (act.at[i] for i in range(4))
    length = length_ref[0]
    off = prepare_bias(length, mask, ramp)

    tick(0)
    tick(1)
    fetches[0].wait()

    def first_stats(i):
        rows = at(i, 128)
        normed, _ = normed_rows(tokens[rows, :].astype(F32))
        resid[rows, :] = normed

    loop(8, first_stats)
    for number in range(2, 5):
        tick(number)
    unpack_small(full[0], vec)

    def first_norm(i):
        rows = at(i, 128)
        attn_in[rows, :] = (resid[rows, :] * vec[0:1, :] + vec[1:2, :]).astype(BF)

    loop(8, first_norm)
    save(attn_in, attn_out)

    def project(weight, target, bias):
        def body(i):
            cols = at(i, 512)
            value = dot(attn_in[...], weight[:, cols], "NN")
            if bias is not None:
                value = value + vec[bias : bias + 1, cols]
            target[:, cols] = value.astype(BF)

        loop(2, body)

    project(query_w, queries, 2)
    save(queries, query_out)
    tick(5)
    project(key_w, keys, None)
    save(keys, key_out)
    tick(6)
    project(value_w, values, 3)
    save(values, value_out)

    def heads(first):
        def body(i, slope_now):
            attention_head(
                first + i, slope_now, off, queries, keys, values, mixed, lse, mask, ramp, tilt
            )
            return slope_now * 0.5

        lax.fori_loop(0, 2, body, jnp.float32(LOG2E * 0.5 ** (first + 1)))

    heads(0)
    tick(7)
    heads(2)
    heads(4)
    tick(8)
    heads(6)
    save(mixed, mixed_out)
    save(lse, lse_out)

    def close_attention(i):
        rows = at(i, 256)
        value = dot(mixed[rows, :], out_w[...], "NN") + tokens[rows, :].astype(F32) + vec[4:5, :]
        resid[rows, :] = value
        normed, _ = normed_rows(value)
        ffn_in[rows, :] = (normed * vec[5:6, :] + vec[6:7, :]).astype(BF)

    loop(4, close_attention)
    save(resid, resid_out)
    save(ffn_in, ffn_out)
    for copy in saves[:5]:
        copy.wait()

    def widen(chunk):
        def body(i):
            rows, cols = at(lax.div(i, 2), 512), at(lax.rem(i, 2), 512)
            weight = up_w[:, at(chunk * 2 + lax.rem(i, 2), 512)]
            hidden = dot(ffn_in[rows, :], weight, "NN") + vec[8 + chunk : 9 + chunk, cols]
            active, steep = gelu_pair(hidden)
            act[chunk, rows, cols] = active.astype(BF)
            slope[chunk % 2, rows, cols] = steep.astype(BF)

        if chunk > 1:
            saves[8 + chunk - 2].wait()
        loop(4, body)
        save(slope.at[chunk % 2], slope_out.at[chunk])


    def spill(j, half):
        rows = pl.ds(pl.multiple_of(j * 1024 + half * 512, 512), 512)
        return pltpu.make_async_copy(stage.at[half], down_out.at[rows, :], stage_sem.at[half])

    def grad_down(j):
        for half in range(2):

            if j:
                spill(j - 1, half).wait()
            active = act[j, :, half * 512 : half * 512 + 512]
            stage[half] = dot(active, cotangent[...], "TN").astype(BF)
            spill(j, half).start()

    tick(9)
    widen(0)
    widen(1)
    fetches[1].wait()
    tick(10)
    widen(2)
    grad_down(0)
    tick(11)
    widen(3)
    grad_down(1)

    def narrow(chunk):
        cols = slice(chunk * 256, chunk * 256 + 256)

        def body(i):
            rows = at(i, 512)
            value = resid[rows, cols] + vec[7:8, cols]
            active = jnp.concatenate([act[j, rows, :] for j in range(4)], axis=1)
            value = value + dot(active, down_w[:, cols], "NN")
            mixed[rows, cols] = value.astype(BF)

        loop(2, body)

        save(mixed.at[:, cols], result_out.at[:, cols])

    tick(12)
    narrow(0)
    narrow(3)
    grad_down(2)
    tick(13)
    narrow(1)
    grad_down(3)
    tick(14)
    narrow(2)
    small_out[...] = vec[...]
    for half in range(2):
        spill(3, half).wait()
    for task in tasks:
        task.finish()
    for copy in saves[5:8] + saves[10:]:
        copy.wait()
    for copy in dumps:
        copy.wait()


def forward_all(length, tokens, cotangent, vectors, weights):
    square = jax.ShapeDtypeStruct((1024, 1024), BF)
    tall = jax.ShapeDtypeStruct((4, 1024, 1024), BF)
    f32 = functools.partial(jax.ShapeDtypeStruct, dtype=F32)
    grid6 = [(4, 2, 2, 2) + w.shape for w in weights]
    hbm, vmem = pl.BlockSpec(memory_space=pltpu.HBM), pl.BlockSpec(memory_space=pltpu.VMEM)
    return pl.pallas_call(
        forward_kernel,
        out_shape=[square, f32((1024, 1024)), f32((8, 1024)), f32((16, 1024))]
        + [jax.ShapeDtypeStruct((4096, 1024), BF)]
        + [square] * 6
        + [tall]
        + [jax.ShapeDtypeStruct(s, BF) for s in grid6],
        in_specs=[pl.BlockSpec(memory_space=pltpu.SMEM)] + [hbm] * 2 + [vmem] * 9 + [hbm] * 6,
        out_specs=[hbm, hbm, hbm, vmem] + [hbm] * 14,
        scratch_shapes=[pltpu.VMEM((4, 2, 2, 2, 16, 128), F32)]
        + [pltpu.VMEM(s, BF) for s in grid6]
        + [pltpu.VMEM((4, 1024, 1024), BF), pltpu.VMEM((2, 1024, 1024), BF)]
        + [pltpu.VMEM((1024, 1024), BF)] * 2
        + [
            pltpu.VMEM((1024, 1024), F32),
            pltpu.VMEM((16, 1024), F32),
            pltpu.VMEM((8, 1024), F32),
            pltpu.VMEM((256, 256), F32),
            pltpu.VMEM((1024, 128), F32),
            pltpu.VMEM((1024, 128), F32),
            pltpu.VMEM((2, 512, 1024), BF),
            pltpu.VMEM((1024, 1024), BF),
            pltpu.VMEM((1024, 1024), BF),
            pltpu.VMEM((16, 128), F32),
            pltpu.SemaphoreType.DMA((13, Gathering.SEMS)),
            pltpu.SemaphoreType.DMA((13, Gathering.SEMS)),
            pltpu.SemaphoreType.DMA((13,)),
            pltpu.SemaphoreType.DMA((20,)),
            pltpu.SemaphoreType.DMA((12,)),
            pltpu.SemaphoreType.DMA((2,)),
            pltpu.SemaphoreType.DMA((2,)),
        ],
        compiler_params=pltpu.CompilerParams(
            collective_id=2, has_side_effects=True, vmem_limit_bytes=62 << 20
        ),
    )(length, tokens, cotangent, *vectors, *weights)


SHARDS = ("down", "up", "out", "query", "key", "value")
SCATTER_CUTS = (4, 4, 1, 1, 1, 2)


def attention_head_back(head, slope, off, refs, lse, mask, ramp, tilt, key_sum, value_sum):
    queries, keys, values, mixed, grad_mixed = refs
    cols = at(head, 128)
    factor = HD**-0.5 * LOG2E
    tilt[...] = ramp[...] * slope
    for i in (3, 2, 1, 0):
        rows, upto, before = slice(i * 256, i * 256 + 256), slice(0, i * 256 + 256), i * 256
        query, grad = queries[rows, cols], grad_mixed[rows, cols]
        product = grad.astype(F32) * mixed[rows, cols].astype(F32)
        inner = jnp.sum(product.T, 0, keepdims=True)
        level = lse[pl.ds(head, 1), rows]
        raw = dot(keys[upto, cols], query, "NT") * factor + wide(tilt[upto, :])
        probs = jnp.exp2(raw[before:] + mask[...] - level)
        if i:
            probs = jnp.concatenate([jnp.exp2(raw[:before] + (off - level)), probs], axis=0)
        grad_probs = dot(values[upto, cols], grad, "NT")
        grad_scores = (probs * (grad_probs - inner)).astype(BF)
        value_part = dot(probs.astype(BF), grad, "NN")
        key_part = dot(grad_scores, query, "NN")
        if i == 3:
            value_sum[...] = value_part
            key_sum[...] = key_part
        else:
            value_sum[upto, :] += value_part
            key_sum[upto, :] += key_part
        query_part = dot(keys[upto, cols], grad_scores, "TN") * HD**-0.5
        queries[rows, cols] = query_part.T.astype(BF)
    keys[:, cols] = (key_sum[...] * HD**-0.5).astype(BF)
    values[:, cols] = value_sum[...].astype(BF)


def backward_kernel(length_ref, vec, lse, *refs):
    refs = list(refs)

    def take(count):
        taken, refs[:count] = refs[:count], []
        return taken

    tokens, cotangent, attn_in, queries, keys, values, mixed, ffn_in, slope, resid = take(10)
    query_w, key_w, value_w, out_w, up_w, down_w, down_part = take(7)
    grad_tokens_out, small_out = take(2)
    out = take(6)
    parts = [down_part] + take(5)
    total, pair, line = take(6), take(6), take(6)
    mine_down, mine, sides_pair, sides_line, arena, grad, stage, strip = take(8)
    key_sum, value_sum, mask, ramp, tilt, sums = take(6)
    small_total, small_slots, small_send, small_recv = take(4)
    send, recv, load_sem, slot_sem, stage_sem, strip_sem = take(6)

    place = Place()
    loads = {}

    def load(source, slot):
        copy = pltpu.make_async_copy(source, arena.at[slot], slot_sem.at[slot])
        copy.start()
        loads[slot] = copy

    def ready(slot):
        loads.pop(slot).wait()
        return arena.at[slot]

    def load_chunk(j):
        load(slope.at[j], j % 2)
        load(down_w.at[pl.ds(j * 1024, 1024), :], 2 + j % 2)
        load(up_w.at[:, pl.ds(j * 1024, 1024)], 4 + j % 2)

    load(cotangent, 6)
    load_chunk(0)
    load(ffn_in, 7)
    place.greet()

    tasks = []
    for i, cut in enumerate(SCATTER_CUTS):
        width = parts[i].shape[-1] // cut
        for j in range(cut):
            g = len(tasks)
            own = mine_down if i == 0 else mine.at[:, :, :, :, pl.ds(0, width)]
            views = [halves(r, cut, width)[j] for r in (parts[i], total[i], pair[i], line[i], out[i])]
            kind = ScatteringSides if g == 0 else Scattering
            if g == 0:
                views[2:4] = sides_pair, sides_line
            tasks.append(
                kind(place, views[0], own, *views[1:], send.at[g], recv.at[g], load_sem.at[g])
            )
    tasks.append(Summing(place, sums, small_total, small_slots, small_send, small_recv))

    ticks = [[0, 1, 8, 10, 12]] + [[g, g + 1, g + 3, g + 5, g + 7] for g in range(1, 10)]
    ticks += [[10, 11, 13, 14, 15], [11, 12, 14, 15, 16], [12, 13, 15, 16, 17]]
    ticks += [[13, 14, 15, 16, 17]]

    def tick(number):
        run_tick(tasks, ticks, number)

    stages = {}

    def emit(part, left, right, width=1024, first=0):
        copies = []
        for half in range(2):
            if half in stages:
                stages.pop(half).wait()
            value = dot(left[:, half * 512 : half * 512 + 512], right[...], "TN")
            stage[half] = value.astype(BF).reshape(2, 2, 2, 2, 32, 1024)
            target = part.at[half * 2 : half * 2 + 2, :, :, :, :, pl.ds(first, width)]
            copy = pltpu.make_async_copy(stage.at[half], target, stage_sem.at[half])
            copy.start()
            stages[half] = copy
            copies.append(copy)

    def settle():
        for half in list(stages):
            stages.pop(half).wait()

    ones = jnp.ones((8, 1024), BF)

    def column_sums(source, row):
        def body(i):
            cols = at(i, 256)
            sums[row : row + 1, cols] = dot(ones, source[:, cols], "NN")[0:1]

        loop(4, body)

    length = length_ref[0]
    off = prepare_bias(length, mask, ramp)
    sums[...] = jnp.zeros_like(sums)
    for number in range(3):
        tick(number)
    cot = ready(6)
    up_part = parts[1]

    for j in range(4):
        if j < 3:
            load_chunk(j + 1)
        hidden_slope, down_chunk, up_chunk = ready(j % 2), ready(2 + j % 2), ready(4 + j % 2)
        if j == 0:
            ffn = ready(7)

        def grad_hidden(i):
            cols = at(i, 512)
            value = dot(cot[...], down_chunk[cols, :], "NT") * hidden_slope[:, cols].astype(F32)
            hidden_slope[:, cols] = value.astype(BF)

        loop(2, grad_hidden)
        column_sums(hidden_slope, 8 + j)
        emit(up_part, ffn, hidden_slope, 1024, j * 1024)

        def grad_ffn(i):
            rows = at(i, 512)
            value = dot(hidden_slope[rows, :], up_chunk[...], "NT")
            if j:
                value = value + grad[rows, :]
            grad[rows, :] = value

        loop(2, grad_ffn)
        if j == 3:
            settle()
        tick(j + 3)

    def load_strip(i):
        return pltpu.make_async_copy(
            resid.at[at(i, 128), :], strip.at[lax.rem(i, 2)], strip_sem.at[lax.rem(i, 2)]
        )

    load(mixed, 2)
    load(out_w, 4)
    load(queries, 3)
    load(keys, 5)
    load(values, 7)
    load_strip(0).start()
    gain = vec[5:6, :]
    branch = arena.at[0]

    def second_norm_back(i):
        @pl.when(i < 7)
        def _():
            load_strip(i + 1).start()

        load_strip(i).wait()
        rows = at(i, 128)
        normed, inverse = normed_rows(strip[lax.rem(i, 2)])
        incoming = grad[rows, :]
        sums[5:6, :] += jnp.sum(incoming * normed, 0, keepdims=True)
        sums[6:7, :] += jnp.sum(incoming, 0, keepdims=True)
        scaled = incoming * gain
        inner = (
            scaled
            - jnp.mean(scaled, -1, keepdims=True)
            - normed * jnp.mean(scaled * normed, -1, keepdims=True)
        )
        value = cot[rows, :].astype(F32) + inverse * inner
        grad[rows, :] = value
        branch[rows, :] = value.astype(BF)

    loop(8, second_norm_back)
    column_sums(cot, 7)
    column_sums(branch, 4)
    load(query_w, 6)
    mix, out_full = ready(2), ready(4)
    grad_mixed = arena.at[1]

    def back_out(i):
        cols = at(i, 512)
        grad_mixed[:, cols] = dot(branch[...], out_full[cols, :], "NT").astype(BF)

    loop(2, back_out)
    emit(parts[2], mix, branch)
    load(key_w, 4)
    query, key, value = ready(3), ready(5), ready(7)
    tick(7)
    settle()
    load(attn_in, 0)

    def heads(first, count):
        def body(i, slope_now):
            attention_head_back(
                first + i,
                slope_now,
                off,
                (query, key, value, mix, grad_mixed),
                lse,
                mask,
                ramp,
                tilt,
                key_sum,
                value_sum,
            )
            return slope_now * 0.5

        lax.fori_loop(0, count, body, jnp.float32(LOG2E * 0.5 ** (first + 1)))

    heads(0, 4)
    tick(8)
    heads(4, 4)
    load(value_w, 2)
    attn = ready(0)
    emit(parts[3], attn, query)
    settle()
    tick(9)
    emit(parts[4], attn, key)
    settle()
    tick(10)
    emit(parts[5], attn, value)
    settle()
    tick(11)
    load(tokens, 1)
    column_sums(query, 2)
    column_sums(value, 3)
    query_full, key_full, value_full = ready(6), ready(4), ready(2)
    first_gain = vec[0:1, :]
    token_rows = ready(1)

    def first_norm_back(i):
        rows = at(i, 256)
        incoming = dot(query[rows, :], query_full[...], "NT")
        incoming = incoming + dot(key[rows, :], key_full[...], "NT")
        incoming = incoming + dot(value[rows, :], value_full[...], "NT")
        normed, inverse = normed_rows(token_rows[rows, :].astype(F32))
        sums[0:1, :] += jnp.sum(incoming * normed, 0, keepdims=True)
        sums[1:2, :] += jnp.sum(incoming, 0, keepdims=True)
        scaled = incoming * first_gain
        inner = (
            scaled
            - jnp.mean(scaled, -1, keepdims=True)
            - normed * jnp.mean(scaled * normed, -1, keepdims=True)
        )
        arena[1, rows, :] = (grad[rows, :] + inverse * inner).astype(BF)

    first_norm_back(0)
    first_norm_back(1)
    tick(12)
    first_norm_back(2)
    first_norm_back(3)
    result = pltpu.make_async_copy(arena.at[1], grad_tokens_out, slot_sem.at[1])
    result.start()
    for number in range(13, 18):
        tick(number)
    small_out[...] = small_total[4]
    result.wait()
    for task in tasks:
        task.finish()


def backward_all(length, vec, lse, arrays, shards):
    hbm, vmem = pl.BlockSpec(memory_space=pltpu.HBM), pl.BlockSpec(memory_space=pltpu.VMEM)
    groups = sum(SCATTER_CUTS)
    results = pl.pallas_call(
        backward_kernel,
        out_shape=[jax.ShapeDtypeStruct((1024, 1024), BF), jax.ShapeDtypeStruct((16, 1024), F32)]
        + [jax.ShapeDtypeStruct(s, F32) for s in shards]
        + [jax.ShapeDtypeStruct((4, 2, 2, 2) + s, BF) for s in shards[1:]],
        in_specs=[pl.BlockSpec(memory_space=pltpu.SMEM), vmem, vmem] + [hbm] * len(arrays),
        out_specs=[hbm, vmem] + [vmem] * 6 + [hbm] * 5,
        scratch_shapes=[pltpu.VMEM((4, 2, 2) + s, BF) for s in shards]
        + [pltpu.VMEM((3, 4) + s, BF) for s in shards]
        + [pltpu.VMEM((3,) + s, BF) for s in shards]
        + [
            pltpu.VMEM((4, 2, 2, 128, 256), BF),
            pltpu.VMEM((4, 2, 2, 32, 1024), BF),
            pltpu.VMEM((3, 2, 2, 128, 256), BF),
            pltpu.VMEM((3, 128, 256), BF),
            pltpu.VMEM((8, 1024, 1024), BF),
            pltpu.VMEM((1024, 1024), F32),
            pltpu.VMEM((2, 2, 2, 2, 2, 32, 1024), BF),
            pltpu.VMEM((2, 128, 1024), F32),
            pltpu.VMEM((1024, 128), F32),
            pltpu.VMEM((1024, 128), F32),
            pltpu.VMEM((256, 256), F32),
            pltpu.VMEM((1024, 128), F32),
            pltpu.VMEM((1024, 128), F32),
            pltpu.VMEM((16, 1024), F32),
            pltpu.VMEM((5, 16, 1024), F32),
            pltpu.VMEM((6, 16, 1024), F32),
            pltpu.SemaphoreType.DMA((Summing.SEMS,)),
            pltpu.SemaphoreType.DMA((Summing.SEMS,)),
            pltpu.SemaphoreType.DMA((groups, Scattering.SEMS)),
            pltpu.SemaphoreType.DMA((groups, Scattering.SEMS)),
            pltpu.SemaphoreType.DMA((groups,)),
            pltpu.SemaphoreType.DMA((8,)),
            pltpu.SemaphoreType.DMA((2,)),
            pltpu.SemaphoreType.DMA((2,)),
        ],
        compiler_params=pltpu.CompilerParams(
            collective_id=3, has_side_effects=True, vmem_limit_bytes=62 << 20
        ),
    )(length, vec, lse, *arrays)
    return results[0], results[1], results[2:8]


def finish_kernel(small, *refs):
    arrays, outs, vectors = refs[:8], refs[8:16], refs[16:25]
    buffers, come, go = refs[25:33], refs[33], refs[34]
    inward = [
        pltpu.make_async_copy(source, buffer, come.at[i])
        for i, (source, buffer) in enumerate(zip(arrays, buffers))
    ]
    outward = [
        pltpu.make_async_copy(buffer, target, go.at[i])
        for i, (buffer, target) in enumerate(zip(buffers, outs))
    ]
    for copy in inward:
        copy.start()
    me = lax.axis_index("wide") * 4 + lax.axis_index("narrow")
    turned = pltpu.roll(small[...], lax.rem(1024 - me * 32, 1024), 1)
    for row in range(8):
        vectors[row][...] = turned[row, :32]
    line, block = 8 + lax.div(me, 8), lax.rem(me, 8)
    rows = lax.broadcasted_iota(jnp.int32, small.shape, 0)
    chosen = pltpu.roll(jnp.where(rows == line, small[...], 0.0), lax.rem(1024 - block * 128, 1024), 1)
    vectors[8][...] = jnp.sum(chosen[:, :128], 0)
    for first, second in zip(inward, outward):
        first.wait()
        second.start()
    for copy in outward:
        copy.wait()


def finish_all(small, arrays, sizes):
    hbm, vmem = pl.BlockSpec(memory_space=pltpu.HBM), pl.BlockSpec(memory_space=pltpu.VMEM)
    results = pl.pallas_call(
        finish_kernel,
        out_shape=[jax.ShapeDtypeStruct(a.shape, a.dtype) for a in arrays]
        + [jax.ShapeDtypeStruct((size,), F32) for size in sizes],
        in_specs=[vmem] + [hbm] * 8,
        out_specs=[hbm] * 8 + [vmem] * 9,
        scratch_shapes=[pltpu.VMEM(a.shape, a.dtype) for a in arrays]
        + [pltpu.SemaphoreType.DMA((8,)), pltpu.SemaphoreType.DMA((8,))],
    )(small, *arrays)
    return results[:8], results[8:]


def fused(tokens, cotangent, seq_length, parts):
    shards = [parts[i] for i in LARGE]
    (
        result, resid, lse, vec, down_part,
        attn_in, queries, keys, values, mixed, ffn_in, slope,
        *weights,
    ) = forward_all(seq_length, tokens, cotangent, [parts[i] for i in SMALL], shards)
    query_w, key_w, value_w, out_w, up_w, down_w = (
        w.reshape(-1, w.shape[-1]) for w in weights
    )
    down_part = down_part.reshape(weights[5].shape)
    order = (13, 11, 7, 2, 4, 5)
    grad_tokens, small, large = backward_all(
        seq_length,
        vec,
        lse,
        [tokens, cotangent, attn_in, queries, keys, values, mixed, ffn_in, slope, resid]
        + [query_w, key_w, value_w, out_w, up_w, down_w, down_part],
        [parts[i].shape for i in order],
    )
    (result, grad_tokens, *large), vectors = finish_all(
        small, [result, grad_tokens, *large], [parts[i].shape[0] for i in SMALL]
    )
    sums = [None] * 15
    for i, array in zip(order + SMALL, [*large, *vectors]):
        sums[i] = array
    return result, grad_tokens, sums


def is_fast():
    return lax.axis_size("wide") == 8 and lax.axis_size("narrow") == 4


def norm_forward(value, gain, shift):
    center = value - jnp.mean(value, -1, keepdims=True)
    inverse = lax.rsqrt(jnp.mean(center * center, -1, keepdims=True) + EPSILON)
    normed = center * inverse
    return (normed * gain.astype(jnp.float32) + shift.astype(jnp.float32), normed, inverse)


def norm_backward(incoming, normed, inverse, gain):
    scaled = incoming * gain.astype(jnp.float32)
    inner = (
        scaled
        - jnp.mean(scaled, -1, keepdims=True)
        - normed * jnp.mean(scaled * normed, -1, keepdims=True)
    )
    return (inverse * inner, jnp.sum(incoming * normed, 0), jnp.sum(incoming, 0))


def gelu_parts(hidden):
    cdf = 0.5 * (1.0 + lax.erf(hidden * 0.7071067811865476))
    density = jnp.exp(-0.5 * hidden * hidden) * 0.3989422804014327
    return (hidden * cdf, cdf + hidden * density)


def masked_scores(queries, keys, length):
    count = queries.shape[0]
    raw = jnp.einsum("qhd,khd->hqk", queries, keys, preferred_element_type=jnp.float32) * HD ** (
        -0.5
    )
    position = jnp.arange(count, dtype=jnp.int32)
    distance = (position[:, None] - position[None, :]).astype(jnp.float32)
    slopes = jnp.exp2(-8.0 * jnp.arange(1, H + 1, dtype=jnp.float32) / H)
    raw = raw - slopes[:, None, None] * distance[None]
    allowed = (position[:, None] >= position[None, :]) & (
        position[:, None] // length == position[None, :] // length
    )
    return jnp.where(allowed[None], raw, -1e30)


def forward(tokens, length, weights):
    (
        first_gain,
        first_shift,
        query_weight,
        query_bias,
        key_weight,
        value_weight,
        value_bias,
        out_weight,
        out_bias,
        second_gain,
        second_shift,
        up_weight,
        up_bias,
        down_weight,
        down_bias,
    ) = weights
    count = tokens.shape[0]
    width = tokens.shape[1]
    inputs = tokens.astype(jnp.float32)
    first_out, first_normed, first_inverse = norm_forward(inputs, first_gain, first_shift)
    attn_in = first_out.astype(jnp.bfloat16)
    queries = (
        (
            jnp.dot(attn_in, query_weight, preferred_element_type=jnp.float32)
            + query_bias.astype(jnp.float32)
        )
        .astype(jnp.bfloat16)
        .reshape(count, H, HD)
    )
    keys = (
        jnp.dot(attn_in, key_weight, preferred_element_type=jnp.float32)
        .astype(jnp.bfloat16)
        .reshape(count, H, HD)
    )
    values = (
        (
            jnp.dot(attn_in, value_weight, preferred_element_type=jnp.float32)
            + value_bias.astype(jnp.float32)
        )
        .astype(jnp.bfloat16)
        .reshape(count, H, HD)
    )
    scores = masked_scores(queries, keys, length)
    top = jnp.max(scores, -1, keepdims=True)
    expo = jnp.exp(scores - top)
    total = jnp.sum(expo, -1, keepdims=True)
    probs = expo / total
    log_total = top + jnp.log(total)
    mixed = jnp.einsum(
        "hqk,khd->qhd", probs.astype(jnp.bfloat16), values, preferred_element_type=jnp.float32
    )
    mixed = mixed.reshape(count, width).astype(jnp.bfloat16)
    resid = (
        inputs
        + jnp.dot(mixed, out_weight, preferred_element_type=jnp.float32)
        + out_bias.astype(jnp.float32)
    )
    second_out, second_normed, second_inverse = norm_forward(resid, second_gain, second_shift)
    ffn_in = second_out.astype(jnp.bfloat16)
    hidden = jnp.dot(ffn_in, up_weight, preferred_element_type=jnp.float32) + up_bias.astype(
        jnp.float32
    )
    active, active_slope = gelu_parts(hidden)
    active_low = active.astype(jnp.bfloat16)
    result = (
        resid
        + jnp.dot(active_low, down_weight, preferred_element_type=jnp.float32)
        + down_bias.astype(jnp.float32)
    )
    return (
        result.astype(jnp.bfloat16),
        attn_in,
        first_normed,
        first_inverse,
        queries,
        keys,
        values,
        log_total,
        mixed,
        second_normed,
        second_inverse,
        ffn_in,
        active_slope,
        active_low,
    )


def backward(cotangent, length, weights, kept):
    (
        first_gain,
        first_shift,
        query_weight,
        query_bias,
        key_weight,
        value_weight,
        value_bias,
        out_weight,
        out_bias,
        second_gain,
        second_shift,
        up_weight,
        up_bias,
        down_weight,
        down_bias,
    ) = weights
    (
        result,
        attn_in,
        first_normed,
        first_inverse,
        queries,
        keys,
        values,
        log_total,
        mixed,
        second_normed,
        second_inverse,
        ffn_in,
        active_slope,
        active_low,
    ) = kept
    count = cotangent.shape[0]
    width = cotangent.shape[1]
    grad_out = cotangent.astype(jnp.float32)
    grad_down_bias = jnp.sum(grad_out, 0)
    grad_down_weight = jnp.einsum(
        "tf,td->fd", active_low, cotangent, preferred_element_type=jnp.float32
    )
    grad_active = jnp.einsum(
        "td,fd->tf", cotangent, down_weight, preferred_element_type=jnp.float32
    )
    grad_hidden = (grad_active * active_slope).astype(jnp.bfloat16)
    grad_up_bias = jnp.sum(grad_hidden.astype(jnp.float32), 0)
    grad_up_weight = jnp.einsum(
        "td,tf->df", ffn_in, grad_hidden, preferred_element_type=jnp.float32
    )
    grad_ffn_in = jnp.einsum(
        "tf,df->td", grad_hidden, up_weight, preferred_element_type=jnp.float32
    )
    grad_second, grad_second_gain, grad_second_shift = norm_backward(
        grad_ffn_in, second_normed, second_inverse, second_gain
    )
    grad_resid = grad_out + grad_second
    grad_branch = grad_resid.astype(jnp.bfloat16)
    grad_out_bias = jnp.sum(grad_branch.astype(jnp.float32), 0)
    grad_out_weight = jnp.einsum(
        "tc,td->cd", mixed, grad_branch, preferred_element_type=jnp.float32
    )
    grad_mixed = jnp.einsum(
        "td,cd->tc", grad_branch, out_weight, preferred_element_type=jnp.float32
    )
    grad_mixed = grad_mixed.astype(jnp.bfloat16).reshape(count, H, HD)
    scores = masked_scores(queries, keys, length)
    probs = jnp.exp(scores - log_total)
    grad_probs = jnp.einsum("qhd,khd->hqk", grad_mixed, values, preferred_element_type=jnp.float32)
    grad_values = jnp.einsum(
        "hqk,qhd->khd", probs.astype(jnp.bfloat16), grad_mixed, preferred_element_type=jnp.float32
    )
    grad_values = grad_values.astype(jnp.bfloat16).reshape(count, width)
    row_total = jnp.sum(grad_probs * probs, -1, keepdims=True)
    grad_scores = (probs * (grad_probs - row_total)).astype(jnp.bfloat16)
    factor = HD ** (-0.5)
    grad_queries = (
        jnp.einsum("hqk,khd->qhd", grad_scores, keys, preferred_element_type=jnp.float32) * factor
    )
    grad_queries = grad_queries.astype(jnp.bfloat16).reshape(count, width)
    grad_keys = (
        jnp.einsum("hqk,qhd->khd", grad_scores, queries, preferred_element_type=jnp.float32)
        * factor
    )
    grad_keys = grad_keys.astype(jnp.bfloat16).reshape(count, width)
    grad_query_bias = jnp.sum(grad_queries.astype(jnp.float32), 0)
    grad_value_bias = jnp.sum(grad_values.astype(jnp.float32), 0)
    grad_query_weight = jnp.einsum(
        "tc,td->cd", attn_in, grad_queries, preferred_element_type=jnp.float32
    )
    grad_key_weight = jnp.einsum(
        "tc,td->cd", attn_in, grad_keys, preferred_element_type=jnp.float32
    )
    grad_value_weight = jnp.einsum(
        "tc,td->cd", attn_in, grad_values, preferred_element_type=jnp.float32
    )
    grad_attn = jnp.einsum(
        "td,cd->tc", grad_queries, query_weight, preferred_element_type=jnp.float32
    )
    grad_attn = grad_attn + jnp.einsum(
        "td,cd->tc", grad_keys, key_weight, preferred_element_type=jnp.float32
    )
    grad_attn = grad_attn + jnp.einsum(
        "td,cd->tc", grad_values, value_weight, preferred_element_type=jnp.float32
    )
    grad_first, grad_first_gain, grad_first_shift = norm_backward(
        grad_attn, first_normed, first_inverse, first_gain
    )
    grad_tokens = (grad_resid + grad_first).astype(jnp.bfloat16)
    sums = spread(
        (
            grad_first_gain,
            grad_first_shift,
            grad_query_weight,
            grad_query_bias,
            grad_key_weight,
            grad_value_weight,
            grad_value_bias,
            grad_out_weight,
            grad_out_bias,
            grad_second_gain,
            grad_second_shift,
            grad_up_weight,
            grad_up_bias,
            grad_down_weight,
            grad_down_bias,
        )
    )
    return (grad_tokens, sums)


def body(
    tokens,
    cotangent,
    seq_length,
    first_gain,
    first_shift,
    query_weight,
    query_bias,
    key_weight,
    value_weight,
    value_bias,
    out_weight,
    out_bias,
    second_gain,
    second_shift,
    up_weight,
    up_bias,
    down_weight,
    down_bias,
):
    shards = (
        first_gain,
        first_shift,
        query_weight,
        query_bias,
        key_weight,
        value_weight,
        value_bias,
        out_weight,
        out_bias,
        second_gain,
        second_shift,
        up_weight,
        up_bias,
        down_weight,
        down_bias,
    )
    if is_fast():
        result, grad_tokens, sums = fused(tokens, cotangent, seq_length, shards)
        return (result, grad_tokens, *sums)
    length = seq_length[0]
    weights = collect(shards)
    kept = forward(tokens, length, weights)
    grad_tokens, sums = backward(cotangent, length, weights, kept)
    (
        g_first_gain,
        g_first_shift,
        g_query_weight,
        g_query_bias,
        g_key_weight,
        g_value_weight,
        g_value_bias,
        g_out_weight,
        g_out_bias,
        g_second_gain,
        g_second_shift,
        g_up_weight,
        g_up_bias,
        g_down_weight,
        g_down_bias,
    ) = sums
    return (
        kept[0],
        grad_tokens,
        g_first_gain,
        g_first_shift,
        g_query_weight,
        g_query_bias,
        g_key_weight,
        g_value_weight,
        g_value_bias,
        g_out_weight,
        g_out_bias,
        g_second_gain,
        g_second_shift,
        g_up_weight,
        g_up_bias,
        g_down_weight,
        g_down_bias,
    )


def solution(mesh):
    placed = (
        P(("wide", "narrow"), None),
        P(("wide", "narrow"), None),
        P(("wide", "narrow")),
        P(("wide", "narrow")),
        P(("wide", "narrow")),
        P(("wide", "narrow"), None),
        P(("wide", "narrow")),
        P(("wide", "narrow"), None),
        P(("wide", "narrow"), None),
        P(("wide", "narrow")),
        P(("wide", "narrow"), None),
        P(("wide", "narrow")),
        P(("wide", "narrow")),
        P(("wide", "narrow")),
        P(("wide", "narrow"), None),
        P(("wide", "narrow")),
        P(("wide", "narrow"), None),
        P(("wide", "narrow")),
    )
    return jax.shard_map(
        body,
        mesh=mesh,
        in_specs=placed,
        out_specs=(
            P(("wide", "narrow"), None),
            P(("wide", "narrow"), None),
            P(("wide", "narrow")),
            P(("wide", "narrow")),
            P(("wide", "narrow"), None),
            P(("wide", "narrow")),
            P(("wide", "narrow"), None),
            P(("wide", "narrow"), None),
            P(("wide", "narrow")),
            P(("wide", "narrow"), None),
            P(("wide", "narrow")),
            P(("wide", "narrow")),
            P(("wide", "narrow")),
            P(("wide", "narrow"), None),
            P(("wide", "narrow")),
            P(("wide", "narrow"), None),
            P(("wide", "narrow")),
        ),
        check_vma=False,
    )
```

```python
import functools

import jax
import jax.numpy as jnp
from jax import lax
from jax.experimental import pallas as pl
from jax.experimental.pallas import tpu as pltpu
from jax.sharding import PartitionSpec as P

H = 8
HD = 128
AXES = ("wide", "narrow")
MESH = pl.DeviceIdType.MESH
BF = jnp.bfloat16
F32 = jnp.float32


class Place:
    def __init__(self):
        wide, narrow = lax.axis_index("wide"), lax.axis_index("narrow")
        self.z, self.x = lax.div(wide, 2), lax.rem(wide, 2)
        self.y, self.c = lax.div(narrow, 2), lax.rem(narrow, 2)
        c, x, y = self.c, self.x, self.y
        self.one = (x + (1 - c) * (1 - 2 * x), y + c * (1 - 2 * y))
        self.two = (x + c * (1 - 2 * x), y + (1 - c) * (1 - 2 * y))
        self.far = (1 - x, 1 - y)
        self.here = (x, y)

    def device(self, z, xy, c):
        return (z * 2 + xy[0], xy[1] * 2 + c)

    def up(self, step):
        return lax.rem(self.z + step, 4)

    def down(self, step):
        return lax.rem(self.z + 4 - step, 4)

    def partners(self):
        z, c = self.z, self.c
        return [self.device(self.up(step), self.here, c) for step in (1, 2, 3)] + [
            self.device(z, self.one, c),
            self.device(z, self.two, c),
            self.device(z, self.here, 1 - c),
        ]

    def greet(self):
        barrier = pltpu.get_barrier_semaphore()
        partners = self.partners()
        for partner in partners:
            pl.semaphore_signal(barrier, inc=1, device_id=partner, device_id_type=MESH)
        pl.semaphore_wait(barrier, len(partners))


def remote(source, target, send, recv, device):
    return pltpu.make_async_remote_copy(
        src_ref=source,
        dst_ref=target,
        send_sem=send,
        recv_sem=recv,
        device_id=device,
        device_id_type=MESH,
    )


class Gathering:
    SEMS = 10
    STAGES = 5

    def __init__(self, place, local, full, send, recv, keep):
        self.place, self.local, self.full = place, local, full
        self.send, self.recv, self.keep = send, recv, keep

    def block(self, xy, c):
        return self.full.at[:, xy[0], xy[1], c]

    def cell(self, z):
        place = self.place
        return self.full.at[z, place.x, place.y, place.c]

    def copy(self, source, target, sem, device):
        return remote(source, target, self.send.at[sem], self.recv.at[sem], device)

    def along(self, step):
        place = self.place
        device = place.device(place.up(step), place.here, place.c)
        return self.copy(self.local, self.cell(place.z), step - 1, device)

    def pieces(self):
        place = self.place
        z, c = place.z, place.c
        one, two = place.device(z, place.one, c), place.device(z, place.two, c)
        twin = place.device(z, place.here, 1 - c)
        mine, first = self.block(place.here, c), self.block(place.one, c)
        second, far = self.block(place.two, c), self.block(place.far, c)
        return {
            3: (mine, one, self.block(place.one, c)),
            4: (mine, two, self.block(place.two, c)),
            5: (mine, twin, self.block(place.here, 1 - c)),
            6: (first, two, self.block(place.far, c)),
            7: (first, twin, self.block(place.two, 1 - c)),
            8: (second, twin, self.block(place.one, 1 - c)),
            9: (far, twin, self.block(place.far, 1 - c)),
        }

    def start(self, sem):
        source, device, _ = self.pieces()[sem]
        self.copy(source, source, sem, device).start()

    def await_recv(self, sem):
        _, device, landing = self.pieces()[sem]
        self.copy(landing, landing, sem, device).wait_recv()

    def own(self):
        return pltpu.make_async_copy(self.local, self.cell(self.place.z), self.keep)

    def stage(self, number):
        place = self.place
        if number == 0:
            self.own().start()
            for step in (1, 2, 3):
                self.along(step).start()
        elif number == 1:
            self.own().wait()
            for step in (1, 2, 3):
                cell = self.cell(place.down(step))
                device = place.device(place.down(step), place.here, place.c)
                self.copy(cell, cell, step - 1, device).wait_recv()
            for sem in (3, 4, 5):
                self.start(sem)
        elif number == 2:
            self.await_recv(3)
            self.start(6)
            self.start(7)
            self.await_recv(4)
            self.start(8)
        elif number == 3:
            self.await_recv(6)
            self.start(9)
        elif number == 4:
            for sem in (5, 7, 8, 9):
                self.await_recv(sem)

    def finish(self):
        for step in (1, 2, 3):
            self.along(step).wait_send()
        for sem in range(3, 10):
            source, device, _ = self.pieces()[sem]
            self.copy(source, source, sem, device).wait_send()


class GatheringSides(Gathering):
    def cell_at(self, xy):
        return self.full.at[self.place.z, xy[0], xy[1], self.place.c]

    def layer(self, z, c):
        return self.full.at[z, :, :, c]

    def moves(self):
        place = self.place
        z, c = place.z, place.c
        one, two = place.device(z, place.one, c), place.device(z, place.two, c)
        twin = place.device(z, place.here, 1 - c)
        here, first, mine = self.cell_at(place.here), self.cell_at(place.one), self.layer(z, c)
        table = {
            0: (self.local, here, one, first),
            1: (self.local, here, two, self.cell_at(place.two)),
            2: (first, first, two, self.cell_at(place.far)),
            6: (mine, mine, twin, self.layer(z, 1 - c)),
        }
        for step in (1, 2, 3):
            other = place.down(step)
            block = self.layer(other, c)
            table[2 + step] = (mine, mine, place.device(place.up(step), place.here, c), block)
            table[6 + step] = (block, block, twin, self.layer(other, 1 - c))
        return table

    def start(self, sem):
        source, target, device, _ = self.moves()[sem]
        self.copy(source, target, sem, device).start()

    def await_recv(self, sem):
        _, _, device, landing = self.moves()[sem]
        self.copy(landing, landing, sem, device).wait_recv()

    def stage(self, number):
        if number == 0:
            self.own().start()
            self.start(0)
            self.start(1)
        elif number == 1:
            self.await_recv(0)
            self.start(2)
            self.await_recv(1)
            self.own().wait()
        elif number == 2:
            self.await_recv(2)
            for sem in (3, 4, 5, 6):
                self.start(sem)
        elif number == 3:
            for step in (1, 2, 3):
                self.await_recv(2 + step)
                self.start(6 + step)
        elif number == 4:
            for sem in (6, 7, 8, 9):
                self.await_recv(sem)

    def finish(self):
        for sem in range(10):
            source, target, device, _ = self.moves()[sem]
            self.copy(source, target, sem, device).wait_send()


class Scattering:
    SEMS = 7
    STAGES = 5

    def __init__(self, place, partial, mine, total, pair, line, out, send, recv, load):
        self.place, self.partial, self.mine = place, partial, mine
        self.total, self.pair, self.line, self.out = total, pair, line, out
        self.send, self.recv, self.load = send, recv, load

    def pieces(self):
        place = self.place
        z, c = place.z, place.c
        one, two = place.device(z, place.one, c), place.device(z, place.two, c)
        twin = place.device(z, place.here, 1 - c)
        total = self.total

        def block(xy):
            return total.at[:, xy[0], xy[1]]

        table = {
            0: (self.partial.at[:, :, :, 1 - c], total, twin),
            1: (block(place.two), self.pair.at[0], two),
            2: (block(place.far), self.pair.at[1], two),
            3: (block(place.one), self.pair.at[2], one),
        }
        for step in (1, 2, 3):
            device = place.device(place.up(step), place.here, c)
            table[3 + step] = (
                total.at[place.up(step), place.x, place.y],
                self.line.at[step - 1],
                device,
            )
        return table

    def copy(self, sem):
        source, target, device = self.pieces()[sem]
        return remote(source, target, self.send.at[sem], self.recv.at[sem], device)

    def own(self):
        return pltpu.make_async_copy(
            self.partial.at[:, :, :, self.place.c], self.mine, self.load
        )

    def join(self):
        total, mine = self.total, self.mine
        self.own().wait()
        self.copy(0).wait_recv()

        def body(z, carry):
            for x in range(2):
                for y in range(2):
                    total[z, x, y] = total[z, x, y] + mine[z, x, y]
            return carry

        lax.fori_loop(0, 4, body, 0)

    def stage(self, number):
        place, total, pair = self.place, self.total, self.pair

        def add(xy, slot):
            def body(z, carry):
                total[z, xy[0], xy[1]] = total[z, xy[0], xy[1]] + pair[slot, z]
                return carry

            lax.fori_loop(0, 4, body, 0)

        if number == 0:
            self.own().start()
            self.copy(0).start()
        elif number == 1:
            self.join()
            self.copy(2).start()
            self.copy(1).start()
        elif number == 2:
            self.copy(2).wait_recv()
            add(place.one, 1)
            self.copy(3).start()
            self.copy(1).wait_recv()
            add(place.here, 0)
        elif number == 3:
            self.copy(3).wait_recv()
            add(place.here, 2)
            for step in (1, 2, 3):
                self.copy(3 + step).start()
        elif number == 4:
            value = total[place.z, place.x, place.y].astype(F32)
            for step in (1, 2, 3):
                self.copy(3 + step).wait_recv()
                value = value + self.line[step - 1].astype(F32)
            self.out[...] = value

    def finish(self):
        for sem in range(7):
            self.copy(sem).wait_send()


class ScatteringSides(Scattering):
    def pieces(self):
        place, total = self.place, self.total
        z, c = place.z, place.c
        one, two = place.device(z, place.one, c), place.device(z, place.two, c)
        twin = place.device(z, place.here, 1 - c)

        def cell(xy):
            return total.at[z, xy[0], xy[1]]

        table = {
            0: (self.partial.at[:, :, :, 1 - c], total, twin),
            1: (cell(place.two), self.line.at[0], two),
            2: (cell(place.far), self.line.at[1], two),
            3: (cell(place.one), self.line.at[2], one),
        }
        for step in (1, 2, 3):
            device = place.device(place.up(step), place.here, c)
            table[3 + step] = (total.at[place.up(step)], self.pair.at[step - 1], device)
        return table

    def stage(self, number):
        place, total, pair, line = self.place, self.total, self.pair, self.line
        z = place.z

        def add(xy, slot):
            total[z, xy[0], xy[1]] = total[z, xy[0], xy[1]] + line[slot]

        if number == 0:
            self.own().start()
            self.copy(0).start()
        elif number == 1:
            self.join()
            for step in (1, 2, 3):
                self.copy(3 + step).start()
        elif number == 2:
            for step in (1, 2, 3):
                self.copy(3 + step).wait_recv()

            def body(x, carry):
                for y in range(2):
                    value = total[z, x, y].astype(F32)
                    for step in range(3):
                        value = value + pair[step, x, y].astype(F32)
                    total[z, x, y] = value.astype(BF)
                return carry

            lax.fori_loop(0, 2, body, 0)
            self.copy(2).start()
            self.copy(1).start()
        elif number == 3:
            self.copy(2).wait_recv()
            add(place.one, 1)
            self.copy(3).start()
            self.copy(1).wait_recv()
            add(place.here, 0)
        elif number == 4:
            self.copy(3).wait_recv()
            value = total[z, place.x, place.y].astype(F32) + line[2].astype(F32)
            self.out[...] = value


class Summing:
    SEMS = 6

    def __init__(self, place, value, total, slots, send, recv):
        self.place, self.value, self.total, self.slots = place, value, total, slots
        self.send, self.recv = send, recv

    def copy(self, sem):
        place = self.place
        device = [
            place.device(place.z, place.here, 1 - place.c),
            place.device(place.z, place.one, place.c),
            place.device(place.z, place.two, place.c),
        ] + [place.device(place.up(step), place.here, place.c) for step in (1, 2, 3)]
        source = self.total.at[min(sem, 3)]
        return remote(source, self.slots.at[sem], self.send.at[sem], self.recv.at[sem], device[sem])

    def stage(self, number):
        total, slots = self.total, self.slots
        if number == 0:
            total[0] = self.value[...]
            self.copy(0).start()
        elif number < 3:
            self.copy(number - 1).wait_recv()
            total[number] = total[number - 1] + slots[number - 1]
            self.copy(number).start()
        elif number == 3:
            self.copy(2).wait_recv()
            total[3] = total[2] + slots[2]
            for sem in (3, 4, 5):
                self.copy(sem).start()
        elif number == 4:
            value = total[3]
            for sem in (3, 4, 5):
                self.copy(sem).wait_recv()
                value = value + slots[sem]
            total[4] = value

    def finish(self):
        for sem in range(6):
            self.copy(sem).wait_send()


def run_tick(tasks, ticks, number, done=None):
    for stage in reversed(range(5)):
        for g, task in enumerate(tasks):
            if ticks[g][stage] == number:
                task.stage(stage)
                if stage == 4 and done is not None:
                    done(g)


def halves(ref, count, width):
    if count == 1:
        return [ref]
    lead = (slice(None),) * (len(ref.shape) - 1)
    return [ref.at[lead + (pl.ds(i * width, width),)] for i in range(count)]


SMALL = (0, 1, 3, 6, 8, 9, 10, 14, 12)
LARGE = (2, 4, 5, 7, 11, 13)


EPSILON = 1e-05


def collect(parts):
    (
        first_gain,
        first_shift,
        query_weight,
        query_bias,
        key_weight,
        value_weight,
        value_bias,
        out_weight,
        out_bias,
        second_gain,
        second_shift,
        up_weight,
        up_bias,
        down_weight,
        down_bias,
    ) = parts
    return (
        lax.all_gather(first_gain, ("wide", "narrow"), axis=0, tiled=True),
        lax.all_gather(first_shift, ("wide", "narrow"), axis=0, tiled=True),
        lax.all_gather(query_weight, ("wide", "narrow"), axis=0, tiled=True),
        lax.all_gather(query_bias, ("wide", "narrow"), axis=0, tiled=True),
        lax.all_gather(key_weight, ("wide", "narrow"), axis=0, tiled=True),
        lax.all_gather(value_weight, ("wide", "narrow"), axis=0, tiled=True),
        lax.all_gather(value_bias, ("wide", "narrow"), axis=0, tiled=True),
        lax.all_gather(out_weight, ("wide", "narrow"), axis=0, tiled=True),
        lax.all_gather(out_bias, ("wide", "narrow"), axis=0, tiled=True),
        lax.all_gather(second_gain, ("wide", "narrow"), axis=0, tiled=True),
        lax.all_gather(second_shift, ("wide", "narrow"), axis=0, tiled=True),
        lax.all_gather(up_weight, ("wide", "narrow"), axis=0, tiled=True),
        lax.all_gather(up_bias, ("wide", "narrow"), axis=0, tiled=True),
        lax.all_gather(down_weight, ("wide", "narrow"), axis=0, tiled=True),
        lax.all_gather(down_bias, ("wide", "narrow"), axis=0, tiled=True),
    )


def spread(parts):
    (
        first_gain,
        first_shift,
        query_weight,
        query_bias,
        key_weight,
        value_weight,
        value_bias,
        out_weight,
        out_bias,
        second_gain,
        second_shift,
        up_weight,
        up_bias,
        down_weight,
        down_bias,
    ) = parts
    return (
        lax.psum_scatter(first_gain, ("wide", "narrow"), scatter_dimension=0, tiled=True),
        lax.psum_scatter(first_shift, ("wide", "narrow"), scatter_dimension=0, tiled=True),
        lax.psum_scatter(query_weight, ("wide", "narrow"), scatter_dimension=0, tiled=True),
        lax.psum_scatter(query_bias, ("wide", "narrow"), scatter_dimension=0, tiled=True),
        lax.psum_scatter(key_weight, ("wide", "narrow"), scatter_dimension=0, tiled=True),
        lax.psum_scatter(value_weight, ("wide", "narrow"), scatter_dimension=0, tiled=True),
        lax.psum_scatter(value_bias, ("wide", "narrow"), scatter_dimension=0, tiled=True),
        lax.psum_scatter(out_weight, ("wide", "narrow"), scatter_dimension=0, tiled=True),
        lax.psum_scatter(out_bias, ("wide", "narrow"), scatter_dimension=0, tiled=True),
        lax.psum_scatter(second_gain, ("wide", "narrow"), scatter_dimension=0, tiled=True),
        lax.psum_scatter(second_shift, ("wide", "narrow"), scatter_dimension=0, tiled=True),
        lax.psum_scatter(up_weight, ("wide", "narrow"), scatter_dimension=0, tiled=True),
        lax.psum_scatter(up_bias, ("wide", "narrow"), scatter_dimension=0, tiled=True),
        lax.psum_scatter(down_weight, ("wide", "narrow"), scatter_dimension=0, tiled=True),
        lax.psum_scatter(down_bias, ("wide", "narrow"), scatter_dimension=0, tiled=True),
    )


LOG2E = 1.4426950408889634
WEIGHTS = ("query", "key", "value", "out", "up", "down")


def dot(left, right, form):
    dims = (((0,) if form[0] == "T" else (1,), (1,) if form[1] == "T" else (0,)), ((), ()))
    return lax.dot_general(left, right, dims, preferred_element_type=F32)


def at(index, size):
    return pl.ds(pl.multiple_of(index * size, size), size)


def loop(count, body, unroll=1):
    def step(i, carry):
        body(i)
        return carry

    lax.fori_loop(0, count, step, 0, unroll=unroll)


def normed_rows(value):
    center = value - jnp.mean(value, -1, keepdims=True)
    inverse = lax.rsqrt(jnp.mean(center * center, -1, keepdims=True) + EPSILON)
    return center * inverse, inverse


def gelu_pair(hidden):
    cdf = 0.5 * (1.0 + lax.erf(hidden * 0.7071067811865476))
    density = jnp.exp2(hidden * hidden * (-0.5 * LOG2E)) * 0.3989422804014327
    return hidden * cdf, cdf + hidden * density


def pack_small(vectors, packed):
    packed[...] = jnp.zeros_like(packed)
    for row, vector in enumerate(vectors):
        size = vector.shape[0]
        packed[row : row + 1, :size] = vector[...].astype(F32).reshape(1, size)


def unpack_small(small, vec):
    table = small.reshape(512, 128)
    lane = lax.broadcasted_iota(jnp.int32, (128, 1024), 0)
    column = lax.broadcasted_iota(jnp.int32, (128, 1024), 1)
    pick = jnp.where(lane == lax.rem(column, 32), 1.0, 0.0).astype(BF)
    device = lax.broadcasted_iota(jnp.int32, (32, 16, 1024), 0)
    owner = lax.div(lax.broadcasted_iota(jnp.int32, (32, 16, 1024), 2), 32)
    spread_out = dot(table[...].astype(BF), pick, "NN").reshape(32, 16, 1024)
    vec[...] = jnp.sum(jnp.where(device == owner, spread_out, 0.0), 0)
    for part in range(4):
        for block in range(8):
            source = (part * 8 + block) * 16 + 8
            vec[8 + part : 9 + part, block * 128 : block * 128 + 128] = table[source : source + 1, :]


def prepare_bias(length, mask, ramp):
    key = lax.broadcasted_iota(jnp.int32, (256, 256), 0)
    query = lax.broadcasted_iota(jnp.int32, (256, 256), 1)
    long = length == 1024
    same = (lax.div(key, 128) == lax.div(query, 128)) | long
    mask[...] = jnp.where((key <= query) & same, 0.0, -1e30)
    ramp[...] = lax.broadcasted_iota(jnp.int32, (1024, 128), 0).astype(F32)
    return jnp.where(long, 0.0, -1e30)


def wide(value):
    return jnp.concatenate([value, value], axis=1)


def attention_head(head, slope, off, queries, keys, values, mixed, lse, mask, ramp, tilt):
    cols = at(head, 128)
    factor = HD**-0.5 * LOG2E
    tilt[...] = ramp[...] * slope
    for i in range(4):
        rows, before = slice(i * 256, i * 256 + 256), slice(0, i * 256)
        query = queries[rows, cols]
        near = dot(keys[rows, cols], query, "NT") * factor + wide(tilt[rows, :]) + mask[...]
        top = jnp.max(near, 0, keepdims=True)
        if i:
            past = dot(keys[before, cols], query, "NT") * factor + wide(tilt[before, :])
            top = jnp.maximum(top, jnp.max(past, 0, keepdims=True) + off)
        near = jnp.exp2(near - top)
        total = jnp.sum(near, 0, keepdims=True)
        out = dot(values[rows, cols], near.astype(BF), "TN")
        if i:
            past = jnp.exp2(past + (off - top))
            total = total + jnp.sum(past, 0, keepdims=True)
            out = out + dot(values[before, cols], past.astype(BF), "TN")
        mixed[rows, cols] = (out * (1.0 / total)).T.astype(BF)
        lse[pl.ds(head, 1), rows] = top + jnp.log2(total)


def forward_kernel(length_ref, tokens_in, cotangent_in, *refs):
    refs = list(refs)

    def take(count):
        taken, refs[:count] = refs[:count], []
        return taken

    vectors = take(9)
    local = take(6)
    result_out, resid_out, lse_out, small_out, down_out = take(5)
    attn_out, query_out, key_out, value_out, mixed_out, ffn_out, slope_out = take(7)
    weight_out = take(6)
    full = take(7)
    act, slope, mixed, ffn_in = take(4)
    resid, vec, lse, mask, ramp, tilt, stage = take(7)
    tokens, cotangent, packed = take(3)
    send, recv, keep, store, dump, stage_sem, input_sem = take(7)
    local = [packed] + local
    fetches = [
        pltpu.make_async_copy(source, target, input_sem.at[i])
        for i, (source, target) in enumerate(((tokens_in, tokens), (cotangent_in, cotangent)))
    ]
    for fetch in fetches:
        fetch.start()
    pack_small(vectors, packed)

    place = Place()
    place.greet()
    tasks, dumps = [], []
    for i, cut in enumerate((1, 1, 1, 1, 1, 4, 4)):
        width = local[i].shape[-1] // cut
        for j in range(cut):
            g = len(tasks)
            views = [halves(ref, cut, width)[j] for ref in (local[i], full[i])]
            kind = GatheringSides if g == 12 else Gathering
            tasks.append(kind(place, *views, send.at[g], recv.at[g], keep.at[g]))
            if i:
                target = halves(weight_out[i - 1], cut, width)[j]
                dumps.append(pltpu.make_async_copy(views[1], target, dump.at[g - 1]))

    ticks = [[0, 1, 2, 3, 4]] + [[g - 1 + stage for stage in range(5)] for g in range(1, 5)]
    ticks += [[g - 3, g - 1, g + 1, g + 2, g + 3] for g in range(5, 12)]
    ticks += [[0, 1, 5, 11, 12]]

    def done(g):
        if g:
            dumps[g - 1].start()

    def tick(number):
        run_tick(tasks, ticks, number, done)

    saves = []

    def save(source, target):
        copy = pltpu.make_async_copy(source, target, store.at[len(saves)])
        copy.start()
        saves.append(copy)

    query_w, key_w, value_w, out_w = (ref.reshape(1024, 1024) for ref in full[1:5])
    up_w, down_w = full[5].reshape(1024, 4096), full[6].reshape(4096, 1024)
    attn_in, queries, keys, values = (act.at[i] for i in range(4))
    length = length_ref[0]
    off = prepare_bias(length, mask, ramp)

    tick(0)
    tick(1)
    fetches[0].wait()

    def first_stats(i):
        rows = at(i, 128)
        normed, _ = normed_rows(tokens[rows, :].astype(F32))
        resid[rows, :] = normed

    loop(8, first_stats)
    for number in range(2, 5):
        tick(number)
    unpack_small(full[0], vec)

    def first_norm(i):
        rows = at(i, 128)
        attn_in[rows, :] = (resid[rows, :] * vec[0:1, :] + vec[1:2, :]).astype(BF)

    loop(8, first_norm)
    save(attn_in, attn_out)

    def project(weight, target, bias):
        def body(i):
            cols = at(i, 512)
            value = dot(attn_in[...], weight[:, cols], "NN")
            if bias is not None:
                value = value + vec[bias : bias + 1, cols]
            target[:, cols] = value.astype(BF)

        loop(2, body, 2)

    project(query_w, queries, 2)
    save(queries, query_out)
    tick(5)
    project(key_w, keys, None)
    save(keys, key_out)
    tick(6)
    project(value_w, values, 3)
    save(values, value_out)

    def heads(first):
        def body(i, slope_now):
            attention_head(
                first + i, slope_now, off, queries, keys, values, mixed, lse, mask, ramp, tilt
            )
            return slope_now * 0.5

        lax.fori_loop(0, 2, body, jnp.float32(LOG2E * 0.5 ** (first + 1)), unroll=2)

    heads(0)
    tick(7)
    heads(2)
    heads(4)
    tick(8)
    heads(6)
    save(mixed, mixed_out)
    save(lse, lse_out)

    def close_attention(i):
        rows = at(i, 256)
        value = dot(mixed[rows, :], out_w[...], "NN") + tokens[rows, :].astype(F32) + vec[4:5, :]
        resid[rows, :] = value
        normed, _ = normed_rows(value)
        ffn_in[rows, :] = (normed * vec[5:6, :] + vec[6:7, :]).astype(BF)

    loop(4, close_attention, 2)
    save(resid, resid_out)
    save(ffn_in, ffn_out)
    for copy in saves[:5]:
        copy.wait()

    def widen(chunk):
        def body(i):
            rows, cols = at(lax.div(i, 2), 512), at(lax.rem(i, 2), 512)
            weight = up_w[:, at(chunk * 2 + lax.rem(i, 2), 512)]
            hidden = dot(ffn_in[rows, :], weight, "NN") + vec[8 + chunk : 9 + chunk, cols]
            active, steep = gelu_pair(hidden)
            act[chunk, rows, cols] = active.astype(BF)
            slope[chunk % 2, rows, cols] = steep.astype(BF)

        if chunk > 1:
            saves[8 + chunk - 2].wait()
        loop(4, body, 2)
        save(slope.at[chunk % 2], slope_out.at[chunk])


    def spill(j, half):
        rows = pl.ds(pl.multiple_of(j * 1024 + half * 512, 512), 512)
        return pltpu.make_async_copy(stage.at[half], down_out.at[rows, :], stage_sem.at[half])

    def grad_down(j):
        for half in range(2):

            if j:
                spill(j - 1, half).wait()
            active = act[j, :, half * 512 : half * 512 + 512]
            stage[half] = dot(active, cotangent[...], "TN").astype(BF)
            spill(j, half).start()

    tick(9)
    widen(0)
    widen(1)
    fetches[1].wait()
    tick(10)
    widen(2)
    grad_down(0)
    tick(11)
    widen(3)
    grad_down(1)

    def narrow(chunk):
        cols = slice(chunk * 256, chunk * 256 + 256)

        def body(i):
            rows = at(i, 512)
            value = resid[rows, cols] + vec[7:8, cols]
            active = jnp.concatenate([act[j, rows, :] for j in range(4)], axis=1)
            value = value + dot(active, down_w[:, cols], "NN")
            mixed[rows, cols] = value.astype(BF)

        loop(2, body, 2)

        save(mixed.at[:, cols], result_out.at[:, cols])

    tick(12)
    narrow(0)
    narrow(3)
    grad_down(2)
    tick(13)
    narrow(1)
    grad_down(3)
    tick(14)
    narrow(2)
    small_out[...] = vec[...]
    for half in range(2):
        spill(3, half).wait()
    for task in tasks:
        task.finish()
    for copy in saves[5:8] + saves[10:]:
        copy.wait()
    for copy in dumps:
        copy.wait()


def forward_all(length, tokens, cotangent, vectors, weights):
    square = jax.ShapeDtypeStruct((1024, 1024), BF)
    tall = jax.ShapeDtypeStruct((4, 1024, 1024), BF)
    f32 = functools.partial(jax.ShapeDtypeStruct, dtype=F32)
    grid6 = [(4, 2, 2, 2) + w.shape for w in weights]
    hbm, vmem = pl.BlockSpec(memory_space=pltpu.HBM), pl.BlockSpec(memory_space=pltpu.VMEM)
    return pl.pallas_call(
        forward_kernel,
        out_shape=[square, f32((1024, 1024)), f32((8, 1024)), f32((16, 1024))]
        + [jax.ShapeDtypeStruct((4096, 1024), BF)]
        + [square] * 6
        + [tall]
        + [jax.ShapeDtypeStruct(s, BF) for s in grid6],
        in_specs=[pl.BlockSpec(memory_space=pltpu.SMEM)] + [hbm] * 2 + [vmem] * 9 + [hbm] * 6,
        out_specs=[hbm, hbm, hbm, vmem] + [hbm] * 14,
        scratch_shapes=[pltpu.VMEM((4, 2, 2, 2, 16, 128), F32)]
        + [pltpu.VMEM(s, BF) for s in grid6]
        + [pltpu.VMEM((4, 1024, 1024), BF), pltpu.VMEM((2, 1024, 1024), BF)]
        + [pltpu.VMEM((1024, 1024), BF)] * 2
        + [
            pltpu.VMEM((1024, 1024), F32),
            pltpu.VMEM((16, 1024), F32),
            pltpu.VMEM((8, 1024), F32),
            pltpu.VMEM((256, 256), F32),
            pltpu.VMEM((1024, 128), F32),
            pltpu.VMEM((1024, 128), F32),
            pltpu.VMEM((2, 512, 1024), BF),
            pltpu.VMEM((1024, 1024), BF),
            pltpu.VMEM((1024, 1024), BF),
            pltpu.VMEM((16, 128), F32),
            pltpu.SemaphoreType.DMA((13, Gathering.SEMS)),
            pltpu.SemaphoreType.DMA((13, Gathering.SEMS)),
            pltpu.SemaphoreType.DMA((13,)),
            pltpu.SemaphoreType.DMA((20,)),
            pltpu.SemaphoreType.DMA((12,)),
            pltpu.SemaphoreType.DMA((2,)),
            pltpu.SemaphoreType.DMA((2,)),
        ],
        compiler_params=pltpu.CompilerParams(
            collective_id=2, has_side_effects=True, vmem_limit_bytes=62 << 20
        ),
    )(length, tokens, cotangent, *vectors, *weights)


SHARDS = ("down", "up", "out", "query", "key", "value")
SCATTER_CUTS = (4, 4, 1, 1, 1, 2)


def attention_head_back(head, slope, off, refs, lse, mask, ramp, tilt, key_sum, value_sum):
    queries, keys, values, mixed, grad_mixed = refs
    cols = at(head, 128)
    factor = HD**-0.5 * LOG2E
    tilt[...] = ramp[...] * slope
    for i in (3, 2, 1, 0):
        rows, upto, before = slice(i * 256, i * 256 + 256), slice(0, i * 256 + 256), i * 256
        query, grad = queries[rows, cols], grad_mixed[rows, cols]
        product = grad.astype(F32) * mixed[rows, cols].astype(F32)
        inner = jnp.sum(product.T, 0, keepdims=True)
        level = lse[pl.ds(head, 1), rows]
        raw = dot(keys[upto, cols], query, "NT") * factor + wide(tilt[upto, :])
        probs = jnp.exp2(raw[before:] + mask[...] - level)
        if i:
            probs = jnp.concatenate([jnp.exp2(raw[:before] + (off - level)), probs], axis=0)
        grad_probs = dot(values[upto, cols], grad, "NT")
        grad_scores = (probs * (grad_probs - inner)).astype(BF)
        value_part = dot(probs.astype(BF), grad, "NN")
        key_part = dot(grad_scores, query, "NN")
        if i == 3:
            value_sum[...] = value_part
            key_sum[...] = key_part
        else:
            value_sum[upto, :] += value_part
            key_sum[upto, :] += key_part
        query_part = dot(keys[upto, cols], grad_scores, "TN") * HD**-0.5
        queries[rows, cols] = query_part.T.astype(BF)
    keys[:, cols] = (key_sum[...] * HD**-0.5).astype(BF)
    values[:, cols] = value_sum[...].astype(BF)


def backward_kernel(length_ref, vec, lse, *refs):
    refs = list(refs)

    def take(count):
        taken, refs[:count] = refs[:count], []
        return taken

    tokens, cotangent, attn_in, queries, keys, values, mixed, ffn_in, slope, resid = take(10)
    query_w, key_w, value_w, out_w, up_w, down_w, down_part = take(7)
    grad_tokens_out, small_out = take(2)
    out = take(6)
    parts = [down_part] + take(5)
    total, pair, line = take(6), take(6), take(6)
    mine_down, mine, sides_pair, sides_line, arena, grad, stage, strip = take(8)
    key_sum, value_sum, mask, ramp, tilt, sums = take(6)
    small_total, small_slots, small_send, small_recv = take(4)
    send, recv, load_sem, slot_sem, stage_sem, strip_sem = take(6)

    place = Place()
    loads = {}

    def load(source, slot):
        copy = pltpu.make_async_copy(source, arena.at[slot], slot_sem.at[slot])
        copy.start()
        loads[slot] = copy

    def ready(slot):
        loads.pop(slot).wait()
        return arena.at[slot]

    def load_chunk(j):
        load(slope.at[j], j % 2)
        load(down_w.at[pl.ds(j * 1024, 1024), :], 2 + j % 2)
        load(up_w.at[:, pl.ds(j * 1024, 1024)], 4 + j % 2)

    load(cotangent, 6)
    load_chunk(0)
    load(ffn_in, 7)
    place.greet()

    tasks = []
    for i, cut in enumerate(SCATTER_CUTS):
        width = parts[i].shape[-1] // cut
        for j in range(cut):
            g = len(tasks)
            own = mine_down.at[g % 2] if i == 0 else mine.at[:, :, :, :, pl.ds(0, width)]
            views = [halves(r, cut, width)[j] for r in (parts[i], total[i], pair[i], line[i], out[i])]
            kind = ScatteringSides if g == 0 else Scattering
            if g == 0:
                views[2:4] = sides_pair, sides_line
            tasks.append(
                kind(place, views[0], own, *views[1:], send.at[g], recv.at[g], load_sem.at[g])
            )
    tasks.append(Summing(place, sums, small_total, small_slots, small_send, small_recv))

    first = (3, 0, 1, 2, 3, 4, 5, 6, 7, 9, 10)
    ticks = [[b, b + 1, b + 3, b + 5, b + 7] for b in first]
    ticks[0] = [3, 4, 9, 11, 13]
    ticks[9:] = [[9, 10, 12, 14, 16], [10, 11, 13, 15, 16]]
    ticks += [[11, 12, 14, 15, 16], [12, 13, 15, 16, 17], [14, 15, 16, 17, 18]]

    def tick(number):
        run_tick(tasks, ticks, number)

    stages = {}

    def emit(part, left, right, width=1024, first=0):
        copies = []
        for half in range(2):
            if half in stages:
                stages.pop(half).wait()
            value = dot(left[:, half * 512 : half * 512 + 512], right[...], "TN")
            stage[half] = value.astype(BF).reshape(2, 2, 2, 2, 32, 1024)
            target = part.at[half * 2 : half * 2 + 2, :, :, :, :, pl.ds(first, width)]
            copy = pltpu.make_async_copy(stage.at[half], target, stage_sem.at[half])
            copy.start()
            stages[half] = copy
            copies.append(copy)

    def settle():
        for half in list(stages):
            stages.pop(half).wait()

    ones = jnp.ones((8, 1024), BF)

    def column_sums(source, row):
        def body(i):
            cols = at(i, 256)
            sums[row : row + 1, cols] = dot(ones, source[:, cols], "NN")[0:1]

        loop(4, body)

    length = length_ref[0]
    off = prepare_bias(length, mask, ramp)
    sums[...] = jnp.zeros_like(sums)
    tick(0)
    cot = ready(6)
    up_part = parts[1]

    for j in range(4):
        if j < 3:
            load_chunk(j + 1)
        hidden_slope, down_chunk, up_chunk = ready(j % 2), ready(2 + j % 2), ready(4 + j % 2)
        if j == 0:
            ffn = ready(7)

        def grad_hidden(i):
            cols = at(i, 512)
            value = dot(cot[...], down_chunk[cols, :], "NT") * hidden_slope[:, cols].astype(F32)
            hidden_slope[:, cols] = value.astype(BF)

        loop(2, grad_hidden, 2)
        column_sums(hidden_slope, 8 + j)
        if j == 0:
            tick(1)
        emit(up_part, ffn, hidden_slope, 1024, j * 1024)
        if j:
            tick(j + 2)

        def grad_ffn(i):
            rows = at(i, 512)
            value = dot(hidden_slope[rows, :], up_chunk[...], "NT")
            if j:
                value = value + grad[rows, :]
            grad[rows, :] = value

        loop(2, grad_ffn, 2)
        if j == 0:
            tick(2)

    settle()

    def load_strip(i):
        return pltpu.make_async_copy(
            resid.at[at(i, 128), :], strip.at[lax.rem(i, 2)], strip_sem.at[lax.rem(i, 2)]
        )

    load(mixed, 2)
    load(out_w, 4)
    load(queries, 3)
    load(keys, 5)
    load(values, 7)
    load_strip(0).start()
    gain = vec[5:6, :]
    branch = arena.at[0]

    def second_norm_back(i):
        @pl.when(i < 7)
        def _():
            load_strip(i + 1).start()

        load_strip(i).wait()
        rows = at(i, 128)
        normed, inverse = normed_rows(strip[lax.rem(i, 2)])
        incoming = grad[rows, :]
        sums[5:6, :] += jnp.sum(incoming * normed, 0, keepdims=True)
        sums[6:7, :] += jnp.sum(incoming, 0, keepdims=True)
        scaled = incoming * gain
        inner = (
            scaled
            - jnp.mean(scaled, -1, keepdims=True)
            - normed * jnp.mean(scaled * normed, -1, keepdims=True)
        )
        value = cot[rows, :].astype(F32) + inverse * inner
        grad[rows, :] = value
        branch[rows, :] = value.astype(BF)

    loop(8, second_norm_back)
    column_sums(cot, 7)
    column_sums(branch, 4)
    tick(6)
    load(query_w, 6)
    mix, out_full = ready(2), ready(4)
    grad_mixed = arena.at[1]

    def back_out(i):
        cols = at(i, 512)
        grad_mixed[:, cols] = dot(branch[...], out_full[cols, :], "NT").astype(BF)

    loop(2, back_out, 2)
    emit(parts[2], mix, branch)
    load(key_w, 4)
    query, key, value = ready(3), ready(5), ready(7)
    settle()
    load(attn_in, 0)

    def heads(first, count):
        def body(i, slope_now):
            attention_head_back(
                first + i,
                slope_now,
                off,
                (query, key, value, mix, grad_mixed),
                lse,
                mask,
                ramp,
                tilt,
                key_sum,
                value_sum,
            )
            return slope_now * 0.5

        lax.fori_loop(0, count, body, jnp.float32(LOG2E * 0.5 ** (first + 1)), unroll=2)

    heads(0, 2)
    tick(7)
    heads(2, 4)
    tick(8)
    heads(6, 2)
    load(value_w, 2)
    attn = ready(0)
    emit(parts[3], attn, query)
    settle()
    tick(9)
    emit(parts[4], attn, key)
    settle()
    tick(10)
    emit(parts[5], attn, value)
    settle()
    tick(11)
    load(tokens, 1)
    column_sums(query, 2)
    column_sums(value, 3)
    tick(12)
    query_full, key_full, value_full = ready(6), ready(4), ready(2)
    first_gain = vec[0:1, :]
    token_rows = ready(1)

    def first_norm_back(i):
        rows = at(i, 256)
        incoming = dot(query[rows, :], query_full[...], "NT")
        incoming = incoming + dot(key[rows, :], key_full[...], "NT")
        incoming = incoming + dot(value[rows, :], value_full[...], "NT")
        normed, inverse = normed_rows(token_rows[rows, :].astype(F32))
        sums[0:1, :] += jnp.sum(incoming * normed, 0, keepdims=True)
        sums[1:2, :] += jnp.sum(incoming, 0, keepdims=True)
        scaled = incoming * first_gain
        inner = (
            scaled
            - jnp.mean(scaled, -1, keepdims=True)
            - normed * jnp.mean(scaled * normed, -1, keepdims=True)
        )
        arena[1, rows, :] = (grad[rows, :] + inverse * inner).astype(BF)

    first_norm_back(0)
    first_norm_back(1)
    tick(13)
    first_norm_back(2)
    first_norm_back(3)
    result = pltpu.make_async_copy(arena.at[1], grad_tokens_out, slot_sem.at[1])
    result.start()
    for number in range(14, 19):
        tick(number)
    small_out[...] = small_total[4]
    result.wait()
    for task in tasks:
        task.finish()


def backward_all(length, vec, lse, arrays, shards):
    hbm, vmem = pl.BlockSpec(memory_space=pltpu.HBM), pl.BlockSpec(memory_space=pltpu.VMEM)
    groups = sum(SCATTER_CUTS)
    results = pl.pallas_call(
        backward_kernel,
        out_shape=[jax.ShapeDtypeStruct((1024, 1024), BF), jax.ShapeDtypeStruct((16, 1024), F32)]
        + [jax.ShapeDtypeStruct(s, F32) for s in shards]
        + [jax.ShapeDtypeStruct((4, 2, 2, 2) + s, BF) for s in shards[1:]],
        in_specs=[pl.BlockSpec(memory_space=pltpu.SMEM), vmem, vmem] + [hbm] * len(arrays),
        out_specs=[hbm, vmem] + [vmem] * 6 + [hbm] * 5,
        scratch_shapes=[pltpu.VMEM((4, 2, 2) + s, BF) for s in shards]
        + [pltpu.VMEM((3, 4) + s, BF) for s in shards]
        + [pltpu.VMEM((3,) + s, BF) for s in shards]
        + [
            pltpu.VMEM((2, 4, 2, 2, 128, 256), BF),
            pltpu.VMEM((4, 2, 2, 32, 1024), BF),
            pltpu.VMEM((3, 2, 2, 128, 256), BF),
            pltpu.VMEM((3, 128, 256), BF),
            pltpu.VMEM((8, 1024, 1024), BF),
            pltpu.VMEM((1024, 1024), F32),
            pltpu.VMEM((2, 2, 2, 2, 2, 32, 1024), BF),
            pltpu.VMEM((2, 128, 1024), F32),
            pltpu.VMEM((1024, 128), F32),
            pltpu.VMEM((1024, 128), F32),
            pltpu.VMEM((256, 256), F32),
            pltpu.VMEM((1024, 128), F32),
            pltpu.VMEM((1024, 128), F32),
            pltpu.VMEM((16, 1024), F32),
            pltpu.VMEM((5, 16, 1024), F32),
            pltpu.VMEM((6, 16, 1024), F32),
            pltpu.SemaphoreType.DMA((Summing.SEMS,)),
            pltpu.SemaphoreType.DMA((Summing.SEMS,)),
            pltpu.SemaphoreType.DMA((groups, Scattering.SEMS)),
            pltpu.SemaphoreType.DMA((groups, Scattering.SEMS)),
            pltpu.SemaphoreType.DMA((groups,)),
            pltpu.SemaphoreType.DMA((8,)),
            pltpu.SemaphoreType.DMA((2,)),
            pltpu.SemaphoreType.DMA((2,)),
        ],
        compiler_params=pltpu.CompilerParams(
            collective_id=3, has_side_effects=True, vmem_limit_bytes=62 << 20
        ),
    )(length, vec, lse, *arrays)
    return results[0], results[1], results[2:8]


def finish_kernel(small, *refs):
    arrays, outs, vectors = refs[:8], refs[8:16], refs[16:25]
    buffers, come, go = refs[25:33], refs[33], refs[34]
    inward = [
        pltpu.make_async_copy(source, buffer, come.at[i])
        for i, (source, buffer) in enumerate(zip(arrays, buffers))
    ]
    outward = [
        pltpu.make_async_copy(buffer, target, go.at[i])
        for i, (buffer, target) in enumerate(zip(buffers, outs))
    ]
    for copy in inward:
        copy.start()
    me = lax.axis_index("wide") * 4 + lax.axis_index("narrow")
    turned = pltpu.roll(small[...], lax.rem(1024 - me * 32, 1024), 1)
    for row in range(8):
        vectors[row][...] = turned[row, :32]
    line, block = 8 + lax.div(me, 8), lax.rem(me, 8)
    rows = lax.broadcasted_iota(jnp.int32, small.shape, 0)
    chosen = pltpu.roll(jnp.where(rows == line, small[...], 0.0), lax.rem(1024 - block * 128, 1024), 1)
    vectors[8][...] = jnp.sum(chosen[:, :128], 0)
    for first, second in zip(inward, outward):
        first.wait()
        second.start()
    for copy in outward:
        copy.wait()


def finish_all(small, arrays, sizes):
    hbm, vmem = pl.BlockSpec(memory_space=pltpu.HBM), pl.BlockSpec(memory_space=pltpu.VMEM)
    results = pl.pallas_call(
        finish_kernel,
        out_shape=[jax.ShapeDtypeStruct(a.shape, a.dtype) for a in arrays]
        + [jax.ShapeDtypeStruct((size,), F32) for size in sizes],
        in_specs=[vmem] + [hbm] * 8,
        out_specs=[hbm] * 8 + [vmem] * 9,
        scratch_shapes=[pltpu.VMEM(a.shape, a.dtype) for a in arrays]
        + [pltpu.SemaphoreType.DMA((8,)), pltpu.SemaphoreType.DMA((8,))],
    )(small, *arrays)
    return results[:8], results[8:]


def fused(tokens, cotangent, seq_length, parts):
    shards = [parts[i] for i in LARGE]
    (
        result, resid, lse, vec, down_part,
        attn_in, queries, keys, values, mixed, ffn_in, slope,
        *weights,
    ) = forward_all(seq_length, tokens, cotangent, [parts[i] for i in SMALL], shards)
    query_w, key_w, value_w, out_w, up_w, down_w = (
        w.reshape(-1, w.shape[-1]) for w in weights
    )
    down_part = down_part.reshape(weights[5].shape)
    order = (13, 11, 7, 2, 4, 5)
    grad_tokens, small, large = backward_all(
        seq_length,
        vec,
        lse,
        [tokens, cotangent, attn_in, queries, keys, values, mixed, ffn_in, slope, resid]
        + [query_w, key_w, value_w, out_w, up_w, down_w, down_part],
        [parts[i].shape for i in order],
    )
    (result, grad_tokens, *large), vectors = finish_all(
        small, [result, grad_tokens, *large], [parts[i].shape[0] for i in SMALL]
    )
    sums = [None] * 15
    for i, array in zip(order + SMALL, [*large, *vectors]):
        sums[i] = array
    return result, grad_tokens, sums


def is_fast():
    return lax.axis_size("wide") == 8 and lax.axis_size("narrow") == 4


def norm_forward(value, gain, shift):
    center = value - jnp.mean(value, -1, keepdims=True)
    inverse = lax.rsqrt(jnp.mean(center * center, -1, keepdims=True) + EPSILON)
    normed = center * inverse
    return (normed * gain.astype(jnp.float32) + shift.astype(jnp.float32), normed, inverse)


def norm_backward(incoming, normed, inverse, gain):
    scaled = incoming * gain.astype(jnp.float32)
    inner = (
        scaled
        - jnp.mean(scaled, -1, keepdims=True)
        - normed * jnp.mean(scaled * normed, -1, keepdims=True)
    )
    return (inverse * inner, jnp.sum(incoming * normed, 0), jnp.sum(incoming, 0))


def gelu_parts(hidden):
    cdf = 0.5 * (1.0 + lax.erf(hidden * 0.7071067811865476))
    density = jnp.exp(-0.5 * hidden * hidden) * 0.3989422804014327
    return (hidden * cdf, cdf + hidden * density)


def masked_scores(queries, keys, length):
    count = queries.shape[0]
    raw = jnp.einsum("qhd,khd->hqk", queries, keys, preferred_element_type=jnp.float32) * HD ** (
        -0.5
    )
    position = jnp.arange(count, dtype=jnp.int32)
    distance = (position[:, None] - position[None, :]).astype(jnp.float32)
    slopes = jnp.exp2(-8.0 * jnp.arange(1, H + 1, dtype=jnp.float32) / H)
    raw = raw - slopes[:, None, None] * distance[None]
    allowed = (position[:, None] >= position[None, :]) & (
        position[:, None] // length == position[None, :] // length
    )
    return jnp.where(allowed[None], raw, -1e30)


def forward(tokens, length, weights):
    (
        first_gain,
        first_shift,
        query_weight,
        query_bias,
        key_weight,
        value_weight,
        value_bias,
        out_weight,
        out_bias,
        second_gain,
        second_shift,
        up_weight,
        up_bias,
        down_weight,
        down_bias,
    ) = weights
    count = tokens.shape[0]
    width = tokens.shape[1]
    inputs = tokens.astype(jnp.float32)
    first_out, first_normed, first_inverse = norm_forward(inputs, first_gain, first_shift)
    attn_in = first_out.astype(jnp.bfloat16)
    queries = (
        (
            jnp.dot(attn_in, query_weight, preferred_element_type=jnp.float32)
            + query_bias.astype(jnp.float32)
        )
        .astype(jnp.bfloat16)
        .reshape(count, H, HD)
    )
    keys = (
        jnp.dot(attn_in, key_weight, preferred_element_type=jnp.float32)
        .astype(jnp.bfloat16)
        .reshape(count, H, HD)
    )
    values = (
        (
            jnp.dot(attn_in, value_weight, preferred_element_type=jnp.float32)
            + value_bias.astype(jnp.float32)
        )
        .astype(jnp.bfloat16)
        .reshape(count, H, HD)
    )
    scores = masked_scores(queries, keys, length)
    top = jnp.max(scores, -1, keepdims=True)
    expo = jnp.exp(scores - top)
    total = jnp.sum(expo, -1, keepdims=True)
    probs = expo / total
    log_total = top + jnp.log(total)
    mixed = jnp.einsum(
        "hqk,khd->qhd", probs.astype(jnp.bfloat16), values, preferred_element_type=jnp.float32
    )
    mixed = mixed.reshape(count, width).astype(jnp.bfloat16)
    resid = (
        inputs
        + jnp.dot(mixed, out_weight, preferred_element_type=jnp.float32)
        + out_bias.astype(jnp.float32)
    )
    second_out, second_normed, second_inverse = norm_forward(resid, second_gain, second_shift)
    ffn_in = second_out.astype(jnp.bfloat16)
    hidden = jnp.dot(ffn_in, up_weight, preferred_element_type=jnp.float32) + up_bias.astype(
        jnp.float32
    )
    active, active_slope = gelu_parts(hidden)
    active_low = active.astype(jnp.bfloat16)
    result = (
        resid
        + jnp.dot(active_low, down_weight, preferred_element_type=jnp.float32)
        + down_bias.astype(jnp.float32)
    )
    return (
        result.astype(jnp.bfloat16),
        attn_in,
        first_normed,
        first_inverse,
        queries,
        keys,
        values,
        log_total,
        mixed,
        second_normed,
        second_inverse,
        ffn_in,
        active_slope,
        active_low,
    )


def backward(cotangent, length, weights, kept):
    (
        first_gain,
        first_shift,
        query_weight,
        query_bias,
        key_weight,
        value_weight,
        value_bias,
        out_weight,
        out_bias,
        second_gain,
        second_shift,
        up_weight,
        up_bias,
        down_weight,
        down_bias,
    ) = weights
    (
        result,
        attn_in,
        first_normed,
        first_inverse,
        queries,
        keys,
        values,
        log_total,
        mixed,
        second_normed,
        second_inverse,
        ffn_in,
        active_slope,
        active_low,
    ) = kept
    count = cotangent.shape[0]
    width = cotangent.shape[1]
    grad_out = cotangent.astype(jnp.float32)
    grad_down_bias = jnp.sum(grad_out, 0)
    grad_down_weight = jnp.einsum(
        "tf,td->fd", active_low, cotangent, preferred_element_type=jnp.float32
    )
    grad_active = jnp.einsum(
        "td,fd->tf", cotangent, down_weight, preferred_element_type=jnp.float32
    )
    grad_hidden = (grad_active * active_slope).astype(jnp.bfloat16)
    grad_up_bias = jnp.sum(grad_hidden.astype(jnp.float32), 0)
    grad_up_weight = jnp.einsum(
        "td,tf->df", ffn_in, grad_hidden, preferred_element_type=jnp.float32
    )
    grad_ffn_in = jnp.einsum(
        "tf,df->td", grad_hidden, up_weight, preferred_element_type=jnp.float32
    )
    grad_second, grad_second_gain, grad_second_shift = norm_backward(
        grad_ffn_in, second_normed, second_inverse, second_gain
    )
    grad_resid = grad_out + grad_second
    grad_branch = grad_resid.astype(jnp.bfloat16)
    grad_out_bias = jnp.sum(grad_branch.astype(jnp.float32), 0)
    grad_out_weight = jnp.einsum(
        "tc,td->cd", mixed, grad_branch, preferred_element_type=jnp.float32
    )
    grad_mixed = jnp.einsum(
        "td,cd->tc", grad_branch, out_weight, preferred_element_type=jnp.float32
    )
    grad_mixed = grad_mixed.astype(jnp.bfloat16).reshape(count, H, HD)
    scores = masked_scores(queries, keys, length)
    probs = jnp.exp(scores - log_total)
    grad_probs = jnp.einsum("qhd,khd->hqk", grad_mixed, values, preferred_element_type=jnp.float32)
    grad_values = jnp.einsum(
        "hqk,qhd->khd", probs.astype(jnp.bfloat16), grad_mixed, preferred_element_type=jnp.float32
    )
    grad_values = grad_values.astype(jnp.bfloat16).reshape(count, width)
    row_total = jnp.sum(grad_probs * probs, -1, keepdims=True)
    grad_scores = (probs * (grad_probs - row_total)).astype(jnp.bfloat16)
    factor = HD ** (-0.5)
    grad_queries = (
        jnp.einsum("hqk,khd->qhd", grad_scores, keys, preferred_element_type=jnp.float32) * factor
    )
    grad_queries = grad_queries.astype(jnp.bfloat16).reshape(count, width)
    grad_keys = (
        jnp.einsum("hqk,qhd->khd", grad_scores, queries, preferred_element_type=jnp.float32)
        * factor
    )
    grad_keys = grad_keys.astype(jnp.bfloat16).reshape(count, width)
    grad_query_bias = jnp.sum(grad_queries.astype(jnp.float32), 0)
    grad_value_bias = jnp.sum(grad_values.astype(jnp.float32), 0)
    grad_query_weight = jnp.einsum(
        "tc,td->cd", attn_in, grad_queries, preferred_element_type=jnp.float32
    )
    grad_key_weight = jnp.einsum(
        "tc,td->cd", attn_in, grad_keys, preferred_element_type=jnp.float32
    )
    grad_value_weight = jnp.einsum(
        "tc,td->cd", attn_in, grad_values, preferred_element_type=jnp.float32
    )
    grad_attn = jnp.einsum(
        "td,cd->tc", grad_queries, query_weight, preferred_element_type=jnp.float32
    )
    grad_attn = grad_attn + jnp.einsum(
        "td,cd->tc", grad_keys, key_weight, preferred_element_type=jnp.float32
    )
    grad_attn = grad_attn + jnp.einsum(
        "td,cd->tc", grad_values, value_weight, preferred_element_type=jnp.float32
    )
    grad_first, grad_first_gain, grad_first_shift = norm_backward(
        grad_attn, first_normed, first_inverse, first_gain
    )
    grad_tokens = (grad_resid + grad_first).astype(jnp.bfloat16)
    sums = spread(
        (
            grad_first_gain,
            grad_first_shift,
            grad_query_weight,
            grad_query_bias,
            grad_key_weight,
            grad_value_weight,
            grad_value_bias,
            grad_out_weight,
            grad_out_bias,
            grad_second_gain,
            grad_second_shift,
            grad_up_weight,
            grad_up_bias,
            grad_down_weight,
            grad_down_bias,
        )
    )
    return (grad_tokens, sums)


def body(
    tokens,
    cotangent,
    seq_length,
    first_gain,
    first_shift,
    query_weight,
    query_bias,
    key_weight,
    value_weight,
    value_bias,
    out_weight,
    out_bias,
    second_gain,
    second_shift,
    up_weight,
    up_bias,
    down_weight,
    down_bias,
):
    shards = (
        first_gain,
        first_shift,
        query_weight,
        query_bias,
        key_weight,
        value_weight,
        value_bias,
        out_weight,
        out_bias,
        second_gain,
        second_shift,
        up_weight,
        up_bias,
        down_weight,
        down_bias,
    )
    if is_fast():
        result, grad_tokens, sums = fused(tokens, cotangent, seq_length, shards)
        return (result, grad_tokens, *sums)
    length = seq_length[0]
    weights = collect(shards)
    kept = forward(tokens, length, weights)
    grad_tokens, sums = backward(cotangent, length, weights, kept)
    (
        g_first_gain,
        g_first_shift,
        g_query_weight,
        g_query_bias,
        g_key_weight,
        g_value_weight,
        g_value_bias,
        g_out_weight,
        g_out_bias,
        g_second_gain,
        g_second_shift,
        g_up_weight,
        g_up_bias,
        g_down_weight,
        g_down_bias,
    ) = sums
    return (
        kept[0],
        grad_tokens,
        g_first_gain,
        g_first_shift,
        g_query_weight,
        g_query_bias,
        g_key_weight,
        g_value_weight,
        g_value_bias,
        g_out_weight,
        g_out_bias,
        g_second_gain,
        g_second_shift,
        g_up_weight,
        g_up_bias,
        g_down_weight,
        g_down_bias,
    )


def solution(mesh):
    placed = (
        P(("wide", "narrow"), None),
        P(("wide", "narrow"), None),
        P(("wide", "narrow")),
        P(("wide", "narrow")),
        P(("wide", "narrow")),
        P(("wide", "narrow"), None),
        P(("wide", "narrow")),
        P(("wide", "narrow"), None),
        P(("wide", "narrow"), None),
        P(("wide", "narrow")),
        P(("wide", "narrow"), None),
        P(("wide", "narrow")),
        P(("wide", "narrow")),
        P(("wide", "narrow")),
        P(("wide", "narrow"), None),
        P(("wide", "narrow")),
        P(("wide", "narrow"), None),
        P(("wide", "narrow")),
    )
    return jax.shard_map(
        body,
        mesh=mesh,
        in_specs=placed,
        out_specs=(
            P(("wide", "narrow"), None),
            P(("wide", "narrow"), None),
            P(("wide", "narrow")),
            P(("wide", "narrow")),
            P(("wide", "narrow"), None),
            P(("wide", "narrow")),
            P(("wide", "narrow"), None),
            P(("wide", "narrow"), None),
            P(("wide", "narrow")),
            P(("wide", "narrow"), None),
            P(("wide", "narrow")),
            P(("wide", "narrow")),
            P(("wide", "narrow")),
            P(("wide", "narrow"), None),
            P(("wide", "narrow")),
            P(("wide", "narrow"), None),
            P(("wide", "narrow")),
        ),
        check_vma=False,
    )
```

```python
import functools

import jax
import jax.numpy as jnp
from jax import lax
from jax.experimental import pallas as pl
from jax.experimental.pallas import tpu as pltpu
from jax.sharding import PartitionSpec as P

H = 8
HD = 128
AXES = ("wide", "narrow")
MESH = pl.DeviceIdType.MESH
BF = jnp.bfloat16
F32 = jnp.float32


class Place:
    def __init__(self):
        wide, narrow = lax.axis_index("wide"), lax.axis_index("narrow")
        self.z, self.x = lax.div(wide, 2), lax.rem(wide, 2)
        self.y, self.c = lax.div(narrow, 2), lax.rem(narrow, 2)
        c, x, y = self.c, self.x, self.y
        self.one = (x + (1 - c) * (1 - 2 * x), y + c * (1 - 2 * y))
        self.two = (x + c * (1 - 2 * x), y + (1 - c) * (1 - 2 * y))
        self.far = (1 - x, 1 - y)
        self.here = (x, y)

    def device(self, z, xy, c):
        return (z * 2 + xy[0], xy[1] * 2 + c)

    def up(self, step):
        return lax.rem(self.z + step, 4)

    def down(self, step):
        return lax.rem(self.z + 4 - step, 4)

    def partners(self):
        z, c = self.z, self.c
        return [self.device(self.up(step), self.here, c) for step in (1, 2, 3)] + [
            self.device(z, self.one, c),
            self.device(z, self.two, c),
            self.device(z, self.here, 1 - c),
        ]

    def greet(self):
        barrier = pltpu.get_barrier_semaphore()
        partners = self.partners()
        for partner in partners:
            pl.semaphore_signal(barrier, inc=1, device_id=partner, device_id_type=MESH)
        pl.semaphore_wait(barrier, len(partners))


def remote(source, target, send, recv, device):
    return pltpu.make_async_remote_copy(
        src_ref=source,
        dst_ref=target,
        send_sem=send,
        recv_sem=recv,
        device_id=device,
        device_id_type=MESH,
    )


class Gathering:
    SEMS = 10
    STAGES = 5

    def __init__(self, place, local, full, send, recv, keep):
        self.place, self.local, self.full = place, local, full
        self.send, self.recv, self.keep = send, recv, keep

    def block(self, xy, c):
        return self.full.at[:, xy[0], xy[1], c]

    def cell(self, z):
        place = self.place
        return self.full.at[z, place.x, place.y, place.c]

    def copy(self, source, target, sem, device):
        return remote(source, target, self.send.at[sem], self.recv.at[sem], device)

    def along(self, step):
        place = self.place
        device = place.device(place.up(step), place.here, place.c)
        return self.copy(self.local, self.cell(place.z), step - 1, device)

    def pieces(self):
        place = self.place
        z, c = place.z, place.c
        one, two = place.device(z, place.one, c), place.device(z, place.two, c)
        twin = place.device(z, place.here, 1 - c)
        mine, first = self.block(place.here, c), self.block(place.one, c)
        second, far = self.block(place.two, c), self.block(place.far, c)
        return {
            3: (mine, one, self.block(place.one, c)),
            4: (mine, two, self.block(place.two, c)),
            5: (mine, twin, self.block(place.here, 1 - c)),
            6: (first, two, self.block(place.far, c)),
            7: (first, twin, self.block(place.two, 1 - c)),
            8: (second, twin, self.block(place.one, 1 - c)),
            9: (far, twin, self.block(place.far, 1 - c)),
        }

    def start(self, sem):
        source, device, _ = self.pieces()[sem]
        self.copy(source, source, sem, device).start()

    def await_recv(self, sem):
        _, device, landing = self.pieces()[sem]
        self.copy(landing, landing, sem, device).wait_recv()

    def own(self):
        return pltpu.make_async_copy(self.local, self.cell(self.place.z), self.keep)

    def stage(self, number):
        place = self.place
        if number == 0:
            self.own().start()
            for step in (1, 2, 3):
                self.along(step).start()
        elif number == 1:
            self.own().wait()
            for step in (1, 2, 3):
                cell = self.cell(place.down(step))
                device = place.device(place.down(step), place.here, place.c)
                self.copy(cell, cell, step - 1, device).wait_recv()
            for sem in (3, 4, 5):
                self.start(sem)
        elif number == 2:
            self.await_recv(3)
            self.start(6)
            self.start(7)
            self.await_recv(4)
            self.start(8)
        elif number == 3:
            self.await_recv(6)
            self.start(9)
        elif number == 4:
            for sem in (5, 7, 8, 9):
                self.await_recv(sem)

    def finish(self):
        for step in (1, 2, 3):
            self.along(step).wait_send()
        for sem in range(3, 10):
            source, device, _ = self.pieces()[sem]
            self.copy(source, source, sem, device).wait_send()


class GatheringSides(Gathering):
    def cell_at(self, xy):
        return self.full.at[self.place.z, xy[0], xy[1], self.place.c]

    def layer(self, z, c):
        return self.full.at[z, :, :, c]

    def moves(self):
        place = self.place
        z, c = place.z, place.c
        one, two = place.device(z, place.one, c), place.device(z, place.two, c)
        twin = place.device(z, place.here, 1 - c)
        here, first, mine = self.cell_at(place.here), self.cell_at(place.one), self.layer(z, c)
        table = {
            0: (self.local, here, one, first),
            1: (self.local, here, two, self.cell_at(place.two)),
            2: (first, first, two, self.cell_at(place.far)),
            6: (mine, mine, twin, self.layer(z, 1 - c)),
        }
        for step in (1, 2, 3):
            other = place.down(step)
            block = self.layer(other, c)
            table[2 + step] = (mine, mine, place.device(place.up(step), place.here, c), block)
            table[6 + step] = (block, block, twin, self.layer(other, 1 - c))
        return table

    def start(self, sem):
        source, target, device, _ = self.moves()[sem]
        self.copy(source, target, sem, device).start()

    def await_recv(self, sem):
        _, _, device, landing = self.moves()[sem]
        self.copy(landing, landing, sem, device).wait_recv()

    def stage(self, number):
        if number == 0:
            self.own().start()
            self.start(0)
            self.start(1)
        elif number == 1:
            self.await_recv(0)
            self.start(2)
            self.await_recv(1)
            self.own().wait()
        elif number == 2:
            self.await_recv(2)
            for sem in (3, 4, 5, 6):
                self.start(sem)
        elif number == 3:
            for step in (1, 2, 3):
                self.await_recv(2 + step)
                self.start(6 + step)
        elif number == 4:
            for sem in (6, 7, 8, 9):
                self.await_recv(sem)

    def finish(self):
        for sem in range(10):
            source, target, device, _ = self.moves()[sem]
            self.copy(source, target, sem, device).wait_send()


class Scattering:
    SEMS = 7
    STAGES = 5

    def __init__(self, place, partial, mine, total, pair, line, out, send, recv, load):
        self.place, self.partial, self.mine = place, partial, mine
        self.total, self.pair, self.line, self.out = total, pair, line, out
        self.send, self.recv, self.load = send, recv, load

    def pieces(self):
        place = self.place
        z, c = place.z, place.c
        one, two = place.device(z, place.one, c), place.device(z, place.two, c)
        twin = place.device(z, place.here, 1 - c)
        total = self.total

        def block(xy):
            return total.at[:, xy[0], xy[1]]

        table = {
            0: (self.partial.at[:, :, :, 1 - c], total, twin),
            1: (block(place.two), self.pair.at[0], two),
            2: (block(place.far), self.pair.at[1], two),
            3: (block(place.one), self.pair.at[2], one),
        }
        for step in (1, 2, 3):
            device = place.device(place.up(step), place.here, c)
            table[3 + step] = (
                total.at[place.up(step), place.x, place.y],
                self.line.at[step - 1],
                device,
            )
        return table

    def copy(self, sem):
        source, target, device = self.pieces()[sem]
        return remote(source, target, self.send.at[sem], self.recv.at[sem], device)

    def own(self):
        return pltpu.make_async_copy(
            self.partial.at[:, :, :, self.place.c], self.mine, self.load
        )

    def join(self):
        total, mine = self.total, self.mine
        self.own().wait()
        self.copy(0).wait_recv()

        def body(z, carry):
            for x in range(2):
                for y in range(2):
                    total[z, x, y] = total[z, x, y] + mine[z, x, y]
            return carry

        lax.fori_loop(0, 4, body, 0)

    def stage(self, number):
        place, total, pair = self.place, self.total, self.pair

        def add(xy, slot):
            def body(z, carry):
                total[z, xy[0], xy[1]] = total[z, xy[0], xy[1]] + pair[slot, z]
                return carry

            lax.fori_loop(0, 4, body, 0)

        if number == 0:
            self.own().start()
            self.copy(0).start()
        elif number == 1:
            self.join()
            self.copy(2).start()
            self.copy(1).start()
        elif number == 2:
            self.copy(2).wait_recv()
            add(place.one, 1)
            self.copy(3).start()
            self.copy(1).wait_recv()
            add(place.here, 0)
        elif number == 3:
            self.copy(3).wait_recv()
            add(place.here, 2)
            for step in (1, 2, 3):
                self.copy(3 + step).start()
        elif number == 4:
            value = total[place.z, place.x, place.y].astype(F32)
            for step in (1, 2, 3):
                self.copy(3 + step).wait_recv()
                value = value + self.line[step - 1].astype(F32)
            self.out[...] = value

    def finish(self):
        for sem in range(7):
            self.copy(sem).wait_send()


class ScatteringSides(Scattering):
    def pieces(self):
        place, total = self.place, self.total
        z, c = place.z, place.c
        one, two = place.device(z, place.one, c), place.device(z, place.two, c)
        twin = place.device(z, place.here, 1 - c)

        def cell(xy):
            return total.at[z, xy[0], xy[1]]

        table = {
            0: (self.partial.at[:, :, :, 1 - c], total, twin),
            1: (cell(place.two), self.line.at[0], two),
            2: (cell(place.far), self.line.at[1], two),
            3: (cell(place.one), self.line.at[2], one),
        }
        for step in (1, 2, 3):
            device = place.device(place.up(step), place.here, c)
            table[3 + step] = (total.at[place.up(step)], self.pair.at[step - 1], device)
        return table

    def stage(self, number):
        place, total, pair, line = self.place, self.total, self.pair, self.line
        z = place.z

        def add(xy, slot):
            total[z, xy[0], xy[1]] = total[z, xy[0], xy[1]] + line[slot]

        if number == 0:
            self.own().start()
            self.copy(0).start()
        elif number == 1:
            self.join()
            for step in (1, 2, 3):
                self.copy(3 + step).start()
        elif number == 2:
            for step in (1, 2, 3):
                self.copy(3 + step).wait_recv()

            def body(x, carry):
                for y in range(2):
                    value = total[z, x, y].astype(F32)
                    for step in range(3):
                        value = value + pair[step, x, y].astype(F32)
                    total[z, x, y] = value.astype(BF)
                return carry

            lax.fori_loop(0, 2, body, 0)
            self.copy(2).start()
            self.copy(1).start()
        elif number == 3:
            self.copy(2).wait_recv()
            add(place.one, 1)
            self.copy(3).start()
            self.copy(1).wait_recv()
            add(place.here, 0)
        elif number == 4:
            self.copy(3).wait_recv()
            value = total[z, place.x, place.y].astype(F32) + line[2].astype(F32)
            self.out[...] = value


class Summing:
    SEMS = 6

    def __init__(self, place, value, total, slots, send, recv):
        self.place, self.value, self.total, self.slots = place, value, total, slots
        self.send, self.recv = send, recv

    def copy(self, sem):
        place = self.place
        device = [
            place.device(place.z, place.here, 1 - place.c),
            place.device(place.z, place.one, place.c),
            place.device(place.z, place.two, place.c),
        ] + [place.device(place.up(step), place.here, place.c) for step in (1, 2, 3)]
        source = self.total.at[min(sem, 3)]
        return remote(source, self.slots.at[sem], self.send.at[sem], self.recv.at[sem], device[sem])

    def stage(self, number):
        total, slots = self.total, self.slots
        if number == 0:
            total[0] = self.value[...]
            self.copy(0).start()
        elif number < 3:
            self.copy(number - 1).wait_recv()
            total[number] = total[number - 1] + slots[number - 1]
            self.copy(number).start()
        elif number == 3:
            self.copy(2).wait_recv()
            total[3] = total[2] + slots[2]
            for sem in (3, 4, 5):
                self.copy(sem).start()
        elif number == 4:
            value = total[3]
            for sem in (3, 4, 5):
                self.copy(sem).wait_recv()
                value = value + slots[sem]
            total[4] = value

    def finish(self):
        for sem in range(6):
            self.copy(sem).wait_send()


def run_tick(tasks, ticks, number, done=None):
    for stage in reversed(range(5)):
        for g, task in enumerate(tasks):
            if ticks[g][stage] == number:
                task.stage(stage)
                if stage == 4 and done is not None:
                    done(g)


def even(count, width):
    return [(i * width // count, width // count) for i in range(count)]


def columns(ref, piece):
    lead = (slice(None),) * (len(ref.shape) - 1)
    return ref.at[lead + (pl.ds(*piece),)]


DOWN_GATHER = ((0, 256), (256, 256), (512, 256), (768, 256))
DOWN_SCATTER = ((0, 256), (256, 256), (512, 256), (768, 256))


SMALL = (0, 1, 3, 6, 8, 9, 10, 14, 12)
LARGE = (2, 4, 5, 7, 11, 13)


EPSILON = 1e-05


def collect(parts):
    (
        first_gain,
        first_shift,
        query_weight,
        query_bias,
        key_weight,
        value_weight,
        value_bias,
        out_weight,
        out_bias,
        second_gain,
        second_shift,
        up_weight,
        up_bias,
        down_weight,
        down_bias,
    ) = parts
    return (
        lax.all_gather(first_gain, ("wide", "narrow"), axis=0, tiled=True),
        lax.all_gather(first_shift, ("wide", "narrow"), axis=0, tiled=True),
        lax.all_gather(query_weight, ("wide", "narrow"), axis=0, tiled=True),
        lax.all_gather(query_bias, ("wide", "narrow"), axis=0, tiled=True),
        lax.all_gather(key_weight, ("wide", "narrow"), axis=0, tiled=True),
        lax.all_gather(value_weight, ("wide", "narrow"), axis=0, tiled=True),
        lax.all_gather(value_bias, ("wide", "narrow"), axis=0, tiled=True),
        lax.all_gather(out_weight, ("wide", "narrow"), axis=0, tiled=True),
        lax.all_gather(out_bias, ("wide", "narrow"), axis=0, tiled=True),
        lax.all_gather(second_gain, ("wide", "narrow"), axis=0, tiled=True),
        lax.all_gather(second_shift, ("wide", "narrow"), axis=0, tiled=True),
        lax.all_gather(up_weight, ("wide", "narrow"), axis=0, tiled=True),
        lax.all_gather(up_bias, ("wide", "narrow"), axis=0, tiled=True),
        lax.all_gather(down_weight, ("wide", "narrow"), axis=0, tiled=True),
        lax.all_gather(down_bias, ("wide", "narrow"), axis=0, tiled=True),
    )


def spread(parts):
    (
        first_gain,
        first_shift,
        query_weight,
        query_bias,
        key_weight,
        value_weight,
        value_bias,
        out_weight,
        out_bias,
        second_gain,
        second_shift,
        up_weight,
        up_bias,
        down_weight,
        down_bias,
    ) = parts
    return (
        lax.psum_scatter(first_gain, ("wide", "narrow"), scatter_dimension=0, tiled=True),
        lax.psum_scatter(first_shift, ("wide", "narrow"), scatter_dimension=0, tiled=True),
        lax.psum_scatter(query_weight, ("wide", "narrow"), scatter_dimension=0, tiled=True),
        lax.psum_scatter(query_bias, ("wide", "narrow"), scatter_dimension=0, tiled=True),
        lax.psum_scatter(key_weight, ("wide", "narrow"), scatter_dimension=0, tiled=True),
        lax.psum_scatter(value_weight, ("wide", "narrow"), scatter_dimension=0, tiled=True),
        lax.psum_scatter(value_bias, ("wide", "narrow"), scatter_dimension=0, tiled=True),
        lax.psum_scatter(out_weight, ("wide", "narrow"), scatter_dimension=0, tiled=True),
        lax.psum_scatter(out_bias, ("wide", "narrow"), scatter_dimension=0, tiled=True),
        lax.psum_scatter(second_gain, ("wide", "narrow"), scatter_dimension=0, tiled=True),
        lax.psum_scatter(second_shift, ("wide", "narrow"), scatter_dimension=0, tiled=True),
        lax.psum_scatter(up_weight, ("wide", "narrow"), scatter_dimension=0, tiled=True),
        lax.psum_scatter(up_bias, ("wide", "narrow"), scatter_dimension=0, tiled=True),
        lax.psum_scatter(down_weight, ("wide", "narrow"), scatter_dimension=0, tiled=True),
        lax.psum_scatter(down_bias, ("wide", "narrow"), scatter_dimension=0, tiled=True),
    )


LOG2E = 1.4426950408889634
WEIGHTS = ("query", "key", "value", "out", "up", "down")


def dot(left, right, form):
    dims = (((0,) if form[0] == "T" else (1,), (1,) if form[1] == "T" else (0,)), ((), ()))
    return lax.dot_general(left, right, dims, preferred_element_type=F32)


def at(index, size):
    return pl.ds(pl.multiple_of(index * size, size), size)


def loop(count, body, unroll=1):
    def step(i, carry):
        body(i)
        return carry

    lax.fori_loop(0, count, step, 0, unroll=unroll)


def normed_rows(value):
    center = value - jnp.mean(value, -1, keepdims=True)
    inverse = lax.rsqrt(jnp.mean(center * center, -1, keepdims=True) + EPSILON)
    return center * inverse, inverse


def gelu_pair(hidden):
    cdf = 0.5 * (1.0 + lax.erf(hidden * 0.7071067811865476))
    density = jnp.exp2(hidden * hidden * (-0.5 * LOG2E)) * 0.3989422804014327
    return hidden * cdf, cdf + hidden * density


def pack_small(vectors, packed):
    packed[...] = jnp.zeros_like(packed)
    for row, vector in enumerate(vectors):
        size = vector.shape[0]
        packed[row : row + 1, :size] = vector[...].astype(F32).reshape(1, size)


def unpack_small(small, vec):
    table = small.reshape(512, 128)
    lane = lax.broadcasted_iota(jnp.int32, (128, 1024), 0)
    column = lax.broadcasted_iota(jnp.int32, (128, 1024), 1)
    pick = jnp.where(lane == lax.rem(column, 32), 1.0, 0.0).astype(BF)
    device = lax.broadcasted_iota(jnp.int32, (32, 16, 1024), 0)
    owner = lax.div(lax.broadcasted_iota(jnp.int32, (32, 16, 1024), 2), 32)
    spread_out = dot(table[...].astype(BF), pick, "NN").reshape(32, 16, 1024)
    vec[...] = jnp.sum(jnp.where(device == owner, spread_out, 0.0), 0)
    for part in range(4):
        for block in range(8):
            source = (part * 8 + block) * 16 + 8
            vec[8 + part : 9 + part, block * 128 : block * 128 + 128] = table[source : source + 1, :]


def prepare_bias(length, mask, ramp):
    key = lax.broadcasted_iota(jnp.int32, (256, 256), 0)
    query = lax.broadcasted_iota(jnp.int32, (256, 256), 1)
    long = length == 1024
    same = (lax.div(key, 128) == lax.div(query, 128)) | long
    mask[...] = jnp.where((key <= query) & same, 0.0, -1e30)
    ramp[...] = lax.broadcasted_iota(jnp.int32, (1024, 128), 0).astype(F32)
    return jnp.where(long, 0.0, -1e30)


def wide(value):
    return jnp.concatenate([value, value], axis=1)


def attention_head(head, slope, off, queries, keys, values, mixed, lse, mask, ramp, tilt):
    cols = at(head, 128)
    factor = HD**-0.5 * LOG2E
    tilt[...] = ramp[...] * slope
    for i in range(4):
        rows, before = slice(i * 256, i * 256 + 256), slice(0, i * 256)
        query = queries[rows, cols]
        near = dot(keys[rows, cols], query, "NT") * factor + wide(tilt[rows, :]) + mask[...]
        top = jnp.max(near, 0, keepdims=True)
        if i:
            past = dot(keys[before, cols], query, "NT") * factor + wide(tilt[before, :])
            top = jnp.maximum(top, jnp.max(past, 0, keepdims=True) + off)
        near = jnp.exp2(near - top)
        total = jnp.sum(near, 0, keepdims=True)
        out = dot(values[rows, cols], near.astype(BF), "TN")
        if i:
            past = jnp.exp2(past + (off - top))
            total = total + jnp.sum(past, 0, keepdims=True)
            out = out + dot(values[before, cols], past.astype(BF), "TN")
        mixed[rows, cols] = (out * (1.0 / total)).T.astype(BF)
        lse[pl.ds(head, 1), rows] = top + jnp.log2(total)


def forward_kernel(length_ref, tokens_in, cotangent_in, *refs):
    refs = list(refs)

    def take(count):
        taken, refs[:count] = refs[:count], []
        return taken

    vectors = take(9)
    local = take(6)
    result_out, resid_out, lse_out, small_out, down_out = take(5)
    attn_out, query_out, key_out, value_out, mixed_out, ffn_out, slope_out = take(7)
    weight_out = take(6)
    full = take(7)
    act, slope, mixed, ffn_in = take(4)
    resid, vec, lse, mask, ramp, tilt, stage = take(7)
    tokens, cotangent, packed = take(3)
    send, recv, keep, store, dump, stage_sem, input_sem = take(7)
    local = [packed] + local
    fetches = [
        pltpu.make_async_copy(source, target, input_sem.at[i])
        for i, (source, target) in enumerate(((tokens_in, tokens), (cotangent_in, cotangent)))
    ]
    for fetch in fetches:
        fetch.start()
    pack_small(vectors, packed)

    place = Place()
    place.greet()
    tasks, dumps = [], []
    cuts = [even(1, ref.shape[-1]) for ref in local[:5]] + [even(4, 4096), DOWN_GATHER]
    for i, pieces in enumerate(cuts):
        for piece in pieces:
            g = len(tasks)
            views = [columns(ref, piece) for ref in (local[i], full[i])]
            kind = GatheringSides if g > 12 else Gathering
            tasks.append(kind(place, *views, send.at[g], recv.at[g], keep.at[g]))
            if i:
                target = columns(weight_out[i - 1], piece)
                dumps.append(pltpu.make_async_copy(views[1], target, dump.at[g - 1]))

    ticks = [[0, 1, 2, 3, 4]] + [[g - 1 + stage for stage in range(5)] for g in range(1, 5)]
    ticks += [[g - 3, g - 1, g + 1, g + 2, g + 3] for g in range(5, 12)]
    ticks += [[9, 11, 13, 14, 15]]

    def done(g):
        if g:
            dumps[g - 1].start()

    def tick(number):
        run_tick(tasks, ticks, number, done)

    saves = []

    def save(source, target):
        copy = pltpu.make_async_copy(source, target, store.at[len(saves)])
        copy.start()
        saves.append(copy)

    query_w, key_w, value_w, out_w = (ref.reshape(1024, 1024) for ref in full[1:5])
    up_w, down_w = full[5].reshape(1024, 4096), full[6].reshape(4096, 1024)
    attn_in, queries, keys, values = (act.at[i] for i in range(4))
    length = length_ref[0]
    off = prepare_bias(length, mask, ramp)

    tick(0)
    tick(1)
    fetches[0].wait()

    def first_stats(i):
        rows = at(i, 128)
        normed, _ = normed_rows(tokens[rows, :].astype(F32))
        resid[rows, :] = normed

    loop(8, first_stats)
    for number in range(2, 5):
        tick(number)
    unpack_small(full[0], vec)

    def first_norm(i):
        rows = at(i, 128)
        attn_in[rows, :] = (resid[rows, :] * vec[0:1, :] + vec[1:2, :]).astype(BF)

    loop(8, first_norm)
    save(attn_in, attn_out)

    def project(weight, target, bias):
        def body(i):
            cols = at(i, 512)
            value = dot(attn_in[...], weight[:, cols], "NN")
            if bias is not None:
                value = value + vec[bias : bias + 1, cols]
            target[:, cols] = value.astype(BF)

        loop(2, body, 2)

    project(query_w, queries, 2)
    save(queries, query_out)
    tick(5)
    project(key_w, keys, None)
    save(keys, key_out)
    tick(6)
    project(value_w, values, 3)
    save(values, value_out)

    def heads(first):
        def body(i, slope_now):
            attention_head(
                first + i, slope_now, off, queries, keys, values, mixed, lse, mask, ramp, tilt
            )
            return slope_now * 0.5

        lax.fori_loop(0, 2, body, jnp.float32(LOG2E * 0.5 ** (first + 1)), unroll=2)

    heads(0)
    tick(7)
    heads(2)
    heads(4)
    tick(8)
    heads(6)
    save(mixed, mixed_out)
    save(lse, lse_out)

    def close_attention(i):
        rows = at(i, 256)
        value = dot(mixed[rows, :], out_w[...], "NN") + tokens[rows, :].astype(F32) + vec[4:5, :]
        resid[rows, :] = value
        normed, _ = normed_rows(value)
        ffn_in[rows, :] = (normed * vec[5:6, :] + vec[6:7, :]).astype(BF)

    loop(4, close_attention, 2)
    save(resid, resid_out)
    save(ffn_in, ffn_out)
    for copy in saves[:5]:
        copy.wait()

    def widen(chunk):
        def body(i):
            rows, cols = at(lax.div(i, 2), 512), at(lax.rem(i, 2), 512)
            weight = up_w[:, at(chunk * 2 + lax.rem(i, 2), 512)]
            hidden = dot(ffn_in[rows, :], weight, "NN") + vec[8 + chunk : 9 + chunk, cols]
            active, steep = gelu_pair(hidden)
            act[chunk, rows, cols] = active.astype(BF)
            slope[chunk % 2, rows, cols] = steep.astype(BF)

        if chunk > 1:
            saves[8 + chunk - 2].wait()
        loop(4, body, 2)
        save(slope.at[chunk % 2], slope_out.at[chunk])


    def spill(j, half):
        rows = pl.ds(pl.multiple_of(j * 1024 + half * 512, 512), 512)
        return pltpu.make_async_copy(stage.at[half], down_out.at[rows, :], stage_sem.at[half])

    def grad_down(j):
        for half in range(2):

            if j:
                spill(j - 1, half).wait()
            active = act[j, :, half * 512 : half * 512 + 512]
            stage[half] = dot(active, cotangent[...], "TN").astype(BF)
            spill(j, half).start()

    tick(9)
    widen(0)
    widen(1)
    fetches[1].wait()
    tick(10)
    widen(2)
    grad_down(0)
    tick(11)
    widen(3)
    grad_down(1)
    grad_down(2)

    def narrow(chunk):
        cols = slice(chunk * 256, chunk * 256 + 256)

        def body(i):
            rows = at(i, 512)
            value = resid[rows, cols] + vec[7:8, cols]
            active = jnp.concatenate([act[j, rows, :] for j in range(4)], axis=1)
            value = value + dot(active, down_w[:, cols], "NN")
            mixed[rows, cols] = value.astype(BF)

        loop(2, body, 2)

        save(mixed.at[:, cols], result_out.at[:, cols])

    tick(12)
    narrow(0)
    tick(13)
    narrow(1)
    grad_down(3)
    tick(14)
    narrow(2)
    tick(15)
    narrow(3)
    small_out[...] = vec[...]
    for half in range(2):
        spill(3, half).wait()
    for task in tasks:
        task.finish()
    for copy in saves[5:8] + saves[10:]:
        copy.wait()
    for copy in dumps:
        copy.wait()


def forward_all(length, tokens, cotangent, vectors, weights):
    square = jax.ShapeDtypeStruct((1024, 1024), BF)
    tall = jax.ShapeDtypeStruct((4, 1024, 1024), BF)
    f32 = functools.partial(jax.ShapeDtypeStruct, dtype=F32)
    grid6 = [(4, 2, 2, 2) + w.shape for w in weights]
    hbm, vmem = pl.BlockSpec(memory_space=pltpu.HBM), pl.BlockSpec(memory_space=pltpu.VMEM)
    return pl.pallas_call(
        forward_kernel,
        out_shape=[square, f32((1024, 1024)), f32((8, 1024)), f32((16, 1024))]
        + [jax.ShapeDtypeStruct((4096, 1024), BF)]
        + [square] * 6
        + [tall]
        + [jax.ShapeDtypeStruct(s, BF) for s in grid6],
        in_specs=[pl.BlockSpec(memory_space=pltpu.SMEM)] + [hbm] * 2 + [vmem] * 9 + [hbm] * 6,
        out_specs=[hbm, hbm, hbm, vmem] + [hbm] * 14,
        scratch_shapes=[pltpu.VMEM((4, 2, 2, 2, 16, 128), F32)]
        + [pltpu.VMEM(s, BF) for s in grid6]
        + [pltpu.VMEM((4, 1024, 1024), BF), pltpu.VMEM((2, 1024, 1024), BF)]
        + [pltpu.VMEM((1024, 1024), BF)] * 2
        + [
            pltpu.VMEM((1024, 1024), F32),
            pltpu.VMEM((16, 1024), F32),
            pltpu.VMEM((8, 1024), F32),
            pltpu.VMEM((256, 256), F32),
            pltpu.VMEM((1024, 128), F32),
            pltpu.VMEM((1024, 128), F32),
            pltpu.VMEM((2, 512, 1024), BF),
            pltpu.VMEM((1024, 1024), BF),
            pltpu.VMEM((1024, 1024), BF),
            pltpu.VMEM((16, 128), F32),
            pltpu.SemaphoreType.DMA((14, Gathering.SEMS)),
            pltpu.SemaphoreType.DMA((14, Gathering.SEMS)),
            pltpu.SemaphoreType.DMA((14,)),
            pltpu.SemaphoreType.DMA((20,)),
            pltpu.SemaphoreType.DMA((13,)),
            pltpu.SemaphoreType.DMA((2,)),
            pltpu.SemaphoreType.DMA((2,)),
        ],
        compiler_params=pltpu.CompilerParams(
            collective_id=2, has_side_effects=True, vmem_limit_bytes=62 << 20
        ),
    )(length, tokens, cotangent, *vectors, *weights)


SHARDS = ("down", "up", "out", "query", "key", "value")
SCATTER_CUTS = (4, 4, 1, 1, 1, 2)


def attention_head_back(head, slope, off, refs, lse, mask, ramp, tilt, key_sum, value_sum):
    queries, keys, values, mixed, grad_mixed = refs
    cols = at(head, 128)
    factor = HD**-0.5 * LOG2E
    tilt[...] = ramp[...] * slope
    for i in (3, 2, 1, 0):
        rows, upto, before = slice(i * 256, i * 256 + 256), slice(0, i * 256 + 256), i * 256
        query, grad = queries[rows, cols], grad_mixed[rows, cols]
        product = grad.astype(F32) * mixed[rows, cols].astype(F32)
        inner = jnp.sum(product.T, 0, keepdims=True)
        level = lse[pl.ds(head, 1), rows]
        raw = dot(keys[upto, cols], query, "NT") * factor + wide(tilt[upto, :])
        probs = jnp.exp2(raw[before:] + mask[...] - level)
        if i:
            probs = jnp.concatenate([jnp.exp2(raw[:before] + (off - level)), probs], axis=0)
        grad_probs = dot(values[upto, cols], grad, "NT")
        grad_scores = (probs * (grad_probs - inner)).astype(BF)
        value_part = dot(probs.astype(BF), grad, "NN")
        key_part = dot(grad_scores, query, "NN")
        if i == 3:
            value_sum[...] = value_part
            key_sum[...] = key_part
        else:
            value_sum[upto, :] += value_part
            key_sum[upto, :] += key_part
        query_part = dot(keys[upto, cols], grad_scores, "TN") * HD**-0.5
        queries[rows, cols] = query_part.T.astype(BF)
    keys[:, cols] = (key_sum[...] * HD**-0.5).astype(BF)
    values[:, cols] = value_sum[...].astype(BF)


def backward_kernel(length_ref, vec, lse, *refs):
    refs = list(refs)

    def take(count):
        taken, refs[:count] = refs[:count], []
        return taken

    tokens, cotangent, attn_in, queries, keys, values, mixed, ffn_in, slope, resid = take(10)
    query_w, key_w, value_w, out_w, up_w, down_w, down_part = take(7)
    grad_tokens_out, small_out = take(2)
    out = take(6)
    parts = [down_part] + take(5)
    total, pair, line = take(6), take(6), take(6)
    mine_down, mine, sides_pair, sides_line, arena, grad, stage, strip = take(8)
    key_sum, value_sum, mask, ramp, tilt, sums = take(6)
    small_total, small_slots, small_send, small_recv = take(4)
    send, recv, load_sem, slot_sem, stage_sem, strip_sem = take(6)

    place = Place()
    loads = {}

    def load(source, slot):
        copy = pltpu.make_async_copy(source, arena.at[slot], slot_sem.at[slot])
        copy.start()
        loads[slot] = copy

    def ready(slot):
        loads.pop(slot).wait()
        return arena.at[slot]

    def load_chunk(j):
        load(slope.at[j], j % 2)
        load(down_w.at[pl.ds(j * 1024, 1024), :], 2 + j % 2)
        load(up_w.at[:, pl.ds(j * 1024, 1024)], 4 + j % 2)

    load(cotangent, 6)
    load_chunk(0)
    load(ffn_in, 7)
    place.greet()

    tasks = []
    for i, cut in enumerate(SCATTER_CUTS):
        pieces = even(cut, parts[i].shape[-1]) if i else DOWN_SCATTER
        for piece in pieces:
            g = len(tasks)
            own = columns(mine if i else mine_down.at[(1, 0, 1, 0)[g]], (0, piece[1]))
            views = [columns(r, piece) for r in (parts[i], total[i], pair[i], line[i], out[i])]
            kind = ScatteringSides if g < 1 else Scattering
            if g < 1:
                room = ((0, 256), (256, 128))[g]
                views[2:4] = columns(sides_pair, room), columns(sides_line, room)
            tasks.append(
                kind(place, views[0], own, *views[1:], send.at[g], recv.at[g], load_sem.at[g])
            )
    tasks.append(Summing(place, sums, small_total, small_slots, small_send, small_recv))

    ticks = [[3, 4, 12, 14, 16]]
    ticks += [[b, b + 1, b + 3, b + 5, b + 7] for b in (0, 1, 2, 3, 4, 5, 6, 7)]
    ticks += [[9, 10, 12, 14, 16], [10, 11, 13, 15, 16]]
    ticks += [[11, 12, 14, 15, 16], [12, 13, 15, 16, 17], [14, 15, 16, 17, 18]]

    def tick(number):
        run_tick(tasks, ticks, number)

    stages = {}

    def emit(part, left, right, width=1024, first=0):
        copies = []
        for half in range(2):
            if half in stages:
                stages.pop(half).wait()
            value = dot(left[:, half * 512 : half * 512 + 512], right[...], "TN")
            stage[half] = value.astype(BF).reshape(2, 2, 2, 2, 32, 1024)
            target = part.at[half * 2 : half * 2 + 2, :, :, :, :, pl.ds(first, width)]
            copy = pltpu.make_async_copy(stage.at[half], target, stage_sem.at[half])
            copy.start()
            stages[half] = copy
            copies.append(copy)

    def settle():
        for half in list(stages):
            stages.pop(half).wait()

    ones = jnp.ones((8, 1024), BF)

    def column_sums(source, row):
        def body(i):
            cols = at(i, 256)
            sums[row : row + 1, cols] = dot(ones, source[:, cols], "NN")[0:1]

        loop(4, body)

    length = length_ref[0]
    off = prepare_bias(length, mask, ramp)
    sums[...] = jnp.zeros_like(sums)
    tick(0)
    cot = ready(6)
    up_part = parts[1]

    for j in range(4):
        if j < 3:
            load_chunk(j + 1)
        hidden_slope, down_chunk, up_chunk = ready(j % 2), ready(2 + j % 2), ready(4 + j % 2)
        if j == 0:
            ffn = ready(7)

        def grad_hidden(i):
            cols = at(i, 512)
            value = dot(cot[...], down_chunk[cols, :], "NT") * hidden_slope[:, cols].astype(F32)
            hidden_slope[:, cols] = value.astype(BF)

        loop(2, grad_hidden, 2)
        column_sums(hidden_slope, 8 + j)
        if j == 0:
            tick(1)
        emit(up_part, ffn, hidden_slope, 1024, j * 1024)
        if j:
            tick(j + 2)

        def grad_ffn(i):
            rows = at(i, 512)
            value = dot(hidden_slope[rows, :], up_chunk[...], "NT")
            if j:
                value = value + grad[rows, :]
            grad[rows, :] = value

        loop(2, grad_ffn, 2)
        if j == 0:
            tick(2)

    settle()

    def load_strip(i):
        return pltpu.make_async_copy(
            resid.at[at(i, 128), :], strip.at[lax.rem(i, 2)], strip_sem.at[lax.rem(i, 2)]
        )

    load(mixed, 2)
    load(out_w, 4)
    load(queries, 3)
    load(keys, 5)
    load(values, 7)
    load_strip(0).start()
    gain = vec[5:6, :]
    branch = arena.at[0]

    def second_norm_back(i):
        @pl.when(i < 7)
        def _():
            load_strip(i + 1).start()

        load_strip(i).wait()
        rows = at(i, 128)
        normed, inverse = normed_rows(strip[lax.rem(i, 2)])
        incoming = grad[rows, :]
        sums[5:6, :] += jnp.sum(incoming * normed, 0, keepdims=True)
        sums[6:7, :] += jnp.sum(incoming, 0, keepdims=True)
        scaled = incoming * gain
        inner = (
            scaled
            - jnp.mean(scaled, -1, keepdims=True)
            - normed * jnp.mean(scaled * normed, -1, keepdims=True)
        )
        value = cot[rows, :].astype(F32) + inverse * inner
        grad[rows, :] = value
        branch[rows, :] = value.astype(BF)

    loop(8, second_norm_back)
    column_sums(cot, 7)
    column_sums(branch, 4)
    tick(6)
    load(query_w, 6)
    mix, out_full = ready(2), ready(4)
    grad_mixed = arena.at[1]

    def back_out(i):
        cols = at(i, 512)
        grad_mixed[:, cols] = dot(branch[...], out_full[cols, :], "NT").astype(BF)

    loop(2, back_out, 2)
    emit(parts[2], mix, branch)
    load(key_w, 4)
    query, key, value = ready(3), ready(5), ready(7)
    settle()
    load(attn_in, 0)

    def heads(first, count):
        def body(i, slope_now):
            attention_head_back(
                first + i,
                slope_now,
                off,
                (query, key, value, mix, grad_mixed),
                lse,
                mask,
                ramp,
                tilt,
                key_sum,
                value_sum,
            )
            return slope_now * 0.5

        lax.fori_loop(0, count, body, jnp.float32(LOG2E * 0.5 ** (first + 1)), unroll=2)

    heads(0, 2)
    tick(7)
    heads(2, 4)
    tick(8)
    heads(6, 2)
    load(value_w, 2)
    attn = ready(0)
    emit(parts[3], attn, query)
    settle()
    tick(9)
    emit(parts[4], attn, key)
    settle()
    tick(10)
    emit(parts[5], attn, value)
    settle()
    tick(11)
    load(tokens, 1)
    column_sums(query, 2)
    column_sums(value, 3)
    tick(12)
    query_full, key_full, value_full = ready(6), ready(4), ready(2)
    first_gain = vec[0:1, :]
    token_rows = ready(1)

    def first_norm_back(i):
        rows = at(i, 256)
        incoming = dot(query[rows, :], query_full[...], "NT")
        incoming = incoming + dot(key[rows, :], key_full[...], "NT")
        incoming = incoming + dot(value[rows, :], value_full[...], "NT")
        normed, inverse = normed_rows(token_rows[rows, :].astype(F32))
        sums[0:1, :] += jnp.sum(incoming * normed, 0, keepdims=True)
        sums[1:2, :] += jnp.sum(incoming, 0, keepdims=True)
        scaled = incoming * first_gain
        inner = (
            scaled
            - jnp.mean(scaled, -1, keepdims=True)
            - normed * jnp.mean(scaled * normed, -1, keepdims=True)
        )
        arena[1, rows, :] = (grad[rows, :] + inverse * inner).astype(BF)

    first_norm_back(0)
    first_norm_back(1)
    tick(13)
    first_norm_back(2)
    first_norm_back(3)
    result = pltpu.make_async_copy(arena.at[1], grad_tokens_out, slot_sem.at[1])
    result.start()
    for number in range(14, 19):
        tick(number)
    small_out[...] = small_total[4]
    result.wait()
    for task in tasks:
        task.finish()


def backward_all(length, vec, lse, arrays, shards):
    hbm, vmem = pl.BlockSpec(memory_space=pltpu.HBM), pl.BlockSpec(memory_space=pltpu.VMEM)
    groups = sum(SCATTER_CUTS)
    results = pl.pallas_call(
        backward_kernel,
        out_shape=[jax.ShapeDtypeStruct((1024, 1024), BF), jax.ShapeDtypeStruct((16, 1024), F32)]
        + [jax.ShapeDtypeStruct(s, F32) for s in shards]
        + [jax.ShapeDtypeStruct((4, 2, 2, 2) + s, BF) for s in shards[1:]],
        in_specs=[pl.BlockSpec(memory_space=pltpu.SMEM), vmem, vmem] + [hbm] * len(arrays),
        out_specs=[hbm, vmem] + [vmem] * 6 + [hbm] * 5,
        scratch_shapes=[pltpu.VMEM((4, 2, 2) + s, BF) for s in shards]
        + [pltpu.VMEM((3, 4) + s, BF) for s in shards]
        + [pltpu.VMEM((3,) + s, BF) for s in shards]
        + [
            pltpu.VMEM((2, 4, 2, 2, 128, 256), BF),
            pltpu.VMEM((4, 2, 2, 32, 1024), BF),
            pltpu.VMEM((3, 2, 2, 128, 384), BF),
            pltpu.VMEM((3, 128, 384), BF),
            pltpu.VMEM((8, 1024, 1024), BF),
            pltpu.VMEM((1024, 1024), F32),
            pltpu.VMEM((2, 2, 2, 2, 2, 32, 1024), BF),
            pltpu.VMEM((2, 128, 1024), F32),
            pltpu.VMEM((1024, 128), F32),
            pltpu.VMEM((1024, 128), F32),
            pltpu.VMEM((256, 256), F32),
            pltpu.VMEM((1024, 128), F32),
            pltpu.VMEM((1024, 128), F32),
            pltpu.VMEM((16, 1024), F32),
            pltpu.VMEM((5, 16, 1024), F32),
            pltpu.VMEM((6, 16, 1024), F32),
            pltpu.SemaphoreType.DMA((Summing.SEMS,)),
            pltpu.SemaphoreType.DMA((Summing.SEMS,)),
            pltpu.SemaphoreType.DMA((groups, Scattering.SEMS)),
            pltpu.SemaphoreType.DMA((groups, Scattering.SEMS)),
            pltpu.SemaphoreType.DMA((groups,)),
            pltpu.SemaphoreType.DMA((8,)),
            pltpu.SemaphoreType.DMA((2,)),
            pltpu.SemaphoreType.DMA((2,)),
        ],
        compiler_params=pltpu.CompilerParams(
            collective_id=3, has_side_effects=True, vmem_limit_bytes=62 << 20
        ),
    )(length, vec, lse, *arrays)
    return results[0], results[1], results[2:8]


def finish_kernel(small, *refs):
    arrays, outs, vectors = refs[:8], refs[8:16], refs[16:25]
    buffers, come, go = refs[25:33], refs[33], refs[34]
    inward = [
        pltpu.make_async_copy(source, buffer, come.at[i])
        for i, (source, buffer) in enumerate(zip(arrays, buffers))
    ]
    outward = [
        pltpu.make_async_copy(buffer, target, go.at[i])
        for i, (buffer, target) in enumerate(zip(buffers, outs))
    ]
    for copy in inward:
        copy.start()
    me = lax.axis_index("wide") * 4 + lax.axis_index("narrow")
    turned = pltpu.roll(small[...], lax.rem(1024 - me * 32, 1024), 1)
    for row in range(8):
        vectors[row][...] = turned[row, :32]
    line, block = 8 + lax.div(me, 8), lax.rem(me, 8)
    rows = lax.broadcasted_iota(jnp.int32, small.shape, 0)
    chosen = pltpu.roll(jnp.where(rows == line, small[...], 0.0), lax.rem(1024 - block * 128, 1024), 1)
    vectors[8][...] = jnp.sum(chosen[:, :128], 0)
    for first, second in zip(inward, outward):
        first.wait()
        second.start()
    for copy in outward:
        copy.wait()


def finish_all(small, arrays, sizes):
    hbm, vmem = pl.BlockSpec(memory_space=pltpu.HBM), pl.BlockSpec(memory_space=pltpu.VMEM)
    results = pl.pallas_call(
        finish_kernel,
        out_shape=[jax.ShapeDtypeStruct(a.shape, a.dtype) for a in arrays]
        + [jax.ShapeDtypeStruct((size,), F32) for size in sizes],
        in_specs=[vmem] + [hbm] * 8,
        out_specs=[hbm] * 8 + [vmem] * 9,
        scratch_shapes=[pltpu.VMEM(a.shape, a.dtype) for a in arrays]
        + [pltpu.SemaphoreType.DMA((8,)), pltpu.SemaphoreType.DMA((8,))],
    )(small, *arrays)
    return results[:8], results[8:]


def fused(tokens, cotangent, seq_length, parts):
    shards = [parts[i] for i in LARGE]
    (
        result, resid, lse, vec, down_part,
        attn_in, queries, keys, values, mixed, ffn_in, slope,
        *weights,
    ) = forward_all(seq_length, tokens, cotangent, [parts[i] for i in SMALL], shards)
    query_w, key_w, value_w, out_w, up_w, down_w = (
        w.reshape(-1, w.shape[-1]) for w in weights
    )
    down_part = down_part.reshape(weights[5].shape)
    order = (13, 11, 7, 2, 4, 5)
    grad_tokens, small, large = backward_all(
        seq_length,
        vec,
        lse,
        [tokens, cotangent, attn_in, queries, keys, values, mixed, ffn_in, slope, resid]
        + [query_w, key_w, value_w, out_w, up_w, down_w, down_part],
        [parts[i].shape for i in order],
    )
    (result, grad_tokens, *large), vectors = finish_all(
        small, [result, grad_tokens, *large], [parts[i].shape[0] for i in SMALL]
    )
    sums = [None] * 15
    for i, array in zip(order + SMALL, [*large, *vectors]):
        sums[i] = array
    return result, grad_tokens, sums


def is_fast():
    return lax.axis_size("wide") == 8 and lax.axis_size("narrow") == 4


def norm_forward(value, gain, shift):
    center = value - jnp.mean(value, -1, keepdims=True)
    inverse = lax.rsqrt(jnp.mean(center * center, -1, keepdims=True) + EPSILON)
    normed = center * inverse
    return (normed * gain.astype(jnp.float32) + shift.astype(jnp.float32), normed, inverse)


def norm_backward(incoming, normed, inverse, gain):
    scaled = incoming * gain.astype(jnp.float32)
    inner = (
        scaled
        - jnp.mean(scaled, -1, keepdims=True)
        - normed * jnp.mean(scaled * normed, -1, keepdims=True)
    )
    return (inverse * inner, jnp.sum(incoming * normed, 0), jnp.sum(incoming, 0))


def gelu_parts(hidden):
    cdf = 0.5 * (1.0 + lax.erf(hidden * 0.7071067811865476))
    density = jnp.exp(-0.5 * hidden * hidden) * 0.3989422804014327
    return (hidden * cdf, cdf + hidden * density)


def masked_scores(queries, keys, length):
    count = queries.shape[0]
    raw = jnp.einsum("qhd,khd->hqk", queries, keys, preferred_element_type=jnp.float32) * HD ** (
        -0.5
    )
    position = jnp.arange(count, dtype=jnp.int32)
    distance = (position[:, None] - position[None, :]).astype(jnp.float32)
    slopes = jnp.exp2(-8.0 * jnp.arange(1, H + 1, dtype=jnp.float32) / H)
    raw = raw - slopes[:, None, None] * distance[None]
    allowed = (position[:, None] >= position[None, :]) & (
        position[:, None] // length == position[None, :] // length
    )
    return jnp.where(allowed[None], raw, -1e30)


def forward(tokens, length, weights):
    (
        first_gain,
        first_shift,
        query_weight,
        query_bias,
        key_weight,
        value_weight,
        value_bias,
        out_weight,
        out_bias,
        second_gain,
        second_shift,
        up_weight,
        up_bias,
        down_weight,
        down_bias,
    ) = weights
    count = tokens.shape[0]
    width = tokens.shape[1]
    inputs = tokens.astype(jnp.float32)
    first_out, first_normed, first_inverse = norm_forward(inputs, first_gain, first_shift)
    attn_in = first_out.astype(jnp.bfloat16)
    queries = (
        (
            jnp.dot(attn_in, query_weight, preferred_element_type=jnp.float32)
            + query_bias.astype(jnp.float32)
        )
        .astype(jnp.bfloat16)
        .reshape(count, H, HD)
    )
    keys = (
        jnp.dot(attn_in, key_weight, preferred_element_type=jnp.float32)
        .astype(jnp.bfloat16)
        .reshape(count, H, HD)
    )
    values = (
        (
            jnp.dot(attn_in, value_weight, preferred_element_type=jnp.float32)
            + value_bias.astype(jnp.float32)
        )
        .astype(jnp.bfloat16)
        .reshape(count, H, HD)
    )
    scores = masked_scores(queries, keys, length)
    top = jnp.max(scores, -1, keepdims=True)
    expo = jnp.exp(scores - top)
    total = jnp.sum(expo, -1, keepdims=True)
    probs = expo / total
    log_total = top + jnp.log(total)
    mixed = jnp.einsum(
        "hqk,khd->qhd", probs.astype(jnp.bfloat16), values, preferred_element_type=jnp.float32
    )
    mixed = mixed.reshape(count, width).astype(jnp.bfloat16)
    resid = (
        inputs
        + jnp.dot(mixed, out_weight, preferred_element_type=jnp.float32)
        + out_bias.astype(jnp.float32)
    )
    second_out, second_normed, second_inverse = norm_forward(resid, second_gain, second_shift)
    ffn_in = second_out.astype(jnp.bfloat16)
    hidden = jnp.dot(ffn_in, up_weight, preferred_element_type=jnp.float32) + up_bias.astype(
        jnp.float32
    )
    active, active_slope = gelu_parts(hidden)
    active_low = active.astype(jnp.bfloat16)
    result = (
        resid
        + jnp.dot(active_low, down_weight, preferred_element_type=jnp.float32)
        + down_bias.astype(jnp.float32)
    )
    return (
        result.astype(jnp.bfloat16),
        attn_in,
        first_normed,
        first_inverse,
        queries,
        keys,
        values,
        log_total,
        mixed,
        second_normed,
        second_inverse,
        ffn_in,
        active_slope,
        active_low,
    )


def backward(cotangent, length, weights, kept):
    (
        first_gain,
        first_shift,
        query_weight,
        query_bias,
        key_weight,
        value_weight,
        value_bias,
        out_weight,
        out_bias,
        second_gain,
        second_shift,
        up_weight,
        up_bias,
        down_weight,
        down_bias,
    ) = weights
    (
        result,
        attn_in,
        first_normed,
        first_inverse,
        queries,
        keys,
        values,
        log_total,
        mixed,
        second_normed,
        second_inverse,
        ffn_in,
        active_slope,
        active_low,
    ) = kept
    count = cotangent.shape[0]
    width = cotangent.shape[1]
    grad_out = cotangent.astype(jnp.float32)
    grad_down_bias = jnp.sum(grad_out, 0)
    grad_down_weight = jnp.einsum(
        "tf,td->fd", active_low, cotangent, preferred_element_type=jnp.float32
    )
    grad_active = jnp.einsum(
        "td,fd->tf", cotangent, down_weight, preferred_element_type=jnp.float32
    )
    grad_hidden = (grad_active * active_slope).astype(jnp.bfloat16)
    grad_up_bias = jnp.sum(grad_hidden.astype(jnp.float32), 0)
    grad_up_weight = jnp.einsum(
        "td,tf->df", ffn_in, grad_hidden, preferred_element_type=jnp.float32
    )
    grad_ffn_in = jnp.einsum(
        "tf,df->td", grad_hidden, up_weight, preferred_element_type=jnp.float32
    )
    grad_second, grad_second_gain, grad_second_shift = norm_backward(
        grad_ffn_in, second_normed, second_inverse, second_gain
    )
    grad_resid = grad_out + grad_second
    grad_branch = grad_resid.astype(jnp.bfloat16)
    grad_out_bias = jnp.sum(grad_branch.astype(jnp.float32), 0)
    grad_out_weight = jnp.einsum(
        "tc,td->cd", mixed, grad_branch, preferred_element_type=jnp.float32
    )
    grad_mixed = jnp.einsum(
        "td,cd->tc", grad_branch, out_weight, preferred_element_type=jnp.float32
    )
    grad_mixed = grad_mixed.astype(jnp.bfloat16).reshape(count, H, HD)
    scores = masked_scores(queries, keys, length)
    probs = jnp.exp(scores - log_total)
    grad_probs = jnp.einsum("qhd,khd->hqk", grad_mixed, values, preferred_element_type=jnp.float32)
    grad_values = jnp.einsum(
        "hqk,qhd->khd", probs.astype(jnp.bfloat16), grad_mixed, preferred_element_type=jnp.float32
    )
    grad_values = grad_values.astype(jnp.bfloat16).reshape(count, width)
    row_total = jnp.sum(grad_probs * probs, -1, keepdims=True)
    grad_scores = (probs * (grad_probs - row_total)).astype(jnp.bfloat16)
    factor = HD ** (-0.5)
    grad_queries = (
        jnp.einsum("hqk,khd->qhd", grad_scores, keys, preferred_element_type=jnp.float32) * factor
    )
    grad_queries = grad_queries.astype(jnp.bfloat16).reshape(count, width)
    grad_keys = (
        jnp.einsum("hqk,qhd->khd", grad_scores, queries, preferred_element_type=jnp.float32)
        * factor
    )
    grad_keys = grad_keys.astype(jnp.bfloat16).reshape(count, width)
    grad_query_bias = jnp.sum(grad_queries.astype(jnp.float32), 0)
    grad_value_bias = jnp.sum(grad_values.astype(jnp.float32), 0)
    grad_query_weight = jnp.einsum(
        "tc,td->cd", attn_in, grad_queries, preferred_element_type=jnp.float32
    )
    grad_key_weight = jnp.einsum(
        "tc,td->cd", attn_in, grad_keys, preferred_element_type=jnp.float32
    )
    grad_value_weight = jnp.einsum(
        "tc,td->cd", attn_in, grad_values, preferred_element_type=jnp.float32
    )
    grad_attn = jnp.einsum(
        "td,cd->tc", grad_queries, query_weight, preferred_element_type=jnp.float32
    )
    grad_attn = grad_attn + jnp.einsum(
        "td,cd->tc", grad_keys, key_weight, preferred_element_type=jnp.float32
    )
    grad_attn = grad_attn + jnp.einsum(
        "td,cd->tc", grad_values, value_weight, preferred_element_type=jnp.float32
    )
    grad_first, grad_first_gain, grad_first_shift = norm_backward(
        grad_attn, first_normed, first_inverse, first_gain
    )
    grad_tokens = (grad_resid + grad_first).astype(jnp.bfloat16)
    sums = spread(
        (
            grad_first_gain,
            grad_first_shift,
            grad_query_weight,
            grad_query_bias,
            grad_key_weight,
            grad_value_weight,
            grad_value_bias,
            grad_out_weight,
            grad_out_bias,
            grad_second_gain,
            grad_second_shift,
            grad_up_weight,
            grad_up_bias,
            grad_down_weight,
            grad_down_bias,
        )
    )
    return (grad_tokens, sums)


def body(
    tokens,
    cotangent,
    seq_length,
    first_gain,
    first_shift,
    query_weight,
    query_bias,
    key_weight,
    value_weight,
    value_bias,
    out_weight,
    out_bias,
    second_gain,
    second_shift,
    up_weight,
    up_bias,
    down_weight,
    down_bias,
):
    shards = (
        first_gain,
        first_shift,
        query_weight,
        query_bias,
        key_weight,
        value_weight,
        value_bias,
        out_weight,
        out_bias,
        second_gain,
        second_shift,
        up_weight,
        up_bias,
        down_weight,
        down_bias,
    )
    if is_fast():
        result, grad_tokens, sums = fused(tokens, cotangent, seq_length, shards)
        return (result, grad_tokens, *sums)
    length = seq_length[0]
    weights = collect(shards)
    kept = forward(tokens, length, weights)
    grad_tokens, sums = backward(cotangent, length, weights, kept)
    (
        g_first_gain,
        g_first_shift,
        g_query_weight,
        g_query_bias,
        g_key_weight,
        g_value_weight,
        g_value_bias,
        g_out_weight,
        g_out_bias,
        g_second_gain,
        g_second_shift,
        g_up_weight,
        g_up_bias,
        g_down_weight,
        g_down_bias,
    ) = sums
    return (
        kept[0],
        grad_tokens,
        g_first_gain,
        g_first_shift,
        g_query_weight,
        g_query_bias,
        g_key_weight,
        g_value_weight,
        g_value_bias,
        g_out_weight,
        g_out_bias,
        g_second_gain,
        g_second_shift,
        g_up_weight,
        g_up_bias,
        g_down_weight,
        g_down_bias,
    )


def solution(mesh):
    placed = (
        P(("wide", "narrow"), None),
        P(("wide", "narrow"), None),
        P(("wide", "narrow")),
        P(("wide", "narrow")),
        P(("wide", "narrow")),
        P(("wide", "narrow"), None),
        P(("wide", "narrow")),
        P(("wide", "narrow"), None),
        P(("wide", "narrow"), None),
        P(("wide", "narrow")),
        P(("wide", "narrow"), None),
        P(("wide", "narrow")),
        P(("wide", "narrow")),
        P(("wide", "narrow")),
        P(("wide", "narrow"), None),
        P(("wide", "narrow")),
        P(("wide", "narrow"), None),
        P(("wide", "narrow")),
    )
    return jax.shard_map(
        body,
        mesh=mesh,
        in_specs=placed,
        out_specs=(
            P(("wide", "narrow"), None),
            P(("wide", "narrow"), None),
            P(("wide", "narrow")),
            P(("wide", "narrow")),
            P(("wide", "narrow"), None),
            P(("wide", "narrow")),
            P(("wide", "narrow"), None),
            P(("wide", "narrow"), None),
            P(("wide", "narrow")),
            P(("wide", "narrow"), None),
            P(("wide", "narrow")),
            P(("wide", "narrow")),
            P(("wide", "narrow")),
            P(("wide", "narrow"), None),
            P(("wide", "narrow")),
            P(("wide", "narrow"), None),
            P(("wide", "narrow")),
        ),
        check_vma=False,
    )
```

```python
import functools

import jax
import jax.numpy as jnp
from jax import lax
from jax.experimental import pallas as pl
from jax.experimental.pallas import tpu as pltpu
from jax.sharding import PartitionSpec as P

H = 8
HD = 128
AXES = ("wide", "narrow")
MESH = pl.DeviceIdType.MESH
BF = jnp.bfloat16
F32 = jnp.float32


class Place:
    def __init__(self):
        wide, narrow = lax.axis_index("wide"), lax.axis_index("narrow")
        self.z, self.x = lax.div(wide, 2), lax.rem(wide, 2)
        self.y, self.c = lax.div(narrow, 2), lax.rem(narrow, 2)
        c, x, y = self.c, self.x, self.y
        self.one = (x + (1 - c) * (1 - 2 * x), y + c * (1 - 2 * y))
        self.two = (x + c * (1 - 2 * x), y + (1 - c) * (1 - 2 * y))
        self.far = (1 - x, 1 - y)
        self.here = (x, y)

    def device(self, z, xy, c):
        return (z * 2 + xy[0], xy[1] * 2 + c)

    def up(self, step):
        return lax.rem(self.z + step, 4)

    def down(self, step):
        return lax.rem(self.z + 4 - step, 4)

    def partners(self):
        z, c = self.z, self.c
        return [self.device(self.up(step), self.here, c) for step in (1, 2, 3)] + [
            self.device(z, self.one, c),
            self.device(z, self.two, c),
            self.device(z, self.here, 1 - c),
        ]

    def greet(self):
        barrier = pltpu.get_barrier_semaphore()
        partners = self.partners()
        for partner in partners:
            pl.semaphore_signal(barrier, inc=1, device_id=partner, device_id_type=MESH)
        pl.semaphore_wait(barrier, len(partners))


def remote(source, target, send, recv, device):
    return pltpu.make_async_remote_copy(
        src_ref=source,
        dst_ref=target,
        send_sem=send,
        recv_sem=recv,
        device_id=device,
        device_id_type=MESH,
    )


class Gathering:
    SEMS = 10
    STAGES = 5

    def __init__(self, place, local, full, send, recv, keep):
        self.place, self.local, self.full = place, local, full
        self.send, self.recv, self.keep = send, recv, keep

    def block(self, xy, c):
        return self.full.at[:, xy[0], xy[1], c]

    def cell(self, z):
        place = self.place
        return self.full.at[z, place.x, place.y, place.c]

    def copy(self, source, target, sem, device):
        return remote(source, target, self.send.at[sem], self.recv.at[sem], device)

    def along(self, step):
        place = self.place
        device = place.device(place.up(step), place.here, place.c)
        return self.copy(self.local, self.cell(place.z), step - 1, device)

    def pieces(self):
        place = self.place
        z, c = place.z, place.c
        one, two = place.device(z, place.one, c), place.device(z, place.two, c)
        twin = place.device(z, place.here, 1 - c)
        mine, first = self.block(place.here, c), self.block(place.one, c)
        second, far = self.block(place.two, c), self.block(place.far, c)
        return {
            3: (mine, one, self.block(place.one, c)),
            4: (mine, two, self.block(place.two, c)),
            5: (mine, twin, self.block(place.here, 1 - c)),
            6: (first, two, self.block(place.far, c)),
            7: (first, twin, self.block(place.two, 1 - c)),
            8: (second, twin, self.block(place.one, 1 - c)),
            9: (far, twin, self.block(place.far, 1 - c)),
        }

    def start(self, sem):
        source, device, _ = self.pieces()[sem]
        self.copy(source, source, sem, device).start()

    def await_recv(self, sem):
        _, device, landing = self.pieces()[sem]
        self.copy(landing, landing, sem, device).wait_recv()

    def own(self):
        return pltpu.make_async_copy(self.local, self.cell(self.place.z), self.keep)

    def stage(self, number):
        place = self.place
        if number == 0:
            self.own().start()
            for step in (1, 2, 3):
                self.along(step).start()
        elif number == 1:
            self.own().wait()
            for step in (1, 2, 3):
                cell = self.cell(place.down(step))
                device = place.device(place.down(step), place.here, place.c)
                self.copy(cell, cell, step - 1, device).wait_recv()
            for sem in (3, 4, 5):
                self.start(sem)
        elif number == 2:
            self.await_recv(3)
            self.start(6)
            self.start(7)
            self.await_recv(4)
            self.start(8)
        elif number == 3:
            self.await_recv(6)
            self.start(9)
        elif number == 4:
            for sem in (5, 7, 8, 9):
                self.await_recv(sem)

    def finish(self):
        for step in (1, 2, 3):
            self.along(step).wait_send()
        for sem in range(3, 10):
            source, device, _ = self.pieces()[sem]
            self.copy(source, source, sem, device).wait_send()


class GatheringSides(Gathering):
    def cell_at(self, xy):
        return self.full.at[self.place.z, xy[0], xy[1], self.place.c]

    def layer(self, z, c):
        return self.full.at[z, :, :, c]

    def moves(self):
        place = self.place
        z, c = place.z, place.c
        one, two = place.device(z, place.one, c), place.device(z, place.two, c)
        twin = place.device(z, place.here, 1 - c)
        here, first, mine = self.cell_at(place.here), self.cell_at(place.one), self.layer(z, c)
        table = {
            0: (self.local, here, one, first),
            1: (self.local, here, two, self.cell_at(place.two)),
            2: (first, first, two, self.cell_at(place.far)),
            6: (mine, mine, twin, self.layer(z, 1 - c)),
        }
        for step in (1, 2, 3):
            other = place.down(step)
            block = self.layer(other, c)
            table[2 + step] = (mine, mine, place.device(place.up(step), place.here, c), block)
            table[6 + step] = (block, block, twin, self.layer(other, 1 - c))
        return table

    def start(self, sem):
        source, target, device, _ = self.moves()[sem]
        self.copy(source, target, sem, device).start()

    def await_recv(self, sem):
        _, _, device, landing = self.moves()[sem]
        self.copy(landing, landing, sem, device).wait_recv()

    def stage(self, number):
        if number == 0:
            self.own().start()
            self.start(0)
            self.start(1)
        elif number == 1:
            self.await_recv(0)
            self.start(2)
            self.await_recv(1)
            self.own().wait()
        elif number == 2:
            self.await_recv(2)
            for sem in (3, 4, 5, 6):
                self.start(sem)
        elif number == 3:
            for step in (1, 2, 3):
                self.await_recv(2 + step)
                self.start(6 + step)
        elif number == 4:
            for sem in (6, 7, 8, 9):
                self.await_recv(sem)

    def finish(self):
        for sem in range(10):
            source, target, device, _ = self.moves()[sem]
            self.copy(source, target, sem, device).wait_send()


class Scattering:
    SEMS = 7
    STAGES = 5

    def __init__(self, place, partial, mine, total, pair, line, out, send, recv, load):
        self.place, self.partial, self.mine = place, partial, mine
        self.total, self.pair, self.line, self.out = total, pair, line, out
        self.send, self.recv, self.load = send, recv, load

    def pieces(self):
        place = self.place
        z, c = place.z, place.c
        one, two = place.device(z, place.one, c), place.device(z, place.two, c)
        twin = place.device(z, place.here, 1 - c)
        total = self.total

        def block(xy):
            return total.at[:, xy[0], xy[1]]

        table = {
            0: (self.partial.at[:, :, :, 1 - c], total, twin),
            1: (block(place.two), self.pair.at[0], two),
            2: (block(place.far), self.pair.at[1], two),
            3: (block(place.one), self.pair.at[2], one),
        }
        for step in (1, 2, 3):
            device = place.device(place.up(step), place.here, c)
            table[3 + step] = (
                total.at[place.up(step), place.x, place.y],
                self.line.at[step - 1],
                device,
            )
        return table

    def copy(self, sem):
        source, target, device = self.pieces()[sem]
        return remote(source, target, self.send.at[sem], self.recv.at[sem], device)

    def own(self):
        return pltpu.make_async_copy(
            self.partial.at[:, :, :, self.place.c], self.mine, self.load
        )

    def join(self):
        total, mine = self.total, self.mine
        self.own().wait()
        self.copy(0).wait_recv()

        def body(z, carry):
            for x in range(2):
                for y in range(2):
                    total[z, x, y] = total[z, x, y] + mine[z, x, y]
            return carry

        lax.fori_loop(0, 4, body, 0)

    def stage(self, number):
        place, total, pair = self.place, self.total, self.pair

        def add(xy, slot):
            def body(z, carry):
                total[z, xy[0], xy[1]] = total[z, xy[0], xy[1]] + pair[slot, z]
                return carry

            lax.fori_loop(0, 4, body, 0)

        if number == 0:
            self.own().start()
            self.copy(0).start()
        elif number == 1:
            self.join()
            self.copy(2).start()
            self.copy(1).start()
        elif number == 2:
            self.copy(2).wait_recv()
            add(place.one, 1)
            self.copy(3).start()
            self.copy(1).wait_recv()
            add(place.here, 0)
        elif number == 3:
            self.copy(3).wait_recv()
            add(place.here, 2)
            for step in (1, 2, 3):
                self.copy(3 + step).start()
        elif number == 4:
            value = total[place.z, place.x, place.y].astype(F32)
            for step in (1, 2, 3):
                self.copy(3 + step).wait_recv()
                value = value + self.line[step - 1].astype(F32)
            self.out[...] = value

    def finish(self):
        for sem in range(7):
            self.copy(sem).wait_send()


class ScatteringSides(Scattering):
    def pieces(self):
        place, total = self.place, self.total
        z, c = place.z, place.c
        one, two = place.device(z, place.one, c), place.device(z, place.two, c)
        twin = place.device(z, place.here, 1 - c)

        def cell(xy):
            return total.at[z, xy[0], xy[1]]

        table = {
            0: (self.partial.at[:, :, :, 1 - c], total, twin),
            1: (cell(place.two), self.line.at[0], two),
            2: (cell(place.far), self.line.at[1], two),
            3: (cell(place.one), self.line.at[2], one),
        }
        for step in (1, 2, 3):
            device = place.device(place.up(step), place.here, c)
            table[3 + step] = (total.at[place.up(step)], self.pair.at[step - 1], device)
        return table

    def stage(self, number):
        place, total, pair, line = self.place, self.total, self.pair, self.line
        z = place.z

        def add(xy, slot):
            total[z, xy[0], xy[1]] = total[z, xy[0], xy[1]] + line[slot]

        if number == 0:
            self.own().start()
            self.copy(0).start()
        elif number == 1:
            self.join()
            for step in (1, 2, 3):
                self.copy(3 + step).start()
        elif number == 2:
            for step in (1, 2, 3):
                self.copy(3 + step).wait_recv()

            def body(x, carry):
                for y in range(2):
                    value = total[z, x, y].astype(F32)
                    for step in range(3):
                        value = value + pair[step, x, y].astype(F32)
                    total[z, x, y] = value.astype(BF)
                return carry

            lax.fori_loop(0, 2, body, 0)
            self.copy(2).start()
            self.copy(1).start()
        elif number == 3:
            self.copy(2).wait_recv()
            add(place.one, 1)
            self.copy(3).start()
            self.copy(1).wait_recv()
            add(place.here, 0)
        elif number == 4:
            self.copy(3).wait_recv()
            value = total[z, place.x, place.y].astype(F32) + line[2].astype(F32)
            self.out[...] = value


class Summing:
    SEMS = 6

    def __init__(self, place, value, total, slots, send, recv):
        self.place, self.value, self.total, self.slots = place, value, total, slots
        self.send, self.recv = send, recv

    def copy(self, sem):
        place = self.place
        device = [
            place.device(place.z, place.here, 1 - place.c),
            place.device(place.z, place.one, place.c),
            place.device(place.z, place.two, place.c),
        ] + [place.device(place.up(step), place.here, place.c) for step in (1, 2, 3)]
        source = self.total.at[min(sem, 3)]
        return remote(source, self.slots.at[sem], self.send.at[sem], self.recv.at[sem], device[sem])

    def stage(self, number):
        total, slots = self.total, self.slots
        if number == 0:
            total[0] = self.value[...]
            self.copy(0).start()
        elif number < 3:
            self.copy(number - 1).wait_recv()
            total[number] = total[number - 1] + slots[number - 1]
            self.copy(number).start()
        elif number == 3:
            self.copy(2).wait_recv()
            total[3] = total[2] + slots[2]
            for sem in (3, 4, 5):
                self.copy(sem).start()
        elif number == 4:
            value = total[3]
            for sem in (3, 4, 5):
                self.copy(sem).wait_recv()
                value = value + slots[sem]
            total[4] = value

    def finish(self):
        for sem in range(6):
            self.copy(sem).wait_send()


def run_tick(tasks, ticks, number, done=None):
    for stage in reversed(range(5)):
        for g, task in enumerate(tasks):
            if ticks[g][stage] == number:
                task.stage(stage)
                if stage == 4 and done is not None:
                    done(g)


def even(count, width):
    return [(i * width // count, width // count) for i in range(count)]


def columns(ref, piece):
    lead = (slice(None),) * (len(ref.shape) - 1)
    return ref.at[lead + (pl.ds(*piece),)]


DOWN_GATHER = ((0, 256), (256, 256), (512, 256), (768, 256))
DOWN_SCATTER = ((0, 256), (256, 256), (512, 256), (768, 256))


SMALL = (0, 1, 3, 6, 8, 9, 10, 14, 12)
LARGE = (2, 4, 5, 7, 11, 13)


EPSILON = 1e-05


def collect(parts):
    (
        first_gain,
        first_shift,
        query_weight,
        query_bias,
        key_weight,
        value_weight,
        value_bias,
        out_weight,
        out_bias,
        second_gain,
        second_shift,
        up_weight,
        up_bias,
        down_weight,
        down_bias,
    ) = parts
    return (
        lax.all_gather(first_gain, ("wide", "narrow"), axis=0, tiled=True),
        lax.all_gather(first_shift, ("wide", "narrow"), axis=0, tiled=True),
        lax.all_gather(query_weight, ("wide", "narrow"), axis=0, tiled=True),
        lax.all_gather(query_bias, ("wide", "narrow"), axis=0, tiled=True),
        lax.all_gather(key_weight, ("wide", "narrow"), axis=0, tiled=True),
        lax.all_gather(value_weight, ("wide", "narrow"), axis=0, tiled=True),
        lax.all_gather(value_bias, ("wide", "narrow"), axis=0, tiled=True),
        lax.all_gather(out_weight, ("wide", "narrow"), axis=0, tiled=True),
        lax.all_gather(out_bias, ("wide", "narrow"), axis=0, tiled=True),
        lax.all_gather(second_gain, ("wide", "narrow"), axis=0, tiled=True),
        lax.all_gather(second_shift, ("wide", "narrow"), axis=0, tiled=True),
        lax.all_gather(up_weight, ("wide", "narrow"), axis=0, tiled=True),
        lax.all_gather(up_bias, ("wide", "narrow"), axis=0, tiled=True),
        lax.all_gather(down_weight, ("wide", "narrow"), axis=0, tiled=True),
        lax.all_gather(down_bias, ("wide", "narrow"), axis=0, tiled=True),
    )


def spread(parts):
    (
        first_gain,
        first_shift,
        query_weight,
        query_bias,
        key_weight,
        value_weight,
        value_bias,
        out_weight,
        out_bias,
        second_gain,
        second_shift,
        up_weight,
        up_bias,
        down_weight,
        down_bias,
    ) = parts
    return (
        lax.psum_scatter(first_gain, ("wide", "narrow"), scatter_dimension=0, tiled=True),
        lax.psum_scatter(first_shift, ("wide", "narrow"), scatter_dimension=0, tiled=True),
        lax.psum_scatter(query_weight, ("wide", "narrow"), scatter_dimension=0, tiled=True),
        lax.psum_scatter(query_bias, ("wide", "narrow"), scatter_dimension=0, tiled=True),
        lax.psum_scatter(key_weight, ("wide", "narrow"), scatter_dimension=0, tiled=True),
        lax.psum_scatter(value_weight, ("wide", "narrow"), scatter_dimension=0, tiled=True),
        lax.psum_scatter(value_bias, ("wide", "narrow"), scatter_dimension=0, tiled=True),
        lax.psum_scatter(out_weight, ("wide", "narrow"), scatter_dimension=0, tiled=True),
        lax.psum_scatter(out_bias, ("wide", "narrow"), scatter_dimension=0, tiled=True),
        lax.psum_scatter(second_gain, ("wide", "narrow"), scatter_dimension=0, tiled=True),
        lax.psum_scatter(second_shift, ("wide", "narrow"), scatter_dimension=0, tiled=True),
        lax.psum_scatter(up_weight, ("wide", "narrow"), scatter_dimension=0, tiled=True),
        lax.psum_scatter(up_bias, ("wide", "narrow"), scatter_dimension=0, tiled=True),
        lax.psum_scatter(down_weight, ("wide", "narrow"), scatter_dimension=0, tiled=True),
        lax.psum_scatter(down_bias, ("wide", "narrow"), scatter_dimension=0, tiled=True),
    )


LOG2E = 1.4426950408889634
WEIGHTS = ("query", "key", "value", "out", "up", "down")


def dot(left, right, form):
    dims = (((0,) if form[0] == "T" else (1,), (1,) if form[1] == "T" else (0,)), ((), ()))
    return lax.dot_general(left, right, dims, preferred_element_type=F32)


def at(index, size):
    return pl.ds(pl.multiple_of(index * size, size), size)


def loop(count, body, unroll=1):
    def step(i, carry):
        body(i)
        return carry

    lax.fori_loop(0, count, step, 0, unroll=unroll)


def normed_rows(value):
    center = value - jnp.mean(value, -1, keepdims=True)
    inverse = lax.rsqrt(jnp.mean(center * center, -1, keepdims=True) + EPSILON)
    return center * inverse, inverse


def gelu_pair(hidden):
    cdf = 0.5 * (1.0 + lax.erf(hidden * 0.7071067811865476))
    density = jnp.exp2(hidden * hidden * (-0.5 * LOG2E)) * 0.3989422804014327
    return hidden * cdf, cdf + hidden * density


def pack_small(vectors, packed):
    packed[...] = jnp.zeros_like(packed)
    for row, vector in enumerate(vectors):
        size = vector.shape[0]
        packed[row : row + 1, :size] = vector[...].astype(F32).reshape(1, size)


def unpack_small(small, vec):
    table = small.reshape(512, 128)
    lane = lax.broadcasted_iota(jnp.int32, (128, 1024), 0)
    column = lax.broadcasted_iota(jnp.int32, (128, 1024), 1)
    pick = jnp.where(lane == lax.rem(column, 32), 1.0, 0.0).astype(BF)
    device = lax.broadcasted_iota(jnp.int32, (32, 16, 1024), 0)
    owner = lax.div(lax.broadcasted_iota(jnp.int32, (32, 16, 1024), 2), 32)
    spread_out = dot(table[...].astype(BF), pick, "NN").reshape(32, 16, 1024)
    vec[...] = jnp.sum(jnp.where(device == owner, spread_out, 0.0), 0)
    for part in range(4):
        for block in range(8):
            source = (part * 8 + block) * 16 + 8
            vec[8 + part : 9 + part, block * 128 : block * 128 + 128] = table[source : source + 1, :]


def prepare_bias(length, mask, ramp):
    key = lax.broadcasted_iota(jnp.int32, (256, 256), 0)
    query = lax.broadcasted_iota(jnp.int32, (256, 256), 1)
    long = length == 1024
    same = (lax.div(key, 128) == lax.div(query, 128)) | long
    mask[...] = jnp.where((key <= query) & same, 0.0, -1e30)
    ramp[...] = lax.broadcasted_iota(jnp.int32, (1024, 128), 0).astype(F32)
    return jnp.where(long, 0.0, -1e30)


def wide(value):
    return jnp.concatenate([value, value], axis=1)


def attention_head(head, slope, off, queries, keys, values, mixed, lse, mask, ramp, tilt):
    cols = at(head, 128)
    factor = HD**-0.5 * LOG2E
    tilt[...] = ramp[...] * slope
    for i in range(4):
        rows, before = slice(i * 256, i * 256 + 256), slice(0, i * 256)
        query = queries[rows, cols]
        near = dot(keys[rows, cols], query, "NT") * factor + wide(tilt[rows, :]) + mask[...]
        top = jnp.max(near, 0, keepdims=True)
        if i:
            past = dot(keys[before, cols], query, "NT") * factor + wide(tilt[before, :])
            top = jnp.maximum(top, jnp.max(past, 0, keepdims=True) + off)
        near = jnp.exp2(near - top)
        total = jnp.sum(near, 0, keepdims=True)
        out = dot(values[rows, cols], near.astype(BF), "TN")
        if i:
            past = jnp.exp2(past + (off - top))
            total = total + jnp.sum(past, 0, keepdims=True)
            out = out + dot(values[before, cols], past.astype(BF), "TN")
        mixed[rows, cols] = (out * (1.0 / total)).T.astype(BF)
        lse[pl.ds(head, 1), rows] = top + jnp.log2(total)


def forward_kernel(length_ref, tokens_in, cotangent_in, *refs):
    refs = list(refs)

    def take(count):
        taken, refs[:count] = refs[:count], []
        return taken

    vectors = take(9)
    local = take(6)
    result_out, resid_out, lse_out, small_out, down_out = take(5)
    attn_out, query_out, key_out, value_out, mixed_out, ffn_out, slope_out = take(7)
    weight_out = take(6)
    full = take(7)
    act, slope, mixed, ffn_in = take(4)
    resid, vec, lse, mask, ramp, tilt, stage = take(7)
    tokens, cotangent, packed = take(3)
    send, recv, keep, store, dump, stage_sem, input_sem = take(7)
    local = [packed] + local
    fetches = [
        pltpu.make_async_copy(source, target, input_sem.at[i])
        for i, (source, target) in enumerate(((tokens_in, tokens), (cotangent_in, cotangent)))
    ]
    for fetch in fetches:
        fetch.start()
    pack_small(vectors, packed)

    place = Place()
    place.greet()
    tasks, dumps = [], []
    cuts = [even(1, ref.shape[-1]) for ref in local[:5]] + [even(4, 4096), DOWN_GATHER]
    for i, pieces in enumerate(cuts):
        for piece in pieces:
            g = len(tasks)
            views = [columns(ref, piece) for ref in (local[i], full[i])]
            kind = GatheringSides if g > 12 else Gathering
            tasks.append(kind(place, *views, send.at[g], recv.at[g], keep.at[g]))
            if i:
                target = columns(weight_out[i - 1], piece)
                dumps.append(pltpu.make_async_copy(views[1], target, dump.at[g - 1]))

    ticks = [[0, 1, 2, 3, 4]] + [[g - 1 + stage for stage in range(5)] for g in range(1, 5)]
    ticks += [[g - 2, g - 1, g + 1, g + 2, g + 3] for g in range(5, 12)]
    ticks += [[10, 11, 13, 14, 15]]

    def done(g):
        if g:
            dumps[g - 1].start()

    def tick(number):
        run_tick(tasks, ticks, number, done)

    saves = []

    def save(source, target):
        copy = pltpu.make_async_copy(source, target, store.at[len(saves)])
        copy.start()
        saves.append(copy)

    query_w, key_w, value_w, out_w = (ref.reshape(1024, 1024) for ref in full[1:5])
    up_w, down_w = full[5].reshape(1024, 4096), full[6].reshape(4096, 1024)
    attn_in, queries, keys, values = (act.at[i] for i in range(4))
    length = length_ref[0]
    off = prepare_bias(length, mask, ramp)

    tick(0)
    tick(1)
    fetches[0].wait()

    def first_stats(i):
        rows = at(i, 128)
        normed, _ = normed_rows(tokens[rows, :].astype(F32))
        resid[rows, :] = normed

    loop(8, first_stats)
    for number in range(2, 5):
        tick(number)
    unpack_small(full[0], vec)

    def first_norm(i):
        rows = at(i, 128)
        attn_in[rows, :] = (resid[rows, :] * vec[0:1, :] + vec[1:2, :]).astype(BF)

    loop(8, first_norm)
    save(attn_in, attn_out)

    def project(weight, target, bias):
        def body(i):
            cols = at(i, 512)
            value = dot(attn_in[...], weight[:, cols], "NN")
            if bias is not None:
                value = value + vec[bias : bias + 1, cols]
            target[:, cols] = value.astype(BF)

        loop(2, body, 2)

    project(query_w, queries, 2)
    save(queries, query_out)
    tick(5)
    project(key_w, keys, None)
    save(keys, key_out)
    tick(6)
    project(value_w, values, 3)
    save(values, value_out)

    def heads(first):
        def body(i, slope_now):
            attention_head(
                first + i, slope_now, off, queries, keys, values, mixed, lse, mask, ramp, tilt
            )
            return slope_now * 0.5

        lax.fori_loop(0, 2, body, jnp.float32(LOG2E * 0.5 ** (first + 1)), unroll=2)

    heads(0)
    tick(7)
    heads(2)
    heads(4)
    tick(8)
    heads(6)
    save(mixed, mixed_out)
    save(lse, lse_out)

    def close_attention(i):
        rows = at(i, 256)
        value = dot(mixed[rows, :], out_w[...], "NN") + tokens[rows, :].astype(F32) + vec[4:5, :]
        resid[rows, :] = value
        normed, _ = normed_rows(value)
        ffn_in[rows, :] = (normed * vec[5:6, :] + vec[6:7, :]).astype(BF)

    loop(4, close_attention, 2)
    save(resid, resid_out)
    save(ffn_in, ffn_out)
    for copy in saves[:5]:
        copy.wait()

    def widen(chunk):
        def body(i):
            rows, cols = at(lax.div(i, 2), 512), at(lax.rem(i, 2), 512)
            weight = up_w[:, at(chunk * 2 + lax.rem(i, 2), 512)]
            hidden = dot(ffn_in[rows, :], weight, "NN") + vec[8 + chunk : 9 + chunk, cols]
            active, steep = gelu_pair(hidden)
            act[chunk, rows, cols] = active.astype(BF)
            slope[chunk % 2, rows, cols] = steep.astype(BF)

        if chunk > 1:
            saves[8 + chunk - 2].wait()
        loop(4, body, 2)
        save(slope.at[chunk % 2], slope_out.at[chunk])


    def spill(j, half):
        rows = pl.ds(pl.multiple_of(j * 1024 + half * 512, 512), 512)
        return pltpu.make_async_copy(stage.at[half], down_out.at[rows, :], stage_sem.at[half])

    def grad_down(j):
        for half in range(2):

            if j:
                spill(j - 1, half).wait()
            active = act[j, :, half * 512 : half * 512 + 512]
            stage[half] = dot(active, cotangent[...], "TN").astype(BF)
            spill(j, half).start()

    tick(9)
    widen(0)
    widen(1)
    fetches[1].wait()
    tick(10)
    widen(2)
    grad_down(0)
    tick(11)
    widen(3)
    grad_down(1)
    grad_down(2)

    def narrow(chunk):
        cols = slice(chunk * 256, chunk * 256 + 256)

        def body(i):
            rows = at(i, 512)
            value = resid[rows, cols] + vec[7:8, cols]
            active = jnp.concatenate([act[j, rows, :] for j in range(4)], axis=1)
            value = value + dot(active, down_w[:, cols], "NN")
            mixed[rows, cols] = value.astype(BF)

        loop(2, body, 2)

        save(mixed.at[:, cols], result_out.at[:, cols])

    tick(12)
    narrow(0)
    tick(13)
    narrow(1)
    grad_down(3)
    tick(14)
    narrow(2)
    tick(15)
    narrow(3)
    small_out[...] = vec[...]
    for half in range(2):
        spill(3, half).wait()
    for task in tasks:
        task.finish()
    for copy in saves[5:8] + saves[10:]:
        copy.wait()
    for copy in dumps:
        copy.wait()


def forward_all(length, tokens, cotangent, vectors, weights):
    square = jax.ShapeDtypeStruct((1024, 1024), BF)
    tall = jax.ShapeDtypeStruct((4, 1024, 1024), BF)
    f32 = functools.partial(jax.ShapeDtypeStruct, dtype=F32)
    grid6 = [(4, 2, 2, 2) + w.shape for w in weights]
    hbm, vmem = pl.BlockSpec(memory_space=pltpu.HBM), pl.BlockSpec(memory_space=pltpu.VMEM)
    return pl.pallas_call(
        forward_kernel,
        out_shape=[square, f32((1024, 1024)), f32((8, 1024)), f32((16, 1024))]
        + [jax.ShapeDtypeStruct((4096, 1024), BF)]
        + [square] * 6
        + [tall]
        + [jax.ShapeDtypeStruct(s, BF) for s in grid6],
        in_specs=[pl.BlockSpec(memory_space=pltpu.SMEM)] + [hbm] * 2 + [vmem] * 9 + [hbm] * 6,
        out_specs=[hbm, hbm, hbm, vmem] + [hbm] * 14,
        scratch_shapes=[pltpu.VMEM((4, 2, 2, 2, 16, 128), F32)]
        + [pltpu.VMEM(s, BF) for s in grid6]
        + [pltpu.VMEM((4, 1024, 1024), BF), pltpu.VMEM((2, 1024, 1024), BF)]
        + [pltpu.VMEM((1024, 1024), BF)] * 2
        + [
            pltpu.VMEM((1024, 1024), F32),
            pltpu.VMEM((16, 1024), F32),
            pltpu.VMEM((8, 1024), F32),
            pltpu.VMEM((256, 256), F32),
            pltpu.VMEM((1024, 128), F32),
            pltpu.VMEM((1024, 128), F32),
            pltpu.VMEM((2, 512, 1024), BF),
            pltpu.VMEM((1024, 1024), BF),
            pltpu.VMEM((1024, 1024), BF),
            pltpu.VMEM((16, 128), F32),
            pltpu.SemaphoreType.DMA((14, Gathering.SEMS)),
            pltpu.SemaphoreType.DMA((14, Gathering.SEMS)),
            pltpu.SemaphoreType.DMA((14,)),
            pltpu.SemaphoreType.DMA((20,)),
            pltpu.SemaphoreType.DMA((13,)),
            pltpu.SemaphoreType.DMA((2,)),
            pltpu.SemaphoreType.DMA((2,)),
        ],
        compiler_params=pltpu.CompilerParams(
            collective_id=2, has_side_effects=True, vmem_limit_bytes=62 << 20
        ),
    )(length, tokens, cotangent, *vectors, *weights)


SHARDS = ("down", "up", "out", "query", "key", "value")
SCATTER_CUTS = (4, 4, 1, 1, 1, 2)


def attention_head_back(head, slope, off, refs, lse, mask, ramp, tilt, key_sum, value_sum):
    queries, keys, values, mixed, grad_mixed = refs
    cols = at(head, 128)
    factor = HD**-0.5 * LOG2E
    tilt[...] = ramp[...] * slope
    for i in (3, 2, 1, 0):
        rows, upto, before = slice(i * 256, i * 256 + 256), slice(0, i * 256 + 256), i * 256
        query, grad = queries[rows, cols], grad_mixed[rows, cols]
        product = grad.astype(F32) * mixed[rows, cols].astype(F32)
        inner = jnp.sum(product.T, 0, keepdims=True)
        level = lse[pl.ds(head, 1), rows]
        raw = dot(keys[upto, cols], query, "NT") * factor + wide(tilt[upto, :])
        probs = jnp.exp2(raw[before:] + mask[...] - level)
        if i:
            probs = jnp.concatenate([jnp.exp2(raw[:before] + (off - level)), probs], axis=0)
        grad_probs = dot(values[upto, cols], grad, "NT")
        grad_scores = (probs * (grad_probs - inner)).astype(BF)
        value_part = dot(probs.astype(BF), grad, "NN")
        key_part = dot(grad_scores, query, "NN")
        if i == 3:
            value_sum[...] = value_part
            key_sum[...] = key_part
        else:
            value_sum[upto, :] += value_part
            key_sum[upto, :] += key_part
        query_part = dot(keys[upto, cols], grad_scores, "TN") * HD**-0.5
        queries[rows, cols] = query_part.T.astype(BF)
    keys[:, cols] = (key_sum[...] * HD**-0.5).astype(BF)
    values[:, cols] = value_sum[...].astype(BF)


def backward_kernel(length_ref, vec, lse, *refs):
    refs = list(refs)

    def take(count):
        taken, refs[:count] = refs[:count], []
        return taken

    tokens, cotangent, attn_in, queries, keys, values, mixed, ffn_in, slope, resid = take(10)
    query_w, key_w, value_w, out_w, up_w, down_w, down_part = take(7)
    grad_tokens_out, small_out = take(2)
    out = take(6)
    parts = [down_part] + take(5)
    total, pair, line = take(6), take(6), take(6)
    mine_down, mine, sides_pair, sides_line, arena, grad, stage, strip = take(8)
    key_sum, value_sum, mask, ramp, tilt, sums = take(6)
    small_total, small_slots, small_send, small_recv = take(4)
    send, recv, load_sem, slot_sem, stage_sem, strip_sem = take(6)

    place = Place()
    loads = {}

    def load(source, slot):
        copy = pltpu.make_async_copy(source, arena.at[slot], slot_sem.at[slot])
        copy.start()
        loads[slot] = copy

    def ready(slot):
        loads.pop(slot).wait()
        return arena.at[slot]

    def load_chunk(j):
        load(slope.at[j], j % 2)
        load(down_w.at[pl.ds(j * 1024, 1024), :], 2 + j % 2)
        load(up_w.at[:, pl.ds(j * 1024, 1024)], 4 + j % 2)

    load(cotangent, 6)
    load_chunk(0)
    load(ffn_in, 7)
    place.greet()

    tasks = []
    for i, cut in enumerate(SCATTER_CUTS):
        pieces = even(cut, parts[i].shape[-1]) if i else DOWN_SCATTER
        for piece in pieces:
            g = len(tasks)
            own = columns(mine if i else mine_down.at[(1, 0, 1, 0)[g]], (0, piece[1]))
            views = [columns(r, piece) for r in (parts[i], total[i], pair[i], line[i], out[i])]
            kind = ScatteringSides if g < 1 else Scattering
            if g < 1:
                room = ((0, 256), (256, 128))[g]
                views[2:4] = columns(sides_pair, room), columns(sides_line, room)
            tasks.append(
                kind(place, views[0], own, *views[1:], send.at[g], recv.at[g], load_sem.at[g])
            )
    tasks.append(Summing(place, sums, small_total, small_slots, small_send, small_recv))

    ticks = [[3, 4, 12, 14, 16]]
    ticks += [[b, b + 1, b + 3, b + 5, b + 7] for b in (0, 1, 2, 3, 4, 5, 6, 7)]
    ticks += [[9, 10, 12, 14, 16], [10, 11, 13, 15, 16]]
    ticks += [[11, 12, 14, 15, 16], [12, 13, 15, 16, 17], [14, 15, 16, 17, 18]]

    def tick(number):
        run_tick(tasks, ticks, number)

    stages = {}

    def emit(part, left, right, width=1024, first=0):
        copies = []
        for half in range(2):
            if half in stages:
                stages.pop(half).wait()
            value = dot(left[:, half * 512 : half * 512 + 512], right[...], "TN")
            stage[half] = value.astype(BF).reshape(2, 2, 2, 2, 32, 1024)
            target = part.at[half * 2 : half * 2 + 2, :, :, :, :, pl.ds(first, width)]
            copy = pltpu.make_async_copy(stage.at[half], target, stage_sem.at[half])
            copy.start()
            stages[half] = copy
            copies.append(copy)

    def settle():
        for half in list(stages):
            stages.pop(half).wait()

    ones = jnp.ones((8, 1024), BF)

    def column_sums(source, row):
        def body(i):
            cols = at(i, 256)
            sums[row : row + 1, cols] = dot(ones, source[:, cols], "NN")[0:1]

        loop(4, body)

    length = length_ref[0]
    off = prepare_bias(length, mask, ramp)
    sums[...] = jnp.zeros_like(sums)
    tick(0)
    cot = ready(6)
    up_part = parts[1]

    for j in range(4):
        if j < 3:
            load_chunk(j + 1)
        hidden_slope, down_chunk, up_chunk = ready(j % 2), ready(2 + j % 2), ready(4 + j % 2)
        if j == 0:
            ffn = ready(7)

        def grad_hidden(i):
            cols = at(i, 512)
            value = dot(cot[...], down_chunk[cols, :], "NT") * hidden_slope[:, cols].astype(F32)
            hidden_slope[:, cols] = value.astype(BF)

        loop(2, grad_hidden, 2)
        column_sums(hidden_slope, 8 + j)
        if j == 0:
            tick(1)
        emit(up_part, ffn, hidden_slope, 1024, j * 1024)
        if j:
            tick(j + 2)

        def grad_ffn(i):
            rows = at(i, 512)
            value = dot(hidden_slope[rows, :], up_chunk[...], "NT")
            if j:
                value = value + grad[rows, :]
            grad[rows, :] = value

        loop(2, grad_ffn, 2)
        if j == 0:
            tick(2)

    settle()

    def load_strip(i):
        return pltpu.make_async_copy(
            resid.at[at(i, 128), :], strip.at[lax.rem(i, 2)], strip_sem.at[lax.rem(i, 2)]
        )

    load(mixed, 2)
    load(out_w, 4)
    load(queries, 3)
    load(keys, 5)
    load(values, 7)
    load_strip(0).start()
    gain = vec[5:6, :]
    branch = arena.at[0]

    def second_norm_back(i):
        @pl.when(i < 7)
        def _():
            load_strip(i + 1).start()

        load_strip(i).wait()
        rows = at(i, 128)
        normed, inverse = normed_rows(strip[lax.rem(i, 2)])
        incoming = grad[rows, :]
        sums[5:6, :] += jnp.sum(incoming * normed, 0, keepdims=True)
        sums[6:7, :] += jnp.sum(incoming, 0, keepdims=True)
        scaled = incoming * gain
        inner = (
            scaled
            - jnp.mean(scaled, -1, keepdims=True)
            - normed * jnp.mean(scaled * normed, -1, keepdims=True)
        )
        value = cot[rows, :].astype(F32) + inverse * inner
        grad[rows, :] = value
        branch[rows, :] = value.astype(BF)

    loop(8, second_norm_back)
    column_sums(cot, 7)
    column_sums(branch, 4)
    tick(6)
    load(query_w, 6)
    mix, out_full = ready(2), ready(4)
    grad_mixed = arena.at[1]

    def back_out(i):
        cols = at(i, 512)
        grad_mixed[:, cols] = dot(branch[...], out_full[cols, :], "NT").astype(BF)

    loop(2, back_out, 2)
    emit(parts[2], mix, branch)
    load(key_w, 4)
    query, key, value = ready(3), ready(5), ready(7)
    settle()
    load(attn_in, 0)

    def heads(first, count):
        def body(i, slope_now):
            attention_head_back(
                first + i,
                slope_now,
                off,
                (query, key, value, mix, grad_mixed),
                lse,
                mask,
                ramp,
                tilt,
                key_sum,
                value_sum,
            )
            return slope_now * 0.5

        lax.fori_loop(0, count, body, jnp.float32(LOG2E * 0.5 ** (first + 1)), unroll=2)

    heads(0, 2)
    tick(7)
    heads(2, 4)
    tick(8)
    heads(6, 2)
    load(value_w, 2)
    attn = ready(0)
    emit(parts[3], attn, query)
    settle()
    tick(9)
    emit(parts[4], attn, key)
    settle()
    tick(10)
    emit(parts[5], attn, value)
    settle()
    tick(11)
    load(tokens, 1)
    column_sums(query, 2)
    column_sums(value, 3)
    tick(12)
    query_full, key_full, value_full = ready(6), ready(4), ready(2)
    first_gain = vec[0:1, :]
    token_rows = ready(1)

    def first_norm_back(i):
        rows = at(i, 256)
        incoming = dot(query[rows, :], query_full[...], "NT")
        incoming = incoming + dot(key[rows, :], key_full[...], "NT")
        incoming = incoming + dot(value[rows, :], value_full[...], "NT")
        normed, inverse = normed_rows(token_rows[rows, :].astype(F32))
        sums[0:1, :] += jnp.sum(incoming * normed, 0, keepdims=True)
        sums[1:2, :] += jnp.sum(incoming, 0, keepdims=True)
        scaled = incoming * first_gain
        inner = (
            scaled
            - jnp.mean(scaled, -1, keepdims=True)
            - normed * jnp.mean(scaled * normed, -1, keepdims=True)
        )
        arena[1, rows, :] = (grad[rows, :] + inverse * inner).astype(BF)

    first_norm_back(0)
    first_norm_back(1)
    tick(13)
    first_norm_back(2)
    first_norm_back(3)
    result = pltpu.make_async_copy(arena.at[1], grad_tokens_out, slot_sem.at[1])
    result.start()
    for number in range(14, 19):
        tick(number)
    small_out[...] = small_total[4]
    result.wait()
    for task in tasks:
        task.finish()


def backward_all(length, vec, lse, arrays, shards):
    hbm, vmem = pl.BlockSpec(memory_space=pltpu.HBM), pl.BlockSpec(memory_space=pltpu.VMEM)
    groups = sum(SCATTER_CUTS)
    results = pl.pallas_call(
        backward_kernel,
        out_shape=[jax.ShapeDtypeStruct((1024, 1024), BF), jax.ShapeDtypeStruct((16, 1024), F32)]
        + [jax.ShapeDtypeStruct(s, F32) for s in shards]
        + [jax.ShapeDtypeStruct((4, 2, 2, 2) + s, BF) for s in shards[1:]],
        in_specs=[pl.BlockSpec(memory_space=pltpu.SMEM), vmem, vmem] + [hbm] * len(arrays),
        out_specs=[hbm, vmem] + [vmem] * 6 + [hbm] * 5,
        scratch_shapes=[pltpu.VMEM((4, 2, 2) + s, BF) for s in shards]
        + [pltpu.VMEM((3, 4) + s, BF) for s in shards]
        + [pltpu.VMEM((3,) + s, BF) for s in shards]
        + [
            pltpu.VMEM((2, 4, 2, 2, 128, 256), BF),
            pltpu.VMEM((4, 2, 2, 32, 1024), BF),
            pltpu.VMEM((3, 2, 2, 128, 384), BF),
            pltpu.VMEM((3, 128, 384), BF),
            pltpu.VMEM((8, 1024, 1024), BF),
            pltpu.VMEM((1024, 1024), F32),
            pltpu.VMEM((2, 2, 2, 2, 2, 32, 1024), BF),
            pltpu.VMEM((2, 128, 1024), F32),
            pltpu.VMEM((1024, 128), F32),
            pltpu.VMEM((1024, 128), F32),
            pltpu.VMEM((256, 256), F32),
            pltpu.VMEM((1024, 128), F32),
            pltpu.VMEM((1024, 128), F32),
            pltpu.VMEM((16, 1024), F32),
            pltpu.VMEM((5, 16, 1024), F32),
            pltpu.VMEM((6, 16, 1024), F32),
            pltpu.SemaphoreType.DMA((Summing.SEMS,)),
            pltpu.SemaphoreType.DMA((Summing.SEMS,)),
            pltpu.SemaphoreType.DMA((groups, Scattering.SEMS)),
            pltpu.SemaphoreType.DMA((groups, Scattering.SEMS)),
            pltpu.SemaphoreType.DMA((groups,)),
            pltpu.SemaphoreType.DMA((8,)),
            pltpu.SemaphoreType.DMA((2,)),
            pltpu.SemaphoreType.DMA((2,)),
        ],
        compiler_params=pltpu.CompilerParams(
            collective_id=3, has_side_effects=True, vmem_limit_bytes=62 << 20
        ),
    )(length, vec, lse, *arrays)
    return results[0], results[1], results[2:8]


def finish_kernel(small, *refs):
    arrays, outs, vectors = refs[:8], refs[8:16], refs[16:25]
    buffers, come, go = refs[25:33], refs[33], refs[34]
    inward = [
        pltpu.make_async_copy(source, buffer, come.at[i])
        for i, (source, buffer) in enumerate(zip(arrays, buffers))
    ]
    outward = [
        pltpu.make_async_copy(buffer, target, go.at[i])
        for i, (buffer, target) in enumerate(zip(buffers, outs))
    ]
    for copy in inward:
        copy.start()
    me = lax.axis_index("wide") * 4 + lax.axis_index("narrow")
    turned = pltpu.roll(small[...], lax.rem(1024 - me * 32, 1024), 1)
    for row in range(8):
        vectors[row][...] = turned[row, :32]
    line, block = 8 + lax.div(me, 8), lax.rem(me, 8)
    rows = lax.broadcasted_iota(jnp.int32, small.shape, 0)
    chosen = pltpu.roll(jnp.where(rows == line, small[...], 0.0), lax.rem(1024 - block * 128, 1024), 1)
    vectors[8][...] = jnp.sum(chosen[:, :128], 0)
    for first, second in zip(inward, outward):
        first.wait()
        second.start()
    for copy in outward:
        copy.wait()


def finish_all(small, arrays, sizes):
    hbm, vmem = pl.BlockSpec(memory_space=pltpu.HBM), pl.BlockSpec(memory_space=pltpu.VMEM)
    results = pl.pallas_call(
        finish_kernel,
        out_shape=[jax.ShapeDtypeStruct(a.shape, a.dtype) for a in arrays]
        + [jax.ShapeDtypeStruct((size,), F32) for size in sizes],
        in_specs=[vmem] + [hbm] * 8,
        out_specs=[hbm] * 8 + [vmem] * 9,
        scratch_shapes=[pltpu.VMEM(a.shape, a.dtype) for a in arrays]
        + [pltpu.SemaphoreType.DMA((8,)), pltpu.SemaphoreType.DMA((8,))],
    )(small, *arrays)
    return results[:8], results[8:]


def fused(tokens, cotangent, seq_length, parts):
    shards = [parts[i] for i in LARGE]
    (
        result, resid, lse, vec, down_part,
        attn_in, queries, keys, values, mixed, ffn_in, slope,
        *weights,
    ) = forward_all(seq_length, tokens, cotangent, [parts[i] for i in SMALL], shards)
    query_w, key_w, value_w, out_w, up_w, down_w = (
        w.reshape(-1, w.shape[-1]) for w in weights
    )
    down_part = down_part.reshape(weights[5].shape)
    order = (13, 11, 7, 2, 4, 5)
    grad_tokens, small, large = backward_all(
        seq_length,
        vec,
        lse,
        [tokens, cotangent, attn_in, queries, keys, values, mixed, ffn_in, slope, resid]
        + [query_w, key_w, value_w, out_w, up_w, down_w, down_part],
        [parts[i].shape for i in order],
    )
    (result, grad_tokens, *large), vectors = finish_all(
        small, [result, grad_tokens, *large], [parts[i].shape[0] for i in SMALL]
    )
    sums = [None] * 15
    for i, array in zip(order + SMALL, [*large, *vectors]):
        sums[i] = array
    return result, grad_tokens, sums


def is_fast():
    return lax.axis_size("wide") == 8 and lax.axis_size("narrow") == 4


def norm_forward(value, gain, shift):
    center = value - jnp.mean(value, -1, keepdims=True)
    inverse = lax.rsqrt(jnp.mean(center * center, -1, keepdims=True) + EPSILON)
    normed = center * inverse
    return (normed * gain.astype(jnp.float32) + shift.astype(jnp.float32), normed, inverse)


def norm_backward(incoming, normed, inverse, gain):
    scaled = incoming * gain.astype(jnp.float32)
    inner = (
        scaled
        - jnp.mean(scaled, -1, keepdims=True)
        - normed * jnp.mean(scaled * normed, -1, keepdims=True)
    )
    return (inverse * inner, jnp.sum(incoming * normed, 0), jnp.sum(incoming, 0))


def gelu_parts(hidden):
    cdf = 0.5 * (1.0 + lax.erf(hidden * 0.7071067811865476))
    density = jnp.exp(-0.5 * hidden * hidden) * 0.3989422804014327
    return (hidden * cdf, cdf + hidden * density)


def masked_scores(queries, keys, length):
    count = queries.shape[0]
    raw = jnp.einsum("qhd,khd->hqk", queries, keys, preferred_element_type=jnp.float32) * HD ** (
        -0.5
    )
    position = jnp.arange(count, dtype=jnp.int32)
    distance = (position[:, None] - position[None, :]).astype(jnp.float32)
    slopes = jnp.exp2(-8.0 * jnp.arange(1, H + 1, dtype=jnp.float32) / H)
    raw = raw - slopes[:, None, None] * distance[None]
    allowed = (position[:, None] >= position[None, :]) & (
        position[:, None] // length == position[None, :] // length
    )
    return jnp.where(allowed[None], raw, -1e30)


def forward(tokens, length, weights):
    (
        first_gain,
        first_shift,
        query_weight,
        query_bias,
        key_weight,
        value_weight,
        value_bias,
        out_weight,
        out_bias,
        second_gain,
        second_shift,
        up_weight,
        up_bias,
        down_weight,
        down_bias,
    ) = weights
    count = tokens.shape[0]
    width = tokens.shape[1]
    inputs = tokens.astype(jnp.float32)
    first_out, first_normed, first_inverse = norm_forward(inputs, first_gain, first_shift)
    attn_in = first_out.astype(jnp.bfloat16)
    queries = (
        (
            jnp.dot(attn_in, query_weight, preferred_element_type=jnp.float32)
            + query_bias.astype(jnp.float32)
        )
        .astype(jnp.bfloat16)
        .reshape(count, H, HD)
    )
    keys = (
        jnp.dot(attn_in, key_weight, preferred_element_type=jnp.float32)
        .astype(jnp.bfloat16)
        .reshape(count, H, HD)
    )
    values = (
        (
            jnp.dot(attn_in, value_weight, preferred_element_type=jnp.float32)
            + value_bias.astype(jnp.float32)
        )
        .astype(jnp.bfloat16)
        .reshape(count, H, HD)
    )
    scores = masked_scores(queries, keys, length)
    top = jnp.max(scores, -1, keepdims=True)
    expo = jnp.exp(scores - top)
    total = jnp.sum(expo, -1, keepdims=True)
    probs = expo / total
    log_total = top + jnp.log(total)
    mixed = jnp.einsum(
        "hqk,khd->qhd", probs.astype(jnp.bfloat16), values, preferred_element_type=jnp.float32
    )
    mixed = mixed.reshape(count, width).astype(jnp.bfloat16)
    resid = (
        inputs
        + jnp.dot(mixed, out_weight, preferred_element_type=jnp.float32)
        + out_bias.astype(jnp.float32)
    )
    second_out, second_normed, second_inverse = norm_forward(resid, second_gain, second_shift)
    ffn_in = second_out.astype(jnp.bfloat16)
    hidden = jnp.dot(ffn_in, up_weight, preferred_element_type=jnp.float32) + up_bias.astype(
        jnp.float32
    )
    active, active_slope = gelu_parts(hidden)
    active_low = active.astype(jnp.bfloat16)
    result = (
        resid
        + jnp.dot(active_low, down_weight, preferred_element_type=jnp.float32)
        + down_bias.astype(jnp.float32)
    )
    return (
        result.astype(jnp.bfloat16),
        attn_in,
        first_normed,
        first_inverse,
        queries,
        keys,
        values,
        log_total,
        mixed,
        second_normed,
        second_inverse,
        ffn_in,
        active_slope,
        active_low,
    )


def backward(cotangent, length, weights, kept):
    (
        first_gain,
        first_shift,
        query_weight,
        query_bias,
        key_weight,
        value_weight,
        value_bias,
        out_weight,
        out_bias,
        second_gain,
        second_shift,
        up_weight,
        up_bias,
        down_weight,
        down_bias,
    ) = weights
    (
        result,
        attn_in,
        first_normed,
        first_inverse,
        queries,
        keys,
        values,
        log_total,
        mixed,
        second_normed,
        second_inverse,
        ffn_in,
        active_slope,
        active_low,
    ) = kept
    count = cotangent.shape[0]
    width = cotangent.shape[1]
    grad_out = cotangent.astype(jnp.float32)
    grad_down_bias = jnp.sum(grad_out, 0)
    grad_down_weight = jnp.einsum(
        "tf,td->fd", active_low, cotangent, preferred_element_type=jnp.float32
    )
    grad_active = jnp.einsum(
        "td,fd->tf", cotangent, down_weight, preferred_element_type=jnp.float32
    )
    grad_hidden = (grad_active * active_slope).astype(jnp.bfloat16)
    grad_up_bias = jnp.sum(grad_hidden.astype(jnp.float32), 0)
    grad_up_weight = jnp.einsum(
        "td,tf->df", ffn_in, grad_hidden, preferred_element_type=jnp.float32
    )
    grad_ffn_in = jnp.einsum(
        "tf,df->td", grad_hidden, up_weight, preferred_element_type=jnp.float32
    )
    grad_second, grad_second_gain, grad_second_shift = norm_backward(
        grad_ffn_in, second_normed, second_inverse, second_gain
    )
    grad_resid = grad_out + grad_second
    grad_branch = grad_resid.astype(jnp.bfloat16)
    grad_out_bias = jnp.sum(grad_branch.astype(jnp.float32), 0)
    grad_out_weight = jnp.einsum(
        "tc,td->cd", mixed, grad_branch, preferred_element_type=jnp.float32
    )
    grad_mixed = jnp.einsum(
        "td,cd->tc", grad_branch, out_weight, preferred_element_type=jnp.float32
    )
    grad_mixed = grad_mixed.astype(jnp.bfloat16).reshape(count, H, HD)
    scores = masked_scores(queries, keys, length)
    probs = jnp.exp(scores - log_total)
    grad_probs = jnp.einsum("qhd,khd->hqk", grad_mixed, values, preferred_element_type=jnp.float32)
    grad_values = jnp.einsum(
        "hqk,qhd->khd", probs.astype(jnp.bfloat16), grad_mixed, preferred_element_type=jnp.float32
    )
    grad_values = grad_values.astype(jnp.bfloat16).reshape(count, width)
    row_total = jnp.sum(grad_probs * probs, -1, keepdims=True)
    grad_scores = (probs * (grad_probs - row_total)).astype(jnp.bfloat16)
    factor = HD ** (-0.5)
    grad_queries = (
        jnp.einsum("hqk,khd->qhd", grad_scores, keys, preferred_element_type=jnp.float32) * factor
    )
    grad_queries = grad_queries.astype(jnp.bfloat16).reshape(count, width)
    grad_keys = (
        jnp.einsum("hqk,qhd->khd", grad_scores, queries, preferred_element_type=jnp.float32)
        * factor
    )
    grad_keys = grad_keys.astype(jnp.bfloat16).reshape(count, width)
    grad_query_bias = jnp.sum(grad_queries.astype(jnp.float32), 0)
    grad_value_bias = jnp.sum(grad_values.astype(jnp.float32), 0)
    grad_query_weight = jnp.einsum(
        "tc,td->cd", attn_in, grad_queries, preferred_element_type=jnp.float32
    )
    grad_key_weight = jnp.einsum(
        "tc,td->cd", attn_in, grad_keys, preferred_element_type=jnp.float32
    )
    grad_value_weight = jnp.einsum(
        "tc,td->cd", attn_in, grad_values, preferred_element_type=jnp.float32
    )
    grad_attn = jnp.einsum(
        "td,cd->tc", grad_queries, query_weight, preferred_element_type=jnp.float32
    )
    grad_attn = grad_attn + jnp.einsum(
        "td,cd->tc", grad_keys, key_weight, preferred_element_type=jnp.float32
    )
    grad_attn = grad_attn + jnp.einsum(
        "td,cd->tc", grad_values, value_weight, preferred_element_type=jnp.float32
    )
    grad_first, grad_first_gain, grad_first_shift = norm_backward(
        grad_attn, first_normed, first_inverse, first_gain
    )
    grad_tokens = (grad_resid + grad_first).astype(jnp.bfloat16)
    sums = spread(
        (
            grad_first_gain,
            grad_first_shift,
            grad_query_weight,
            grad_query_bias,
            grad_key_weight,
            grad_value_weight,
            grad_value_bias,
            grad_out_weight,
            grad_out_bias,
            grad_second_gain,
            grad_second_shift,
            grad_up_weight,
            grad_up_bias,
            grad_down_weight,
            grad_down_bias,
        )
    )
    return (grad_tokens, sums)


def body(
    tokens,
    cotangent,
    seq_length,
    first_gain,
    first_shift,
    query_weight,
    query_bias,
    key_weight,
    value_weight,
    value_bias,
    out_weight,
    out_bias,
    second_gain,
    second_shift,
    up_weight,
    up_bias,
    down_weight,
    down_bias,
):
    shards = (
        first_gain,
        first_shift,
        query_weight,
        query_bias,
        key_weight,
        value_weight,
        value_bias,
        out_weight,
        out_bias,
        second_gain,
        second_shift,
        up_weight,
        up_bias,
        down_weight,
        down_bias,
    )
    if is_fast():
        result, grad_tokens, sums = fused(tokens, cotangent, seq_length, shards)
        return (result, grad_tokens, *sums)
    length = seq_length[0]
    weights = collect(shards)
    kept = forward(tokens, length, weights)
    grad_tokens, sums = backward(cotangent, length, weights, kept)
    (
        g_first_gain,
        g_first_shift,
        g_query_weight,
        g_query_bias,
        g_key_weight,
        g_value_weight,
        g_value_bias,
        g_out_weight,
        g_out_bias,
        g_second_gain,
        g_second_shift,
        g_up_weight,
        g_up_bias,
        g_down_weight,
        g_down_bias,
    ) = sums
    return (
        kept[0],
        grad_tokens,
        g_first_gain,
        g_first_shift,
        g_query_weight,
        g_query_bias,
        g_key_weight,
        g_value_weight,
        g_value_bias,
        g_out_weight,
        g_out_bias,
        g_second_gain,
        g_second_shift,
        g_up_weight,
        g_up_bias,
        g_down_weight,
        g_down_bias,
    )


def solution(mesh):
    placed = (
        P(("wide", "narrow"), None),
        P(("wide", "narrow"), None),
        P(("wide", "narrow")),
        P(("wide", "narrow")),
        P(("wide", "narrow")),
        P(("wide", "narrow"), None),
        P(("wide", "narrow")),
        P(("wide", "narrow"), None),
        P(("wide", "narrow"), None),
        P(("wide", "narrow")),
        P(("wide", "narrow"), None),
        P(("wide", "narrow")),
        P(("wide", "narrow")),
        P(("wide", "narrow")),
        P(("wide", "narrow"), None),
        P(("wide", "narrow")),
        P(("wide", "narrow"), None),
        P(("wide", "narrow")),
    )
    return jax.shard_map(
        body,
        mesh=mesh,
        in_specs=placed,
        out_specs=(
            P(("wide", "narrow"), None),
            P(("wide", "narrow"), None),
            P(("wide", "narrow")),
            P(("wide", "narrow")),
            P(("wide", "narrow"), None),
            P(("wide", "narrow")),
            P(("wide", "narrow"), None),
            P(("wide", "narrow"), None),
            P(("wide", "narrow")),
            P(("wide", "narrow"), None),
            P(("wide", "narrow")),
            P(("wide", "narrow")),
            P(("wide", "narrow")),
            P(("wide", "narrow"), None),
            P(("wide", "narrow")),
            P(("wide", "narrow"), None),
            P(("wide", "narrow")),
        ),
        check_vma=False,
    )
```
